32 devices in a mesh: frames: 8 (over z, y), rep: 4 (over x, core).
Axes of the slice: x: 2, y: 2, z: 4, core: 2. Of those that a mesh axis runs over, the one named last changes fastest.
Arguments:
- frames_in: bfloat16 [192, 7, 7, 512], P(('frames', 'rep'))
- cotangent: bfloat16 [192, 7, 7, 512], P(('frames', 'rep')), may hold values from -6 to 6
- lengths: int32 [33], replicated, may hold values from 1 to 10, as said below
- spatial_weights: float32 [2, 4608, 1152], P(None, 'frames', 'rep'), may hold values from -0.09375 to 0.09375
- spatial_first: float32 [2, 4608, 1152], P(None, 'frames', 'rep')
- spatial_second: float32 [2, 4608, 1152], P(None, 'frames', 'rep'), may hold values from 2352 to 9408
- temporal_weights: float32 [2, 3456, 512], P(None, 'frames', 'rep'), may hold values from -0.109375 to 0.109375
- temporal_first: float32 [2, 3456, 512], P(None, 'frames', 'rep')
- temporal_second: float32 [2, 3456, 512], P(None, 'frames', 'rep'), may hold values from 2352 to 9408
- mid_norm: float32 [2, 2, 1152], replicated
- mid_first: float32 [2, 2, 1152], replicated
- mid_second: float32 [2, 2, 1152], replicated, may hold values from 4704 to 18816
- out_norm: float32 [2, 2, 512], replicated
- out_first: float32 [2, 2, 512], replicated
- out_second: float32 [2, 2, 512], replicated, may hold values from 4704 to 18816
Outputs:
- block_out: bfloat16 [192, 7, 7, 512], P(('frames', 'rep'))
- input_grad: float32 [192, 7, 7, 512], P(('frames', 'rep'))
- spatial_new: float32 [2, 4608, 1152], P(None, 'frames', 'rep')
- spatial_first_new: float32 [2, 4608, 1152], P(None, 'frames', 'rep')
- spatial_second_new: float32 [2, 4608, 1152], P(None, 'frames', 'rep')
- spatial_low: bfloat16 [2, 4608, 1152], P(None, 'frames', 'rep')
- temporal_new: float32 [2, 3456, 512], P(None, 'frames', 'rep')
- temporal_first_new: float32 [2, 3456, 512], P(None, 'frames', 'rep')
- temporal_second_new: float32 [2, 3456, 512], P(None, 'frames', 'rep')
- temporal_low: bfloat16 [2, 3456, 512], P(None, 'frames', 'rep')
- mid_norm_new: float32 [2, 2, 1152], replicated
- mid_first_new: float32 [2, 2, 1152], replicated
- mid_second_new: float32 [2, 2, 1152], replicated
- out_norm_new: float32 [2, 2, 512], replicated
- out_first_new: float32 [2, 2, 512], replicated
- out_second_new: float32 [2, 2, 512], replicated
The draws below stay inside these ranges and needn't reach their ends.
Inputs may be any that keep to these rules, and one draw needn't show every extreme that they name: `lengths`: the clips cover all 192 frames in order; every device's block of 6 frames holds exactly one clip start besides frame 0, never at the block's first frame.
All inputs are finite; a program needn't handle non-finite values.
Results may differ from the reference program's by a relative error of at most 0.018.
Values may be sent and summed in bfloat16 or wider, within the bound.
No kernel may reach another device: no remote copies, remote signals or barrier semaphores. Data moves between devices by JAX's collectives and lax.ppermute only.
A program may use at most 320 MiB of HBM per device.

```python
import math
import jax
import jax.numpy as jnp
from jax import lax

D = 512
MID = 1152
HH = 7
WW = 7
F_DEV = 6
BLOCKS = 1
STEP = 5
UNITS = 2
FRAMES = 192


def moment_draw(key, shape, spread):
    return jax.random.normal(key, shape, jnp.float32) * spread


def norm_draw(key, channels):
    gain_key, bias_key = jax.random.split(key)
    gains = jax.random.uniform(gain_key, (UNITS, 1, channels), jnp.float32, 0.7, 1.3)
    biases = jax.random.normal(bias_key, (UNITS, 1, channels), jnp.float32) * 0.3
    return jnp.concatenate([gains, biases], axis=1)


def draw_frames_in(key, part):
    key = jax.random.fold_in(key, 1)
    position = jnp.arange(FRAMES, dtype=jnp.float32) / FRAMES
    values = jax.random.truncated_normal(key, -4.0, 4.0, (FRAMES, HH, WW, D), jnp.float32)
    spread = 0.5 + position
    return (values * spread[:, None, None, None]).astype(jnp.bfloat16)


def draw_lengths(key, part):
    key = jax.random.fold_in(key, 2)
    offset_key, chosen_key = jax.random.split(key)
    devices = FRAMES // F_DEV
    offsets = jax.random.randint(offset_key, (devices,), 1, F_DEV)
    chosen = jax.random.randint(chosen_key, (), 0, devices - 2)
    device_ids = jnp.arange(devices, dtype=jnp.int32)
    offsets = jnp.where(device_ids == chosen, 1, offsets)
    offsets = jnp.where(device_ids == chosen + 1, F_DEV - 1, offsets)
    offsets = jnp.where(device_ids == devices - 1, F_DEV - 1, offsets)
    cuts = device_ids * F_DEV + offsets
    bounds = jnp.concatenate([jnp.zeros((1,), jnp.int32), cuts.astype(jnp.int32), jnp.full((1,), FRAMES, jnp.int32)])
    return (bounds[1:] - bounds[:-1]).astype(jnp.int32)


def draw_spatial_first(key, part):
    key = jax.random.fold_in(key, 3)
    return moment_draw(key, (UNITS, 9 * D, MID), 0.5 * math.sqrt(FRAMES * HH * WW))


def draw_temporal_first(key, part):
    key = jax.random.fold_in(key, 4)
    return moment_draw(key, (UNITS, 3 * MID, D), 0.5 * math.sqrt(FRAMES * HH * WW))


def draw_mid_norm(key, part):
    key = jax.random.fold_in(key, 5)
    return norm_draw(key, MID)


def draw_mid_first(key, part):
    key = jax.random.fold_in(key, 6)
    return moment_draw(key, (UNITS, 2, MID), 0.7 * math.sqrt(FRAMES * HH * WW))


def draw_out_norm(key, part):
    key = jax.random.fold_in(key, 7)
    return norm_draw(key, D)


def draw_out_first(key, part):
    key = jax.random.fold_in(key, 8)
    return moment_draw(key, (UNITS, 2, D), 0.7 * math.sqrt(FRAMES * HH * WW))


def level_of(own_key, extent, cuts, low, high):
    def one(dim, parts):
        steps = jax.random.uniform(jax.random.fold_in(jax.random.fold_in(own_key, 6), dim), (parts,), jnp.float32, low / len(cuts), high / len(cuts))
        return jnp.repeat(jnp.exp(steps), extent[dim] // parts).reshape((-1,) + (1,) * (len(extent) - dim - 1))

    gain = one(*cuts[0])
    for cut in cuts[1:]:
        gain = gain * one(*cut)
    return gain


def gaussian(own_key, dims, scale, reach, cuts=(), kind=jnp.bfloat16):
    values = jax.random.normal(own_key, dims, jnp.float32) * scale
    if len(cuts) > 0:
        values = level_of(own_key, dims, cuts, -0.22, 0.18) * values
    return jnp.clip(values, min=-reach, max=reach).astype(kind)


def setup_inputs(seed: int = 0) -> dict:
    splits = jax.random.split(jax.random.key(seed), 16)
    return {
        "frames_in": draw_frames_in(jax.random.fold_in(splits[15], 71), 0),
        "cotangent": gaussian(splits[1], (FRAMES, HH, WW, D), 1.0, 6.0, ((0, 32),)),
        "lengths": draw_lengths(jax.random.fold_in(splits[15], 71), 0),
        "spatial_weights": gaussian(splits[3], (UNITS, 9 * D, MID), (9 * D) ** -0.5, 0.09375, ((1, 8), (2, 4)), jnp.float32),
        "spatial_first": draw_spatial_first(jax.random.fold_in(splits[15], 71), 0),
        "spatial_second": jnp.clip(jnp.exp(math.log(9408.0) - 1.3862944 * jax.random.uniform(splits[5], (UNITS, 9 * D, MID), jnp.float32) ** level_of(splits[5], (UNITS, 9 * D, MID), ((1, 8), (2, 4)), -0.2, 0.2)), 2352.0, 9408.0),
        "temporal_weights": gaussian(splits[6], (UNITS, 3 * MID, D), (3 * MID) ** -0.5, 0.109375, ((1, 8), (2, 4)), jnp.float32),
        "temporal_first": draw_temporal_first(jax.random.fold_in(splits[15], 71), 0),
        "temporal_second": jnp.clip(jnp.exp(math.log(9408.0) - 1.3862944 * jax.random.uniform(splits[8], (UNITS, 3 * MID, D), jnp.float32) ** level_of(splits[8], (UNITS, 3 * MID, D), ((1, 8), (2, 4)), -0.2, 0.2)), 2352.0, 9408.0),
        "mid_norm": draw_mid_norm(jax.random.fold_in(splits[15], 71), 0),
        "mid_first": draw_mid_first(jax.random.fold_in(splits[15], 71), 0),
        "mid_second": jnp.clip(jnp.exp(jax.random.uniform(splits[11], (UNITS, 2, MID), jnp.float32, math.log(4704.0), math.log(18816.0))), 4704.0, 18816.0),
        "out_norm": draw_out_norm(jax.random.fold_in(splits[15], 71), 0),
        "out_first": draw_out_first(jax.random.fold_in(splits[15], 71), 0),
        "out_second": jnp.clip(jnp.exp(jax.random.uniform(splits[14], (UNITS, 2, D), jnp.float32, math.log(4704.0), math.log(18816.0))), 4704.0, 18816.0),
    }


NORM_EPS = 1e-05
ADAM_EPS = 1e-08
BETA_ONE = 0.5
BETA_TWO = 0.5
RATE_WEIGHT = 0.015
RATE_NORM = 0.2
DECAY = 0.05
HIGHEST = lax.Precision.HIGHEST

@jax.custom_vjp
def low(v):
    return lax.optimization_barrier(v.astype(jnp.bfloat16)).astype(jnp.float32)

@jax.custom_vjp
def low_back(v):
    return v

def low_keep(v):
    return (low(v), None)

def low_pass(kept, grad):
    return (grad,)

def back_keep(v):
    return (v, None)

def back_low(kept, grad):
    return (low(grad),)
low.defvjp(low_keep, low_pass)
low_back.defvjp(back_keep, back_low)

def clip_masks(lengths):
    clip_ends = jnp.cumsum(lengths).astype(jnp.int32)
    starts = jnp.concatenate([jnp.zeros((1,), jnp.int32), clip_ends[:-1]]).astype(jnp.int32)
    frame_ids = jnp.arange(FRAMES, dtype=jnp.int32)
    opening = jnp.any(frame_ids[:, None] == starts[None, :], axis=1)
    keep_prev = jnp.where(opening, 0.0, 1.0).astype(jnp.float32)
    keep_next = jnp.concatenate([keep_prev[1:], jnp.zeros((1,), jnp.float32)])
    return (keep_prev, keep_next)

def group_conv(group, weight):
    padded = jnp.pad(group, ((0, 0), (1, 1), (1, 1), (0, 0)))
    pieces = [padded[:, row_tap:row_tap + HH, col_tap:col_tap + WW, :] for row_tap in range(3) for col_tap in range(3)]
    patches = jnp.concatenate(pieces, axis=-1)
    result = jnp.dot(patches.reshape(-1, patches.shape[-1]), weight, precision=HIGHEST)
    return result.reshape(group.shape[0], HH, WW, -1)

def spatial_conv(act, weight):
    groups = act.reshape(-1, F_DEV, HH, WW, act.shape[-1])
    runner = jax.checkpoint(group_conv)
    result = lax.map(lambda group: runner(group, weight), groups)
    return result.reshape(FRAMES, HH, WW, -1)

def temporal_conv(middle, weight, keep_prev, keep_next):
    channels = middle.shape[-1]
    rows = middle.reshape(-1, channels)
    earlier = jnp.dot(rows, weight[:channels], precision=HIGHEST).reshape(FRAMES, HH * WW, -1)
    current = jnp.dot(rows, weight[channels:2 * channels], precision=HIGHEST).reshape(FRAMES, HH * WW, -1)
    later = jnp.dot(rows, weight[2 * channels:], precision=HIGHEST).reshape(FRAMES, HH * WW, -1)
    zero_frame = jnp.zeros_like(earlier[:1])
    from_prev = jnp.concatenate([zero_frame, earlier[:-1]], axis=0) * keep_prev[:, None, None]
    from_next = jnp.concatenate([later[1:], zero_frame], axis=0) * keep_next[:, None, None]
    return (from_prev + current + from_next).reshape(FRAMES, HH, WW, -1)

def batch_norm(values, params):
    center = lax.optimization_barrier(jnp.mean(values, axis=(0, 1, 2)))
    shifted = values - center
    spread = lax.optimization_barrier(jnp.mean(shifted * shifted, axis=(0, 1, 2)))
    return shifted * lax.rsqrt(spread + NORM_EPS) * params[0] + params[1]

def conv_unit(act, spatial_w, temporal_w, mid_params, out_params, keep_prev, keep_next):
    spatial_out = low_back(spatial_conv(low(act), low(spatial_w)))
    middle = low(jax.nn.silu(batch_norm(spatial_out, mid_params)))
    temporal_out = low_back(temporal_conv(middle, low(temporal_w), keep_prev, keep_next))
    return batch_norm(temporal_out, out_params)

def adam_step(param, grad, first, second, rate, decay):
    first_new = BETA_ONE * first + (1.0 - BETA_ONE) * grad
    second_new = BETA_TWO * second + (1.0 - BETA_TWO) * grad * grad
    fix_one = 1.0 - BETA_ONE ** STEP
    fix_two = 1.0 - BETA_TWO ** STEP
    update = first_new / fix_one / (jnp.sqrt(second_new / fix_two) + ADAM_EPS)
    return (param - rate * (update + decay * param), first_new, second_new)

def reference(frames_in, cotangent, lengths, spatial_weights, spatial_first, spatial_second, temporal_weights, temporal_first, temporal_second, mid_norm, mid_first, mid_second, out_norm, out_first, out_second):
    keep_prev, keep_next = clip_masks(lengths)

    def forward(state, spatial, temporal, mid_params, out_params):
        for block_id in range(BLOCKS):
            first_unit = 2 * block_id
            second_unit = first_unit + 1
            first_out = conv_unit(state, spatial[first_unit], temporal[first_unit], mid_params[first_unit], out_params[first_unit], keep_prev, keep_next)
            second_out = conv_unit(jax.nn.silu(first_out), spatial[second_unit], temporal[second_unit], mid_params[second_unit], out_params[second_unit], keep_prev, keep_next)
            state = jax.nn.silu(second_out + state)
        return state
    result, pullback = jax.vjp(forward, frames_in.astype(jnp.float32), spatial_weights, temporal_weights, mid_norm, out_norm)
    input_grad, spatial_grad, temporal_grad, mid_grad, out_grad = pullback(cotangent.astype(jnp.float32))
    spatial_new, spatial_first_new, spatial_second_new = adam_step(spatial_weights, spatial_grad, spatial_first, spatial_second, RATE_WEIGHT, DECAY)
    temporal_new, temporal_first_new, temporal_second_new = adam_step(temporal_weights, temporal_grad, temporal_first, temporal_second, RATE_WEIGHT, DECAY)
    mid_new, mid_first_new, mid_second_new = adam_step(mid_norm, mid_grad, mid_first, mid_second, RATE_NORM, 0.0)
    out_new, out_first_new, out_second_new = adam_step(out_norm, out_grad, out_first, out_second, RATE_NORM, 0.0)
    return (result.astype(jnp.bfloat16), input_grad, spatial_new, spatial_first_new, spatial_second_new, spatial_new.astype(jnp.bfloat16), temporal_new, temporal_first_new, temporal_second_new, temporal_new.astype(jnp.bfloat16), mid_new, mid_first_new, mid_second_new, out_new, out_first_new, out_second_new)
```

```python
import jax
import jax.numpy as jnp
from jax import lax
from jax.sharding import PartitionSpec as P

STEP = 5
NORM_EPS = 1e-05
ADAM_EPS = 1e-08
BETA_ONE = 0.5
BETA_TWO = 0.5
RATE_WEIGHT = 0.015
RATE_NORM = 0.2
DECAY = 0.05
BF = jnp.bfloat16
F32 = jnp.float32


def silu_slope(values):
    sigmoid = jax.nn.sigmoid(values)
    return sigmoid * (1.0 + values * (1.0 - sigmoid))


def swap(parts, axis):
    return lax.all_to_all(parts, axis, 0, 0, tiled=True)


def from_all(value, axis):
    count = lax.axis_size(axis)
    return swap(jnp.broadcast_to(value[None], (count,) + value.shape), axis)


def neighbours(first, last, axis):
    count = lax.axis_size(axis)
    before = lax.ppermute(last, axis, [(i, i + 1) for i in range(count - 1)])
    after = lax.ppermute(first, axis, [(i + 1, i) for i in range(count - 1)])
    return before, after


def moments(values, axis):
    rows = values.shape[0]
    center = jnp.mean(values, axis=0)
    spread = jnp.sum(jnp.square(values - center), axis=0)
    both = from_all(jnp.stack([center, spread]), axis)
    count = both.shape[0]
    mean = jnp.mean(both[:, 0], axis=0)
    total = jnp.sum(both[:, 1], axis=0) + rows * jnp.sum(jnp.square(both[:, 0] - mean), axis=0)
    return mean, lax.rsqrt(total / (rows * count) + NORM_EPS)


def gradient_sums(upstream, normed, axis):
    both = from_all(jnp.stack([jnp.sum(upstream * normed, axis=0), jnp.sum(upstream, axis=0)]), axis)
    return jnp.sum(both, axis=0)


def patches_of(act):
    height, width, frames, channels = act.shape
    padded = jnp.pad(act, ((1, 1), (1, 1), (0, 0), (0, 0)))
    pieces = [
        padded[i : i + height, j : j + width] for i in range(3) for j in range(3)
    ]
    return jnp.concatenate(pieces, axis=-1).reshape(height * width * frames, 9 * channels)


def adjoint(patch_grad, shape):
    height, width, frames, channels = shape
    grid = patch_grad.reshape(height, width, frames, 9, channels)
    total = jnp.zeros((height + 2, width + 2, frames, channels), F32)
    for i in range(3):
        for j in range(3):
            total = total.at[i : i + height, j : j + width].add(grid[:, :, :, 3 * i + j])
    return total[1 : height + 1, 1 : width + 1]


def split_columns(values, count):
    rows, cols = values.shape
    return values.reshape(rows, count, cols // count).transpose(1, 0, 2)


def sum_over(parts, axis):
    return jnp.sum(swap(parts, axis).astype(F32), axis=0)


def adam_step(param, gradient, moment_one, moment_two, rate, decay):
    first_new = BETA_ONE * moment_one + (1.0 - BETA_ONE) * gradient
    second_new = BETA_TWO * moment_two + (1.0 - BETA_TWO) * gradient * gradient
    fix_one = 1.0 - BETA_ONE**STEP
    fix_two = 1.0 - BETA_TWO**STEP
    update = first_new / fix_one / (jnp.sqrt(second_new / fix_two) + ADAM_EPS)
    return (param - rate * (update + decay * param), first_new, second_new)


def window_of(middle, before, after, keep_prev, keep_next):
    earlier = jnp.concatenate([before[:, None], middle[:, :-1]], axis=1) * keep_prev
    later = jnp.concatenate([middle[:, 1:], after[:, None]], axis=1) * keep_next
    return earlier, later


def mm(a, b, dims):
    return lax.dot_general(a, b, (dims, ((), ())), preferred_element_type=F32)


def on_device(
    frames_in, cotangent, lengths,
    spatial_weights, spatial_first, spatial_second,
    temporal_weights, temporal_first, temporal_second,
    mid_norm, mid_first, mid_second,
    out_norm, out_first, out_second,
):
    own_frames, height, width, depth = frames_in.shape
    n_f, n_r = lax.axis_size("frames"), lax.axis_size("rep")
    me_r = lax.axis_index("rep")
    frames = own_frames * n_r
    pixels = height * width
    rows = pixels * frames
    total = rows * n_f
    mid = spatial_weights.shape[2]
    cols = depth // n_r
    units = spatial_weights.shape[0]

    spatial_low = spatial_weights.astype(BF)
    temporal_low = temporal_weights.astype(BF)
    spatial_w = [lax.all_gather(spatial_low[u], "frames", axis=0, tiled=True) for u in range(units)]
    temporal_w = []
    for u in range(units):
        shard = lax.all_gather(temporal_low[u], "frames", axis=0, tiled=True)
        shard = shard.reshape(3, n_r, mid, cols).transpose(1, 0, 2, 3)
        shard = swap(shard, "rep")
        temporal_w.append(shard.transpose(1, 2, 0, 3).reshape(3, mid, depth))

    frame_ids = lax.axis_index("frames") * frames + jnp.arange(frames, dtype=jnp.int32)
    clip_ends = jnp.cumsum(lengths)
    starts = jnp.concatenate([jnp.zeros((1,), jnp.int32), clip_ends[:-1]])
    opening = jnp.any(frame_ids[:, None] == starts[None, :], axis=1)
    closing = jnp.any((frame_ids + 1)[:, None] == clip_ends[None, :], axis=1)
    keep_prev = jnp.where(opening, 0.0, 1.0).astype(BF)[None, :, None]
    keep_next = jnp.where(closing, 0.0, 1.0).astype(BF)[None, :, None]

    act = lax.all_gather(frames_in, "rep", axis=0, tiled=True).transpose(1, 2, 0, 3)
    state_cols = lax.dynamic_slice_in_dim(act.reshape(rows, depth), me_r * cols, cols, axis=1)
    state_cols = state_cols.astype(F32)
    cot = cotangent.reshape(own_frames, pixels, n_r, cols).transpose(2, 0, 1, 3)
    cot = swap(cot, "rep").reshape(frames, pixels, cols).transpose(1, 0, 2)
    cot = cot.reshape(rows, cols).astype(F32)

    mid_own = lax.dynamic_slice_in_dim(mid_norm, me_r * mid, mid, axis=2)
    out_own = lax.dynamic_slice_in_dim(out_norm, me_r * cols, cols, axis=2)

    saved = []
    out_cols = None
    for u in range(units):
        patches = patches_of(act)
        spatial = mm(patches, spatial_w[u], ((1,), (0,)))
        grid = spatial.reshape(pixels, frames, mid)
        before, after = neighbours(grid[:, 0], grid[:, -1], "frames")
        mean, inverse = moments(spatial, "frames")
        gain, bias = mid_own[u, 0], mid_own[u, 1]

        def activate(v):
            return jax.nn.silu((v - mean) * inverse * gain + bias).astype(BF)

        middle = activate(grid)
        earlier, later = window_of(middle, activate(before), activate(after), keep_prev, keep_next)
        window = jnp.stack([earlier, middle, later]).reshape(3, rows, mid)
        part = sum(mm(window[k], temporal_w[u][k], ((1,), (0,))) for k in range(3))
        temporal = sum_over(split_columns(part.astype(BF), n_r), "rep")
        out_mean, out_inverse = moments(temporal, "frames")
        out_normed = (temporal - out_mean) * out_inverse
        out_cols = out_normed * out_own[u, 0] + out_own[u, 1]
        saved.append((act, spatial, mean, inverse, window, out_normed, out_inverse, out_cols))
        if u + 1 < units:
            low = jax.nn.silu(out_cols).astype(BF)
            low = lax.all_gather(low, "rep", axis=1, tiled=True)
            act = low.reshape(height, width, frames, depth)

    summed = out_cols + state_cols
    block = jax.nn.silu(summed).astype(BF)
    block = block.reshape(pixels, n_r, own_frames, cols).transpose(1, 2, 0, 3)
    block = swap(block, "rep")
    block_out = block.transpose(1, 2, 0, 3).reshape(frames_in.shape)

    summed_grad = cot * silu_slope(summed)
    upstream = summed_grad
    spatial_grads, temporal_grads = [None] * units, [None] * units
    norm_grads = [None] * units
    input_grad = None
    for u in reversed(range(units)):
        act, spatial, mean, inverse, window, out_normed, out_inverse, out_cols = saved[u]
        out_sums = gradient_sums(upstream, out_normed, "frames")
        dt = (
            out_own[u, 0] * out_inverse
            * (upstream - out_sums[1] / total - out_normed * (out_sums[0] / total))
        ).astype(BF)
        dt = lax.all_gather(dt, "rep", axis=1, tiled=True)
        grid = dt.reshape(pixels, frames, depth)
        before, after = neighbours(grid[:, 0], grid[:, -1], "frames")
        earlier, later = window_of(grid, before, after, keep_prev, keep_next)
        d_mid = (
            mm(later.reshape(rows, depth), temporal_w[u][0], ((1,), (1,)))
            + mm(dt, temporal_w[u][1], ((1,), (1,)))
            + mm(earlier.reshape(rows, depth), temporal_w[u][2], ((1,), (1,)))
        )
        t_term = mm(window, dt, ((1,), (0,))).astype(BF)
        t_term = t_term.reshape(3, mid, n_r, cols).transpose(2, 0, 1, 3)
        t_term = swap(t_term, "rep").transpose(1, 0, 2, 3).reshape(n_f, -1, cols)
        temporal_grads[u] = sum_over(t_term, "frames")

        normed = (spatial - mean) * inverse
        gain, bias = mid_own[u, 0], mid_own[u, 1]
        d_mid = d_mid * silu_slope(normed * gain + bias)
        mid_sums = gradient_sums(d_mid, normed, "frames")
        d_spatial = (
            gain * inverse * (d_mid - mid_sums[1] / total - normed * (mid_sums[0] / total))
        ).astype(BF)
        patch_grad = mm(d_spatial, spatial_w[u], ((1,), (1,)))
        d_act = adjoint(patch_grad, act.shape).reshape(rows, depth)
        s_term = mm(patches_of(act), d_spatial, ((0,), (0,))).astype(BF)
        spatial_grads[u] = sum_over(s_term.reshape(n_f, -1, mid), "frames")
        norm_grads[u] = (mid_sums, out_sums)
        if u > 0:
            upstream = sum_over(split_columns(d_act.astype(BF), n_r), "rep")
            upstream = upstream * silu_slope(saved[u - 1][7])
        else:
            mine = jnp.arange(n_r)[:, None, None] == me_r
            parts = split_columns(d_act, n_r) + jnp.where(mine, summed_grad[None], 0.0)
            parts = parts.astype(BF).reshape(n_r, pixels, n_r, own_frames, cols)
            parts = parts.transpose(2, 3, 1, 0, 4).reshape(n_r, own_frames * pixels, depth)
            input_grad = sum_over(parts, "rep").reshape(frames_in.shape)

    flat = jnp.concatenate(
        [jnp.concatenate([m.reshape(-1), o.reshape(-1)]) for m, o in norm_grads]
    )
    flat = from_all(flat, "rep").reshape(n_r, units, -1)
    mid_grad = flat[:, :, : 2 * mid].reshape(n_r, units, 2, mid).transpose(1, 2, 0, 3)
    mid_grad = mid_grad.reshape(units, 2, n_r * mid)
    out_grad = flat[:, :, 2 * mid :].reshape(n_r, units, 2, cols).transpose(1, 2, 0, 3)
    out_grad = out_grad.reshape(units, 2, depth)

    spatial_new, spatial_first_new, spatial_second_new = adam_step(
        spatial_weights, jnp.stack(spatial_grads), spatial_first, spatial_second, RATE_WEIGHT, DECAY
    )
    temporal_new, temporal_first_new, temporal_second_new = adam_step(
        temporal_weights, jnp.stack(temporal_grads), temporal_first, temporal_second, RATE_WEIGHT, DECAY
    )
    mid_new, mid_first_new, mid_second_new = adam_step(
        mid_norm, mid_grad, mid_first, mid_second, RATE_NORM, 0.0
    )
    out_new, out_first_new, out_second_new = adam_step(
        out_norm, out_grad, out_first, out_second, RATE_NORM, 0.0
    )
    return (
        block_out, input_grad,
        spatial_new, spatial_first_new, spatial_second_new, spatial_new.astype(BF),
        temporal_new, temporal_first_new, temporal_second_new, temporal_new.astype(BF),
        mid_new, mid_first_new, mid_second_new,
        out_new, out_first_new, out_second_new,
    )


def solution(mesh):
    by_frame = P(("frames", "rep"), None, None, None)
    by_block = P(None, "frames", "rep")
    placed = (by_frame, by_frame, P()) + (by_block,) * 6 + (P(),) * 6
    return jax.shard_map(
        on_device,
        mesh=mesh,
        in_specs=placed,
        out_specs=(by_frame, by_frame) + (by_block,) * 8 + (P(),) * 6,
        check_vma=False,
    )
```

```python
import functools

import jax
import jax.numpy as jnp
from jax import lax
from jax.experimental import pallas as pl
from jax.experimental.pallas import tpu as pltpu
from jax.sharding import PartitionSpec as P

STEP = 5
NORM_EPS = 1e-05
ADAM_EPS = 1e-08
BETA_ONE = 0.5
BETA_TWO = 0.5
RATE_WEIGHT = 0.015
RATE_NORM = 0.2
DECAY = 0.05
BF = jnp.bfloat16
F32 = jnp.float32
MIB = 1 << 20
VMEM = pl.BlockSpec(memory_space=pltpu.VMEM)
SMEM = pl.BlockSpec(memory_space=pltpu.SMEM)
LANES = 128


def shape(dims, dtype):
    return jax.ShapeDtypeStruct(tuple(dims), dtype)


def run(body, outs, args, name, scratch=(), limit=40, scalars=0, flops=0, moved=0):
    return pl.pallas_call(
        body,
        out_shape=tuple(outs),
        in_specs=[SMEM] * scalars + [VMEM] * (len(args) - scalars),
        out_specs=tuple(VMEM for _ in outs),
        scratch_shapes=list(scratch),
        compiler_params=pltpu.CompilerParams(vmem_limit_bytes=limit * MIB),
        cost_estimate=pl.CostEstimate(flops=flops, bytes_accessed=moved, transcendentals=0),
        name=name,
    )(*args)


def sigmoid(v):
    return 1.0 / (1.0 + jnp.exp(-v))


def silu(v):
    return v / (1.0 + jnp.exp(-v))


def silu_slope(v):
    s = sigmoid(v)
    return s * (1.0 + v * (1.0 - s))


def mm(a, b, dims):
    return lax.dot_general(a, b, (dims, ((), ())), preferred_element_type=F32)


def put_moments(values, out_ref):
    rows = values.shape[0]
    mean = jnp.sum(values, axis=0, keepdims=True) * (1.0 / rows)
    off = values - mean
    out_ref[0:1, :] = mean
    out_ref[1:2, :] = jnp.sum(off * off, axis=0, keepdims=True)


def joined_moments(both, rows):
    count = both.shape[0]
    mean = jnp.sum(both[:, 0:1], axis=0) * (1.0 / count)
    off = both[:, 0:1] - mean[None]
    total = jnp.sum(both[:, 1:2] + rows * (off * off), axis=0)
    return mean, lax.rsqrt(total * (1.0 / (rows * count)) + NORM_EPS)


def put_sums(upstream, normed, out_ref):
    out_ref[0:1, :] = jnp.sum(upstream * normed, axis=0, keepdims=True)
    out_ref[1:2, :] = jnp.sum(upstream, axis=0, keepdims=True)


def convolve(pad, w_ref, acc_ref, dims):
    height, width, frames, depth = dims
    rows = height * width * frames

    def tap(k, carry):
        piece = pad[pl.ds(k // 3, height), pl.ds(k % 3, width)]
        piece = piece.reshape(rows, depth).astype(BF)
        w = w_ref[:, pl.ds(pl.multiple_of(k * depth, LANES), depth)]
        part = mm(piece, w, ((1,), (1,)))

        @pl.when(k == 0)
        def _():
            acc_ref[...] = part

        @pl.when(k > 0)
        def _():
            acc_ref[...] += part

        return carry

    lax.fori_loop(0, 9, tap, 0)


def widened(scr, values, before, after):
    frames = values.shape[1]
    scr[:, 8 : 8 + frames, :] = values
    scr[:, 7:8, :] = before
    scr[:, 8 + frames : 9 + frames, :] = after


def dense_wire(mid, k, count):
    return mid % 32 == 0 and (2 * k) % LANES == 0 and k % LANES == LANES // 2 and count % 2 == 0


def low_half(shape_):
    return lax.broadcasted_iota(jnp.int32, shape_, 1) < LANES // 2


def fold(top, bottom, out_ref, k):
    edge = k - LANES // 2
    out_ref[:, 0:edge] = top[:, 0:edge].astype(out_ref.dtype)
    mixed = jnp.where(low_half((top.shape[0], LANES)), top[:, edge : edge + LANES], bottom[:, 0:LANES])
    out_ref[:, edge : edge + LANES] = mixed.astype(out_ref.dtype)
    out_ref[:, edge + LANES : 2 * k] = bottom[:, LANES : k + LANES // 2].astype(out_ref.dtype)


def pack_body(w_ref, out_ref, scr):
    units, mid, k = w_ref.shape
    half, wide = mid // 2, k + LANES // 2
    for u in range(units):
        scr[:, 0:k] = w_ref[u]
        fold(scr[0:half, :], pltpu.roll(scr[half:mid, :], LANES // 2, 1), out_ref.at[u], k)


def unpack_body(wire_ref, out_ref):
    count, half, double = wire_ref.shape
    k = double // 2
    wide, back = k + LANES // 2, k
    edge = k - LANES // 2
    for i in range(count // 2):
        even, odd = wire_ref[2 * i].astype(F32), wire_ref[2 * i + 1].astype(F32)
        pairs = (
            (0, even[:, 0:wide], pltpu.roll(odd[:, 0:wide], LANES // 2, 1)),
            (half, pltpu.roll(even[:, edge:double], back, 1), odd[:, edge:double]),
        )
        for start, top, bottom in pairs:
            fold(top, bottom, out_ref.at[start : start + half, double * i : double * (i + 1)], k)


def spatial_body(act_ref, w_ref, s_ref, first_ref, last_ref, mom_ref, pad, *, dims):
    height, width, frames, depth = dims
    pad[...] = jnp.zeros(pad.shape, F32)
    pad[1 : height + 1, 1 : width + 1] = act_ref[...].astype(F32).reshape(dims)
    convolve(pad, w_ref, s_ref, dims)
    put_spatial(s_ref, first_ref, last_ref, mom_ref, dims)


def put_spatial(s_ref, first_ref, last_ref, mom_ref, dims):
    height, width, frames, depth = dims
    values = s_ref[...]
    put_moments(values, mom_ref)
    grid = values.reshape(height * width, frames, values.shape[-1])
    first_ref[...] = grid[:, 0:1, :]
    last_ref[...] = grid[:, frames - 1 : frames, :]


def next_body(
    ids_ref, t0, t1, t2, t3, both_ref, norm_ref, w_ref,
    s_ref, first_ref, last_ref, mom_ref, act_ref, pad, *, dims
):
    height, width, frames, depth = dims
    rows = height * width * frames
    pad[...] = jnp.zeros(pad.shape, F32)
    for j, t_ref in enumerate((t0, t1, t2, t3)):
        b = ids_ref[j]
        mean, inverse = joined_moments(both_ref[:, b], rows)
        norm = norm_ref[b]
        y = (t_ref[...].astype(F32) - mean) * (inverse * norm[0:1]) + norm[1:2]
        a = silu(y)
        at = pl.ds(pl.multiple_of(b * LANES, LANES), LANES)
        act_ref[:, at] = a.astype(BF)
        pad[1 : height + 1, 1 : width + 1, :, at] = a.reshape(height, width, frames, LANES)
    convolve(pad, w_ref, s_ref, dims)
    put_spatial(s_ref, first_ref, last_ref, mom_ref, dims)


def temporal_body(
    ids_ref, s_ref, both_ref, before_ref, after_ref, norm_ref, keep_ref, w_ref,
    send_ref, kept_ref, win_ref, stat_ref, scr, part, *, dims
):
    height, width, frames, depth = dims
    pixels = height * width
    rows = pixels * frames
    mid = s_ref.shape[-1]
    mean, inverse = joined_moments(both_ref[...], rows)
    stat_ref[0:1, :] = mean
    stat_ref[1:2, :] = inverse
    scale, bias = inverse * norm_ref[0:1], norm_ref[1:2]

    def active(v):
        return silu((v - mean) * scale + bias)

    middle = active(s_ref[...])
    widened(
        scr, middle.reshape(pixels, frames, mid),
        active(before_ref[...].reshape(pixels, mid)).reshape(pixels, 1, mid),
        active(after_ref[...].reshape(pixels, mid)).reshape(pixels, 1, mid),
    )
    win_ref[0] = (scr[:, 7 : 7 + frames, :] * keep_ref[0][None]).reshape(rows, mid).astype(BF)
    win_ref[1] = middle.astype(BF)
    win_ref[2] = (scr[:, 9 : 9 + frames, :] * keep_ref[1][None]).reshape(rows, mid).astype(BF)
    part[...] = mm(win_ref[0], w_ref[0], ((1,), (0,)))
    part[...] += mm(win_ref[1], w_ref[1], ((1,), (0,)))
    part[...] += mm(win_ref[2], w_ref[2], ((1,), (0,)))
    put_halves(ids_ref, part, send_ref, kept_ref)


def put_halves(ids_ref, part, send_ref, kept_ref):
    core = ids_ref[4]
    for i in range(2):
        other = pl.multiple_of((2 * i + 1 - core) * LANES, LANES)
        own = pl.multiple_of((2 * i + core) * LANES, LANES)
        send_ref[i] = part[:, pl.ds(other, LANES)].astype(BF)
        kept_ref[i] = part[:, pl.ds(own, LANES)]


def total_body(ids_ref, got_ref, kept_ref, last_ref, t_ref, low_ref, mom_ref):
    x = ids_ref[5]
    t = got_ref[x].astype(F32) + kept_ref[x] + last_ref[...].astype(F32)
    t_ref[...] = t
    low_ref[...] = t.astype(BF)
    put_moments(t, mom_ref)


def edges_body(b0, b1, b2, b3, first_ref, last_ref, *, dims):
    height, width, frames, depth = dims
    for j, ref in enumerate((b0, b1, b2, b3)):
        grid = ref[...].astype(F32).reshape(height * width, frames, LANES)
        first_ref[j] = grid[:, 0:1, :]
        last_ref[j] = grid[:, frames - 1 : frames, :]


def top_body(ids_ref, t_ref, both_ref, norm_ref, x_ref, cot_ref, block_ref, g_ref, low_ref, sums_ref):
    rows = t_ref.shape[0]
    b = ids_ref[0]
    mean, inverse = joined_moments(both_ref[:, b], rows)
    norm = norm_ref[b]
    normed = (t_ref[...] - mean) * inverse
    summed = normed * norm[0:1] + norm[1:2] + x_ref[...].astype(F32)
    block_ref[...] = silu(summed).astype(BF)
    g = cot_ref[...].astype(F32) * silu_slope(summed)
    g_ref[...] = g
    low_ref[...] = g.astype(BF)
    put_sums(g, normed, sums_ref)


def below_body(ids_ref, got_ref, kept_ref, last_ref, t_ref, both_ref, norm_ref, low_ref, sums_ref):
    rows = t_ref.shape[0]
    b, x = ids_ref[0], ids_ref[5]
    d_act = got_ref[x].astype(F32) + kept_ref[x] + last_ref[...].astype(F32)
    mean, inverse = joined_moments(both_ref[:, b], rows)
    norm = norm_ref[b]
    normed = (t_ref[...] - mean) * inverse
    g = d_act * silu_slope(normed * norm[0:1] + norm[1:2])
    low_ref[...] = g.astype(BF)
    put_sums(g, normed, sums_ref)


def dt_body(
    ids_ref, g0, g1, g2, g3, t0, t1, t2, t3, both_ref, sums_ref, norm_ref, win_ref,
    dt_ref, coef_ref, grad_ref, sum_ref, *, total
):
    rows = g0.shape[0]
    mid = win_ref.shape[-1]
    n_r = norm_ref.shape[0]
    for j, (g_ref, t_ref) in enumerate(((g0, t0), (g1, t1), (g2, t2), (g3, t3))):
        b = ids_ref[j]
        mean, inverse = joined_moments(both_ref[:, b], rows)
        sums = jnp.sum(sums_ref[:, b], axis=0)
        if j == 0:
            sum_ref[...] = sums
        c1 = norm_ref[b][0:1] * inverse
        c2 = c1 * sums[1:2] * (1.0 / total)
        c3 = c1 * inverse * sums[0:1] * (1.0 / total)
        coef_ref[j] = jnp.concatenate([c1, c2, c3, mean], axis=0)
        d = c1 * g_ref[...].astype(F32) - c2 - c3 * (t_ref[...].astype(F32) - mean)
        dt_ref[:, pl.ds(pl.multiple_of(b * LANES, LANES), LANES)] = d.astype(BF)
    dt = dt_ref[...]
    for k in range(3):
        term = mm(win_ref[k], dt, ((0,), (0,)))
        for r in range(n_r):
            grad_ref[r, k * mid : (k + 1) * mid, :] = term[:, r * LANES : (r + 1) * LANES].astype(BF)


def middle_body(
    ids_ref, dt_ref, coef_ref, gb_ref, ga_ref, tb_ref, ta_ref, keep_ref, w_ref, s_ref, stat_ref, norm_ref,
    d_ref, sums_ref, scr, *, dims
):
    height, width, frames, depth = dims
    pixels = height * width
    rows = pixels * frames
    scr[:, 8 : 8 + frames, :] = dt_ref[...].astype(F32).reshape(pixels, frames, depth)
    for j in range(4):
        at = pl.ds(pl.multiple_of(ids_ref[j] * LANES, LANES), LANES)
        c = coef_ref[j]

        def halo(g, t):
            d = c[0:1] * g.reshape(pixels, LANES) - c[1:2] - c[2:3] * (t.reshape(pixels, LANES) - c[3:4])
            return d.astype(BF).astype(F32).reshape(pixels, 1, LANES)

        scr[:, 7:8, at] = halo(gb_ref[j], tb_ref[j])
        scr[:, 8 + frames : 9 + frames, at] = halo(ga_ref[j], ta_ref[j])
    later = (scr[:, 9 : 9 + frames, :] * keep_ref[1][None]).reshape(rows, depth).astype(BF)
    earlier = (scr[:, 7 : 7 + frames, :] * keep_ref[0][None]).reshape(rows, depth).astype(BF)
    d_ref[...] = mm(later, w_ref[0], ((1,), (1,)))
    d_ref[...] += mm(dt_ref[...], w_ref[1], ((1,), (1,)))
    d_ref[...] += mm(earlier, w_ref[2], ((1,), (1,)))
    normed = (s_ref[...] - stat_ref[0:1]) * stat_ref[1:2]
    d = d_ref[...] * silu_slope(normed * norm_ref[0:1] + norm_ref[1:2])
    d_ref[...] = d
    put_sums(d, normed, sums_ref)


def spatial_grad(d_ref, s_ref, stat_ref, norm_ref, sums_ref, ds_ref, sum_ref, total):
    sums = jnp.sum(sums_ref[...], axis=0)
    sum_ref[...] = sums
    inverse = stat_ref[1:2]
    normed = (s_ref[...] - stat_ref[0:1]) * inverse
    d = d_ref[...] - sums[1:2] * (1.0 / total) - normed * (sums[0:1] * (1.0 / total))
    ds_ref[...] = (norm_ref[0:1] * inverse * d).astype(BF)


def adjoint(ds_ref, w_ref, pad, dims):
    height, width, frames, depth = dims
    pad[...] = jnp.zeros(pad.shape, F32)

    def tap(k, carry):
        w = w_ref[:, pl.ds(pl.multiple_of(k * depth, LANES), depth)]
        part = mm(ds_ref[...], w, ((1,), (0,)))
        at = (pl.ds(k // 3, height), pl.ds(k % 3, width))
        pad[at] = pad[at] + part.reshape(dims)
        return carry

    lax.fori_loop(0, 9, tap, 0)


def input_body(
    ids_ref, d_ref, s_ref, stat_ref, norm_ref, sums_ref, w_ref,
    ds_ref, send_ref, kept_ref, sum_ref, pad, part, *, dims, total
):
    height, width, frames, depth = dims
    spatial_grad(d_ref, s_ref, stat_ref, norm_ref, sums_ref, ds_ref, sum_ref, total)
    adjoint(ds_ref, w_ref, pad, dims)
    part[...] = pad[1 : height + 1, 1 : width + 1].reshape(part.shape)
    put_halves(ids_ref, part, send_ref, kept_ref)


def last_body(
    ids_ref, d_ref, s_ref, stat_ref, norm_ref, sums_ref, w_ref, g_ref,
    ds_ref, out_ref, sum_ref, pad, *, dims, total
):
    height, width, frames, depth = dims
    spatial_grad(d_ref, s_ref, stat_ref, norm_ref, sums_ref, ds_ref, sum_ref, total)
    adjoint(ds_ref, w_ref, pad, dims)
    at = (slice(1, height + 1), slice(1, width + 1), slice(None),
          pl.ds(pl.multiple_of(ids_ref[0] * LANES, LANES), LANES))
    pad[at] = pad[at] + g_ref[...].reshape(height, width, frames, LANES)
    out_ref[...] = pad[1 : height + 1, 1 : width + 1].reshape(out_ref.shape).astype(BF)


def weight_body(act_ref, ds_ref, out_ref, pad, acc, *, dims, dense):
    height, width, frames, depth = dims
    rows = height * width * frames
    mid = ds_ref.shape[-1]
    pad[...] = jnp.zeros(pad.shape, F32)
    pad[1 : height + 1, 1 : width + 1] = act_ref[...].astype(F32).reshape(dims)
    flipped = ds_ref[...].astype(F32).T.astype(BF)

    def tap(k, carry):
        piece = pad[pl.ds(k // 3, height), pl.ds(k % 3, width)]
        piece = piece.reshape(rows, depth).astype(BF)
        acc[:, pl.ds(pl.multiple_of(k * depth, LANES), depth)] = mm(flipped, piece, ((1,), (0,)))
        return carry

    lax.fori_loop(0, 9, tap, 0)
    if not dense:
        out_ref[...] = acc[...].astype(BF)
        return
    count, half, double = out_ref.shape
    k = double // 2
    wide, edge = k + LANES // 2, k - LANES // 2
    for f in range(count):
        if f % 2 == 0:
            top = acc[0:half, k * f : k * f + wide]
            bottom = pltpu.roll(acc[half:mid, k * f : k * f + wide], LANES // 2, 1)
        else:
            start = k * f - LANES // 2
            top = pltpu.roll(acc[0:half, start : start + wide], k, 1)
            bottom = acc[half:mid, start : start + wide]
        fold(top, bottom, out_ref.at[f], k)


def adam_step(param, gradient, moment_one, moment_two, rate, decay):
    first_new = BETA_ONE * moment_one + (1.0 - BETA_ONE) * gradient
    second_new = BETA_TWO * moment_two + (1.0 - BETA_TWO) * gradient * gradient
    fix_one = 1.0 - BETA_ONE**STEP
    fix_two = 1.0 - BETA_TWO**STEP
    update = first_new / fix_one / (jnp.sqrt(second_new / fix_two) + ADAM_EPS)
    return (param - rate * (update + decay * param), first_new, second_new)


def unfold(total, k):
    top = total[:, 0:k]
    bottom = total[:, k : 2 * k]
    return jnp.concatenate([top, bottom], axis=0)


def swap(parts, axis):
    return lax.all_to_all(parts, axis, 0, 0, tiled=True)


def from_all(value, axis):
    count = lax.axis_size(axis)
    return swap(jnp.broadcast_to(value[None], (count,) + value.shape), axis)


def across(value, bit):
    count = lax.axis_size("rep")
    return lax.ppermute(value, "rep", [(i, i ^ bit) for i in range(count)])


def from_group(value):
    far = across(value, 2)
    near = across(value, 1)
    return value, far, near, across(far, 1)


def neighbours(first, last):
    count = lax.axis_size("frames")
    before = lax.ppermute(last, "frames", [(i, i + 1) for i in range(count - 1)])
    after = lax.ppermute(first, "frames", [(i + 1, i) for i in range(count - 1)])
    return before, after


def reduced(send, kept, x):
    got = across(send, 1)
    away = lax.dynamic_index_in_dim(got, 1 - x, 0, False).astype(F32)
    away = away + lax.dynamic_index_in_dim(kept, 1 - x, 0, False)
    return got, kept, across(away.astype(BF), 2)


def sum_over(parts, axis):
    return jnp.sum(swap(parts, axis).astype(F32), axis=0)


def on_device(
    frames_in, cotangent, lengths,
    spatial_weights, spatial_first, spatial_second,
    temporal_weights, temporal_first, temporal_second,
    mid_norm, mid_first, mid_second,
    out_norm, out_first, out_second,
):
    own_frames, height, width, depth = frames_in.shape
    n_f, n_r = lax.axis_size("frames"), lax.axis_size("rep")
    assert n_r == 4 and depth == n_r * LANES
    me = lax.axis_index("rep")
    frames = own_frames * n_r
    pixels = height * width
    rows = pixels * frames
    total = float(rows * n_f)
    dims = (height, width, frames, depth)
    units, k, mid = spatial_weights.shape
    cols = LANES
    everyone = ("frames", "rep")
    ids = jnp.stack([me, me ^ 2, me ^ 1, me ^ 3, me & 1, me >> 1]).astype(jnp.int32)
    dense = dense_wire(mid, k, n_f)
    spatial_flops = 2 * rows * 9 * depth * mid
    temporal_flops = 2 * rows * 3 * depth * mid
    pad = pltpu.VMEM((height + 2, width + 2, frames, depth), F32)

    turned = jnp.swapaxes(spatial_weights, 1, 2)
    if dense:
        (wire,) = run(
            pack_body, [shape((units, mid // 2, 2 * k), BF)], [turned], "pack",
            [pltpu.VMEM((mid, k + LANES // 2), F32)],
        )
    else:
        wire = turned.astype(BF)
    temporal_low = temporal_weights.astype(BF)
    spatial_w, temporal_w = [], []
    for u in range(units):
        held = lax.all_gather(wire[u], "frames", axis=0)
        if dense:
            (held,) = run(unpack_body, [shape((mid, n_f * k), BF)], [held], "unpack")
        else:
            held = held.transpose(1, 0, 2).reshape(mid, n_f * k)
        spatial_w.append(held)
        shard = lax.all_gather(temporal_low[u], "frames", axis=0, tiled=True)
        shard = shard.reshape(3, n_r, mid, cols).transpose(1, 0, 2, 3)
        shard = swap(shard, "rep")
        temporal_w.append(shard.transpose(1, 2, 0, 3).reshape(3, mid, depth))

    frame_ids = lax.axis_index("frames") * frames + jnp.arange(frames, dtype=jnp.int32)
    clip_ends = jnp.cumsum(lengths)
    starts = jnp.concatenate([jnp.zeros((1,), jnp.int32), clip_ends[:-1]])
    opening = jnp.any(frame_ids[:, None] == starts[None, :], axis=1)
    closing = jnp.any((frame_ids + 1)[:, None] == clip_ends[None, :], axis=1)
    keep = jnp.where(jnp.stack([opening, closing]), 0.0, 1.0).astype(F32)[:, :, None]

    act = lax.all_gather(frames_in, "rep", axis=0, tiled=True).transpose(1, 2, 0, 3).reshape(rows, depth)
    state_cols = lax.dynamic_slice_in_dim(act, me * cols, cols, axis=1)
    cot = cotangent.reshape(own_frames, pixels, n_r, cols).transpose(2, 0, 1, 3)
    cot = swap(cot, "rep").reshape(frames, pixels, cols).transpose(1, 0, 2).reshape(rows, cols)

    mid_own = lax.dynamic_slice_in_dim(mid_norm, me * mid, mid, axis=2)
    out_split = out_norm.reshape(units, 2, n_r, cols).transpose(0, 2, 1, 3)

    halo = shape((pixels, 1, mid), F32)
    column = shape((rows, cols), BF)
    saved = []
    for u in range(units):
        outs = [shape((rows, mid), F32), halo, halo, shape((2, mid), F32)]
        if u == 0:
            spatial, first, last, mom = run(
                functools.partial(spatial_body, dims=dims), outs, [act, spatial_w[u]],
                f"spatial_{u}", [pad], flops=spatial_flops, moved=8 * MIB,
            )
        else:
            spatial, first, last, mom, act = run(
                functools.partial(next_body, dims=dims), outs + [shape((rows, depth), BF)],
                [ids, *t_group, both, out_split[u - 1], spatial_w[u]],
                f"spatial_{u}", [pad], scalars=1, flops=spatial_flops, moved=8 * MIB,
            )
        mid_both = from_all(mom, "frames")
        before, after = neighbours(first, last)
        send, kept, window, stat = run(
            functools.partial(temporal_body, dims=dims),
            [shape((2, rows, cols), BF), shape((2, rows, cols), F32), shape((3, rows, mid), BF), shape((2, mid), F32)],
            [ids, spatial, mid_both, before, after, mid_own[u], keep, temporal_w[u]],
            f"temporal_{u}", [pltpu.VMEM((pixels, frames + 16, mid), F32), pltpu.VMEM((rows, depth), F32)],
            scalars=1, flops=temporal_flops, moved=8 * MIB,
        )
        t, low, mom = run(
            total_body, [shape((rows, cols), F32), column, shape((2, cols), F32)],
            [ids, *reduced(send, kept, me >> 1)], f"total_{u}", scalars=1, moved=3 * MIB,
        )
        both = from_all(mom, everyone).reshape(n_f, n_r, 2, cols)
        t_group = from_group(low)
        edge = [shape((n_r, pixels, 1, cols), F32)] * 2
        t_edges = neighbours(*run(functools.partial(edges_body, dims=dims), edge, t_group, f"edges_{u}"))
        saved.append((act, spatial, stat, window, t, t_group, both, t_edges))

    d_norms = [None] * units
    spatial_parts, temporal_parts = [None] * units, [None] * units
    for u in reversed(range(units)):
        act, spatial, stat, window, t, t_group, both, t_edges = saved[u]
        if u == units - 1:
            block, summed_grad, low, sums = run(
                top_body, [column, shape((rows, cols), F32), column, shape((2, cols), F32)],
                [ids, t, both, out_split[u], state_cols, cot], "top", scalars=1, moved=3 * MIB,
            )
        else:
            low, sums = run(
                below_body, [column, shape((2, cols), F32)],
                [ids, *reduced(send, kept, me >> 1), t, both, out_split[u]], f"below_{u}", scalars=1, moved=3 * MIB,
            )
        sums = from_all(sums, everyone).reshape(n_f, n_r, 2, cols)
        g_group = from_group(low)
        g_edges = neighbours(*run(functools.partial(edges_body, dims=dims), edge, g_group, f"g_edges_{u}"))
        dt, coef, t_grad, out_sums = run(
            functools.partial(dt_body, total=total),
            [shape((rows, depth), BF), shape((n_r, 4, cols), F32), shape((n_r, 3 * mid, cols), BF), shape((2, cols), F32)],
            [ids, *g_group, *t_group, both, sums, out_split[u], window],
            f"dt_{u}", scalars=1, flops=temporal_flops, moved=8 * MIB,
        )
        t_grad = swap(t_grad, "rep").reshape(n_r, 3, mid, cols).transpose(1, 0, 2, 3)
        temporal_parts[u] = swap(t_grad.reshape(n_f, -1, cols), "frames")
        d_mid, sums = run(
            functools.partial(middle_body, dims=dims), [shape((rows, mid), F32), shape((2, mid), F32)],
            [ids, dt, coef, g_edges[0], g_edges[1], t_edges[0], t_edges[1], keep, temporal_w[u], spatial, stat, mid_own[u]],
            f"middle_{u}", [pltpu.VMEM((pixels, frames + 16, depth), F32)],
            scalars=1, flops=temporal_flops, moved=8 * MIB,
        )
        sums = from_all(sums, "frames")
        ds_shape, sum_shape = shape((rows, mid), BF), shape((2, mid), F32)
        if u > 0:
            ds, send, kept, mid_sums = run(
                functools.partial(input_body, dims=dims, total=total),
                [ds_shape, shape((2, rows, cols), BF), shape((2, rows, cols), F32), sum_shape],
                [ids, d_mid, spatial, stat, mid_own[u], sums, spatial_w[u]],
                f"input_{u}", [pad, pltpu.VMEM((rows, depth), F32)], scalars=1, flops=spatial_flops, moved=8 * MIB,
            )
        else:
            ds, d_input, mid_sums = run(
                functools.partial(last_body, dims=dims, total=total),
                [ds_shape, shape((rows, depth), BF), sum_shape],
                [ids, d_mid, spatial, stat, mid_own[u], sums, spatial_w[u], summed_grad],
                f"input_{u}", [pad], scalars=1, flops=spatial_flops, moved=8 * MIB,
            )
        wire_shape = shape((n_f, mid // 2, 2 * k) if dense else (mid, n_f * k), BF)
        (s_grad,) = run(
            functools.partial(weight_body, dims=dims, dense=dense), [wire_shape], [act, ds],
            f"weight_{u}", [pad, pltpu.VMEM((mid, n_f * k), F32)], flops=spatial_flops, moved=8 * MIB,
        )
        if not dense:
            s_grad = s_grad.reshape(mid, n_f, k).transpose(1, 0, 2)
        spatial_parts[u] = swap(s_grad, "frames")
        d_norms[u] = (mid_sums, out_sums)

    parts = d_input.reshape(pixels, n_r, own_frames, depth).transpose(1, 2, 0, 3)
    input_grad = sum_over(parts, "rep").reshape(frames_in.shape)
    block = swap(block.reshape(pixels, n_r, own_frames, cols).transpose(1, 2, 0, 3), "rep")
    block_out = block.transpose(1, 2, 0, 3).reshape(frames_in.shape)

    flat = jnp.concatenate([jnp.concatenate([m.reshape(-1), o.reshape(-1)]) for m, o in d_norms])
    flat = from_all(flat, "rep").reshape(n_r, units, -1)
    mid_grad = flat[:, :, : 2 * mid].reshape(n_r, units, 2, mid).transpose(1, 2, 0, 3)
    mid_grad = mid_grad.reshape(units, 2, n_r * mid)
    out_grad = flat[:, :, 2 * mid :].reshape(n_r, units, 2, cols).transpose(1, 2, 0, 3)
    out_grad = out_grad.reshape(units, 2, depth)

    spatial_grads = []
    for part in spatial_parts:
        grad = jnp.sum(part.astype(F32), axis=0)
        spatial_grads.append(unfold(grad, k) if dense else grad)
    temporal_grads = [jnp.sum(part.astype(F32), axis=0) for part in temporal_parts]

    flip = functools.partial(jnp.swapaxes, axis1=1, axis2=2)
    s_new, s_first_new, s_second_new = adam_step(
        flip(spatial_weights), jnp.stack(spatial_grads), flip(spatial_first), flip(spatial_second), RATE_WEIGHT, DECAY
    )
    temporal_new, temporal_first_new, temporal_second_new = adam_step(
        temporal_weights, jnp.stack(temporal_grads), temporal_first, temporal_second, RATE_WEIGHT, DECAY
    )
    mid_new, mid_first_new, mid_second_new = adam_step(mid_norm, mid_grad, mid_first, mid_second, RATE_NORM, 0.0)
    out_new, out_first_new, out_second_new = adam_step(out_norm, out_grad, out_first, out_second, RATE_NORM, 0.0)
    return (
        block_out, input_grad,
        flip(s_new), flip(s_first_new), flip(s_second_new), flip(s_new).astype(BF),
        temporal_new, temporal_first_new, temporal_second_new, temporal_new.astype(BF),
        mid_new, mid_first_new, mid_second_new,
        out_new, out_first_new, out_second_new,
    )


def solution(mesh):
    by_frame = P(("frames", "rep"), None, None, None)
    by_block = P(None, "frames", "rep")
    placed = (by_frame, by_frame, P()) + (by_block,) * 6 + (P(),) * 6
    return jax.shard_map(
        on_device,
        mesh=mesh,
        in_specs=placed,
        out_specs=(by_frame, by_frame) + (by_block,) * 8 + (P(),) * 6,
        check_vma=False,
    )
```

```python
import functools

import jax
import jax.numpy as jnp
from jax import lax
from jax.experimental import pallas as pl
from jax.experimental.pallas import tpu as pltpu
from jax.sharding import PartitionSpec as P

STEP = 5
NORM_EPS = 1e-05
ADAM_EPS = 1e-08
BETA_ONE = 0.5
BETA_TWO = 0.5
RATE_WEIGHT = 0.015
RATE_NORM = 0.2
DECAY = 0.05
BF = jnp.bfloat16
F32 = jnp.float32
MIB = 1 << 20
VMEM = pl.BlockSpec(memory_space=pltpu.VMEM)
SMEM = pl.BlockSpec(memory_space=pltpu.SMEM)
LANES = 128


def shape(dims, dtype):
    return jax.ShapeDtypeStruct(tuple(dims), dtype)


def run(body, outs, args, name, scratch=(), limit=24, scalars=0, flops=0, moved=0, after=()):
    def kernel(*refs):
        body(*refs[len(after) :])

    return pl.pallas_call(
        kernel,
        out_shape=tuple(outs),
        in_specs=[pl.BlockSpec(memory_space=pl.ANY)] * len(after) + [SMEM] * scalars + [VMEM] * (len(args) - scalars),
        out_specs=tuple(VMEM for _ in outs),
        scratch_shapes=list(scratch),
        compiler_params=pltpu.CompilerParams(vmem_limit_bytes=limit * MIB),
        cost_estimate=pl.CostEstimate(flops=30 * flops, bytes_accessed=30 * moved, transcendentals=0),
        name=name,
    )(*after, *args)


def sigmoid(v):
    return 1.0 / (1.0 + jnp.exp(-v))


def silu(v):
    return v / (1.0 + jnp.exp(-v))


def silu_slope(v):
    s = sigmoid(v)
    return s * (1.0 + v * (1.0 - s))


def mm(a, b, dims):
    return lax.dot_general(a, b, (dims, ((), ())), preferred_element_type=F32)


def put_moments(values, out_ref):
    rows = values.shape[0]
    mean = jnp.sum(values, axis=0, keepdims=True) * (1.0 / rows)
    off = values - mean
    out_ref[0:1, :] = mean
    out_ref[1:2, :] = jnp.sum(off * off, axis=0, keepdims=True)


def joined_moments(both, rows):
    count = both.shape[0]
    mean = jnp.sum(both[:, 0:1], axis=0) * (1.0 / count)
    off = both[:, 0:1] - mean[None]
    total = jnp.sum(both[:, 1:2] + rows * (off * off), axis=0)
    return mean, lax.rsqrt(total * (1.0 / (rows * count)) + NORM_EPS)


def put_sums(upstream, normed, out_ref):
    out_ref[0:1, :] = jnp.sum(upstream * normed, axis=0, keepdims=True)
    out_ref[1:2, :] = jnp.sum(upstream, axis=0, keepdims=True)


def convolve(pad, w_ref, acc_ref, dims):
    height, width, frames, depth = dims
    rows = height * width * frames

    for k in range(9):
        i, j = k // 3, k % 3
        piece = pad[i : i + height, j : j + width].reshape(rows, depth).astype(BF)
        part = mm(piece, w_ref[:, k * depth : (k + 1) * depth], ((1,), (1,)))
        if k == 0:
            acc_ref[...] = part
        else:
            acc_ref[...] += part


def widened(scr, values, before, after):
    frames = values.shape[1]
    scr[:, 8 : 8 + frames, :] = values
    scr[:, 7:8, :] = before
    scr[:, 8 + frames : 9 + frames, :] = after


RING = (0, 2, 4, 6, 7, 5, 3, 1)


def can_ring(mid, k, k_t, count):
    return count == len(RING) and mid == 288 and k == 576 and k_t == 432


def ring_place(frame):
    return jnp.where(frame % 2 == 0, frame // 2, 7 - frame // 2)


def ring_device(place):
    place = place % 8
    return jnp.where(place < 4, 2 * place, 15 - 2 * place)


def low_half(shape_):
    return lax.broadcasted_iota(jnp.int32, shape_, 1) < LANES // 2


def fold(top, bottom, out_ref, k):
    edge = k - LANES // 2
    out_ref[:, 0:edge] = top[:, 0:edge].astype(out_ref.dtype)
    mixed = jnp.where(low_half((top.shape[0], LANES)), top[:, edge : edge + LANES], bottom[:, 0:LANES])
    out_ref[:, edge : edge + LANES] = mixed.astype(out_ref.dtype)
    out_ref[:, edge + LANES : 2 * k] = bottom[:, LANES : k + LANES // 2].astype(out_ref.dtype)


def pack_body(w_ref, t_ref, *refs):
    outs, scr = refs[:-1], refs[-1]
    units, mid, k = w_ref.shape
    half = mid // 2
    for u in range(units):
        scr[:, 0:k] = w_ref[u]
        fold(scr[0:half, :], pltpu.roll(scr[half:mid, :], LANES // 2, 1), outs[u].at[0:half], k)
        rows = outs[u].shape[0] - half
        for i in range(2 * k // LANES):
            at = slice(i * LANES, (i + 1) * LANES)
            outs[u][half:, at] = t_ref[u, rows * i : rows * (i + 1), :].astype(BF)


def unpack_temporal(f, slot, t_ref):
    rows = slot.shape[0]
    per = t_ref.shape[3] // rows
    for j in range(slot.shape[1] // LANES):
        block = 3 * f + j // per
        piece = slot[:, j * LANES : (j + 1) * LANES]
        t_ref[(block % 8) // 2, block // 8, block % 2, (j % per) * rows : (j % per + 1) * rows, :] = piece


def unpack_body(ids_ref, *refs):
    slots, outs = refs[:8], refs[-2:] if len(refs) == 10 else refs[9:]
    w_ref, t_ref = outs[:2]
    if len(outs) > 2:
        outs[2][...] = refs[8][...]
    half, k = w_ref.shape[0] // 2, w_ref.shape[1] // 8
    edge, wide = k - LANES // 2, k + LANES // 2
    for i, slot in enumerate(slots):
        f = ids_ref[6 + i]
        base = (f // 2) * (2 * k)
        values = slot[0:half, :].astype(F32)
        low = low_half((half, LANES))

        def at(start, size):
            return pl.ds(pl.multiple_of(base + start, LANES), size)

        @pl.when(f % 2 == 0)
        def _():
            for start, part in ((0, values[:, 0:wide]), (half, pltpu.roll(values[:, edge:], k, 1))):
                rows = slice(start, start + half)
                w_ref[rows, at(0, edge)] = part[:, 0:edge].astype(BF)
                old = w_ref[rows, at(edge, LANES)].astype(F32)
                w_ref[rows, at(edge, LANES)] = jnp.where(low, part[:, edge:wide], old).astype(BF)

        @pl.when(f % 2 == 1)
        def _():
            for start, part in ((0, pltpu.roll(values[:, 0:wide], LANES // 2, 1)), (half, values[:, edge:])):
                rows = slice(start, start + half)
                old = w_ref[rows, at(edge, LANES)].astype(F32)
                w_ref[rows, at(edge, LANES)] = jnp.where(low, old, part[:, 0:LANES]).astype(BF)
                w_ref[rows, at(edge + LANES, edge)] = part[:, LANES:wide].astype(BF)

        unpack_temporal(f, slot.at[half:], t_ref)


def spatial_body(act_ref, w_ref, s_ref, pad, *, dims):
    height, width, frames, depth = dims
    pad[...] = jnp.zeros(pad.shape, F32)
    pad[1 : height + 1, 1 : width + 1] = act_ref[...].astype(F32).reshape(dims)
    convolve(pad, w_ref, s_ref, dims)


def moments_body(s_ref, first_ref, last_ref, mom_ref, *, dims):
    put_spatial(s_ref, first_ref, last_ref, mom_ref, dims)


def put_spatial(s_ref, first_ref, last_ref, mom_ref, dims):
    height, width, frames, depth = dims
    values = s_ref[...]
    put_moments(values, mom_ref)
    grid = values.reshape(height * width, frames, values.shape[-1])
    first_ref[...] = grid[:, 0:1, :]
    last_ref[...] = grid[:, frames - 1 : frames, :]


def next_body(
    ids_ref, t0, t1, t2, t3, both_ref, norm_ref, w_ref,
    s_ref, first_ref, last_ref, mom_ref, act_ref, pad, *, dims
):
    height, width, frames, depth = dims
    rows = height * width * frames
    pad[...] = jnp.zeros(pad.shape, F32)
    for j, t_ref in enumerate((t0, t1, t2, t3)):
        b = ids_ref[j]
        mean, inverse = joined_moments(both_ref[:, b], rows)
        norm = norm_ref[b]
        y = (t_ref[...].astype(F32) - mean) * (inverse * norm[0:1]) + norm[1:2]
        a = silu(y)
        at = pl.ds(pl.multiple_of(b * LANES, LANES), LANES)
        act_ref[:, at] = a.astype(BF)
        pad[1 : height + 1, 1 : width + 1, :, at] = a.reshape(height, width, frames, LANES)
    convolve(pad, w_ref, s_ref, dims)
    put_spatial(s_ref, first_ref, last_ref, mom_ref, dims)


def temporal_body(
    ids_ref, s_ref, both_ref, before_ref, after_ref, norm_ref, keep_ref, w_ref,
    send_ref, kept_ref, win_ref, stat_ref, row_ref, scr, part, *, dims
):
    height, width, frames, depth = dims
    pixels = height * width
    rows = pixels * frames
    mid = s_ref.shape[-1]
    mean, inverse = joined_moments(both_ref[...], rows)
    stat_ref[0:1, :] = mean
    stat_ref[1:2, :] = inverse
    scale, bias = inverse * norm_ref[0:1], norm_ref[1:2]

    def active(v):
        return silu((v - mean) * scale + bias)

    middle = active(s_ref[...])
    widened(
        scr, middle.reshape(pixels, frames, mid),
        active(before_ref[...].reshape(pixels, mid)).reshape(pixels, 1, mid),
        active(after_ref[...].reshape(pixels, mid)).reshape(pixels, 1, mid),
    )
    win_ref[0] = (scr[:, 7 : 7 + frames, :] * keep_ref[0][None]).reshape(rows, mid).astype(BF)
    win_ref[1] = middle.astype(BF)
    win_ref[2] = (scr[:, 9 : 9 + frames, :] * keep_ref[1][None]).reshape(rows, mid).astype(BF)
    for r in range(w_ref.shape[0]):
        row_ref[:, :, r * LANES : (r + 1) * LANES] = w_ref[r]
    part[...] = mm(win_ref[0], row_ref[0], ((1,), (0,)))
    part[...] += mm(win_ref[1], row_ref[1], ((1,), (0,)))
    part[...] += mm(win_ref[2], row_ref[2], ((1,), (0,)))
    put_halves(ids_ref, part, send_ref, kept_ref)


def put_halves(ids_ref, part, send_ref, kept_ref):
    core = ids_ref[4]
    for i in range(2):
        other = pl.multiple_of((2 * i + 1 - core) * LANES, LANES)
        own = pl.multiple_of((2 * i + core) * LANES, LANES)
        send_ref[i] = part[:, pl.ds(other, LANES)].astype(BF)
        kept_ref[i] = part[:, pl.ds(own, LANES)]


def total_body(ids_ref, got_ref, kept_ref, last_ref, t_ref, low_ref, mom_ref):
    x = ids_ref[5]
    t = got_ref[x].astype(F32) + kept_ref[x] + last_ref[...].astype(F32)
    t_ref[...] = t
    low_ref[...] = t.astype(BF)
    put_moments(t, mom_ref)


def edges_body(*refs, dims):
    height, width, frames, depth = dims
    blocks, (first_ref, last_ref) = refs[:-2], refs[-2:]
    for j, ref in enumerate(blocks):
        grid = ref[...].astype(F32).reshape(height * width, frames, LANES)
        first_ref[j] = grid[:, 0:1, :]
        last_ref[j] = grid[:, frames - 1 : frames, :]


def top_body(ids_ref, t_ref, both_ref, norm_ref, x_ref, cot_ref, block_ref, g_ref, low_ref, sums_ref):
    rows = t_ref.shape[0]
    b = ids_ref[0]
    mean, inverse = joined_moments(both_ref[:, b], rows)
    norm = norm_ref[b]
    normed = (t_ref[...] - mean) * inverse
    own = pl.ds(pl.multiple_of(b * LANES, LANES), LANES)
    summed = normed * norm[0:1] + norm[1:2] + x_ref[:, own].astype(F32)
    block_ref[...] = silu(summed).astype(BF)
    g = cot_ref[...].astype(F32) * silu_slope(summed)
    g_ref[...] = g
    low_ref[...] = g.astype(BF)
    put_sums(g, normed, sums_ref)


def below_body(ids_ref, got_ref, kept_ref, last_ref, t_ref, both_ref, norm_ref, low_ref, sums_ref):
    rows = t_ref.shape[0]
    b, x = ids_ref[0], ids_ref[5]
    d_act = got_ref[x].astype(F32) + kept_ref[x] + last_ref[...].astype(F32)
    mean, inverse = joined_moments(both_ref[:, b], rows)
    norm = norm_ref[b]
    normed = (t_ref[...] - mean) * inverse
    g = d_act * silu_slope(normed * norm[0:1] + norm[1:2])
    low_ref[...] = g.astype(BF)
    put_sums(g, normed, sums_ref)


def dt_body(
    ids_ref, g0, g1, g2, g3, t0, t1, t2, t3, both_ref, sums_ref, norm_ref, win_ref,
    dt_ref, coef_ref, grad_ref, sum_ref, *, total
):
    rows = g0.shape[0]
    mid = win_ref.shape[-1]
    n_r = norm_ref.shape[0]
    for j, (g_ref, t_ref) in enumerate(((g0, t0), (g1, t1), (g2, t2), (g3, t3))):
        b = ids_ref[j]
        mean, inverse = joined_moments(both_ref[:, b], rows)
        sums = jnp.sum(sums_ref[:, b], axis=0)
        if j == 0:
            sum_ref[...] = sums
        c1 = norm_ref[b][0:1] * inverse
        c2 = c1 * sums[1:2] * (1.0 / total)
        c3 = c1 * inverse * sums[0:1] * (1.0 / total)
        coef_ref[j] = jnp.concatenate([c1, c2, c3, mean], axis=0)
        d = c1 * g_ref[...].astype(F32) - c2 - c3 * (t_ref[...].astype(F32) - mean)
        dt_ref[:, pl.ds(pl.multiple_of(b * LANES, LANES), LANES)] = d.astype(BF)
    dt = dt_ref[...]
    for k in range(3):
        term = mm(win_ref[k], dt, ((0,), (0,)))
        for r in range(n_r):
            grad_ref[r, k * mid : (k + 1) * mid, :] = term[:, r * LANES : (r + 1) * LANES].astype(BF)


def middle_body(
    ids_ref, dt_ref, coef_ref, before_ref, after_ref, keep_ref, w_ref, s_ref, stat_ref, norm_ref,
    d_ref, sums_ref, scr, *, dims
):
    height, width, frames, depth = dims
    pixels = height * width
    rows = pixels * frames
    scr[:, 8 : 8 + frames, :] = dt_ref[...].astype(F32).reshape(pixels, frames, depth)
    for j in range(4):
        at = pl.ds(pl.multiple_of(ids_ref[j] * LANES, LANES), LANES)
        c = coef_ref[j]

        def halo(g, t):
            d = c[0:1] * g.reshape(pixels, LANES) - c[1:2] - c[2:3] * (t.reshape(pixels, LANES) - c[3:4])
            return d.astype(BF).astype(F32).reshape(pixels, 1, LANES)

        scr[:, 7:8, at] = halo(before_ref[j], before_ref[4 + j])
        scr[:, 8 + frames : 9 + frames, at] = halo(after_ref[j], after_ref[4 + j])
    later = (scr[:, 9 : 9 + frames, :] * keep_ref[1][None]).reshape(rows, depth).astype(BF)
    earlier = (scr[:, 7 : 7 + frames, :] * keep_ref[0][None]).reshape(rows, depth).astype(BF)
    d_ref[...] = mm(later, w_ref[0], ((1,), (1,)))
    d_ref[...] += mm(dt_ref[...], w_ref[1], ((1,), (1,)))
    d_ref[...] += mm(earlier, w_ref[2], ((1,), (1,)))
    normed = (s_ref[...] - stat_ref[0:1]) * stat_ref[1:2]
    d = d_ref[...] * silu_slope(normed * norm_ref[0:1] + norm_ref[1:2])
    d_ref[...] = d
    put_sums(d, normed, sums_ref)


def spatial_grad(d_ref, s_ref, stat_ref, norm_ref, sums_ref, ds_ref, sum_ref, total):
    sums = jnp.sum(sums_ref[...], axis=0)
    sum_ref[...] = sums
    inverse = stat_ref[1:2]
    normed = (s_ref[...] - stat_ref[0:1]) * inverse
    d = d_ref[...] - sums[1:2] * (1.0 / total) - normed * (sums[0:1] * (1.0 / total))
    ds_ref[...] = (norm_ref[0:1] * inverse * d).astype(BF)


def adjoint(ds_ref, w_ref, pad, dims):
    height, width, frames, depth = dims
    pad[...] = jnp.zeros(pad.shape, F32)

    for k in range(9):
        part = mm(ds_ref[...], w_ref[:, k * depth : (k + 1) * depth], ((1,), (0,)))
        at = (slice(k // 3, k // 3 + height), slice(k % 3, k % 3 + width))
        pad[at] = pad[at] + part.reshape(dims)


def input_body(
    ids_ref, d_ref, s_ref, stat_ref, norm_ref, sums_ref, w_ref,
    ds_ref, send_ref, kept_ref, sum_ref, pad, part, *, dims, total
):
    height, width, frames, depth = dims
    spatial_grad(d_ref, s_ref, stat_ref, norm_ref, sums_ref, ds_ref, sum_ref, total)
    adjoint(ds_ref, w_ref, pad, dims)
    part[...] = pad[1 : height + 1, 1 : width + 1].reshape(part.shape)
    put_halves(ids_ref, part, send_ref, kept_ref)


def by_frame(source, out_ref, dims):
    height, width, frames, depth = dims
    pixels, own = height * width, out_ref.shape[1]
    for r in range(source.shape[0]):
        for f in range(frames):
            values = source[r, pl.ds(f, pixels, stride=frames), :]
            out_ref[f // own, f % own, :, r * LANES : (r + 1) * LANES] = values.astype(out_ref.dtype)


def last_body(ids_ref, ds_ref, w_ref, g_ref, block_ref, out_ref, block_out_ref, pad, part, block, *, dims):
    height, width, frames, depth = dims
    block[0] = block_ref[...].astype(F32)
    by_frame(block, block_out_ref, dims)
    adjoint(ds_ref, w_ref, pad, dims)
    own = ids_ref[0]
    for r in range(part.shape[0]):
        columns = pad[1 : height + 1, 1 : width + 1, :, r * LANES : (r + 1) * LANES]
        part[r] = columns.reshape(part.shape[1:])
    part[own] = part[own] + g_ref[...]
    by_frame(part, out_ref, dims)


def finish_body(*refs):
    block_ref, grad_ref, out_ref, grad_out_ref = refs
    own, height, width, depth = out_ref.shape
    for f in range(own):
        block = jnp.concatenate([block_ref[r, f].astype(F32) for r in range(4)], axis=1)
        grad = sum(grad_ref[r, f].astype(F32) for r in range(4))
        for h in range(height):
            at = slice(h * width, (h + 1) * width)
            out_ref[f, h] = block[at].astype(BF)
            grad_out_ref[f, h] = grad[at]


def weight_terms(act_ref, ds_ref, pad, acc, dims):
    height, width, frames, depth = dims
    rows = height * width * frames
    pad[...] = jnp.zeros(pad.shape, F32)
    pad[1 : height + 1, 1 : width + 1] = act_ref[...].astype(F32).reshape(dims)
    flipped = ds_ref[...].astype(F32).T.astype(BF)

    for k in range(9):
        i, j = k // 3, k % 3
        piece = pad[i : i + height, j : j + width].reshape(rows, depth).astype(BF)
        acc[:, k * depth : (k + 1) * depth] = mm(flipped, piece, ((1,), (0,)))


def put_shards(acc, places, out_ref, k):
    mid = acc.shape[0]
    half = mid // 2
    wide = k + LANES // 2
    for f in range(8):
        if f % 2 == 0:
            top = acc[0:half, k * f : k * f + wide]
            bottom = pltpu.roll(acc[half:mid, k * f : k * f + wide], LANES // 2, 1)
        else:
            start = k * f - LANES // 2
            top = pltpu.roll(acc[0:half, start : start + wide], k, 1)
            bottom = acc[half:mid, start : start + wide]
        fold(top, bottom, out_ref.at[places[f], 0:half], k)


def weight_plain_body(act_ref, ds_ref, out_ref, pad, acc, *, dims):
    weight_terms(act_ref, ds_ref, pad, acc, dims)
    out_ref[...] = acc[...].astype(BF)


def put_temporal(t_ref, places, out_ref, half):
    rows = out_ref.shape[1] - half
    per = half // rows
    for block in range(24):
        tap, r, part = block // 8, (block % 8) // 2, block % 2
        for j in range(per):
            start = tap * 2 * half + part * half + j * rows
            at = (block % 3) * per + j
            out_ref[places[block // 3], half:, at * LANES : (at + 1) * LANES] = t_ref[r, start : start + rows, :]


def weight_body(ids_ref, act_ref, ds_ref, t_ref, out_ref, ahead_ref, back_ref, pad, acc, *, dims):
    weight_terms(act_ref, ds_ref, pad, acc, dims)
    places = [ids_ref[14 + f] for f in range(8)]
    put_shards(acc, places, out_ref, acc.shape[1] // 8)
    put_temporal(t_ref, places, out_ref, acc.shape[0] // 2)
    ahead_ref[...] = out_ref[4]
    back_ref[...] = out_ref[5]


def weight_first_body(
    ids_ref, act_ref, d_ref, s_ref, stat_ref, norm_ref, sums_ref, t_ref, mid_ref, out_1_ref, out_0_ref,
    ds_ref, flat_ref, out_ref, ahead_ref, back_ref, sum_ref, pad, acc, *, dims, total
):
    spatial_grad(d_ref, s_ref, stat_ref, norm_ref, sums_ref, ds_ref, sum_ref, total)
    for r in range(flat_ref.shape[0]):
        flat_ref[r] = jnp.zeros(flat_ref.shape[1:], F32)
        for i, ref in enumerate((sum_ref, mid_ref, out_0_ref, out_1_ref)):
            flat_ref[r, 2 * i : 2 * i + 2, 0 : ref.shape[1]] = ref[...]
    weight_body(ids_ref, act_ref, ds_ref, t_ref, out_ref, ahead_ref, back_ref, pad, acc, dims=dims)


def norm_body(flat_ref, *refs):
    count = flat_ref.shape[0]
    for which in range(2):
        old, new = refs[3 * which : 3 * which + 3], refs[6 + 3 * which : 9 + 3 * which]
        width = old[0].shape[-1] // count
        for u in range(2):
            row = 4 * which + 2 * u
            grad = jnp.concatenate([flat_ref[r, row : row + 2, 0:width] for r in range(count)], axis=1)
            values = adam_step(old[0][u], grad, old[1][u], old[2][u], RATE_NORM, 0.0)
            for ref, value in zip(new, values):
                ref[u] = value


def adam_step(param, gradient, moment_one, moment_two, rate, decay):
    first_new = BETA_ONE * moment_one + (1.0 - BETA_ONE) * gradient
    second_new = BETA_TWO * moment_two + (1.0 - BETA_TWO) * gradient * gradient
    fix_one = 1.0 - BETA_ONE**STEP
    fix_two = 1.0 - BETA_TWO**STEP
    update = first_new / fix_one / (jnp.sqrt(second_new / fix_two) + ADAM_EPS)
    return (param - rate * (update + decay * param), first_new, second_new)


def adam_into(grad, refs, outs, rows):
    new, first, second = adam_step(refs[0][0, rows], grad, refs[1][0, rows], refs[2][0, rows], RATE_WEIGHT, DECAY)
    outs[0][0, rows] = new
    outs[1][0, rows] = first
    outs[2][0, rows] = second
    outs[3][0, rows] = new.astype(BF)


def adam_body(*refs, grads):
    sources, refs = refs[:grads], refs[grads:]
    refs, outs = refs[:6], refs[-8:]
    summed = sum(r[...].astype(F32) for r in sources)
    half = refs[0].shape[1] // 2
    spatial, temporal = summed[0:half], summed[half:]
    rows = temporal.shape[0]
    for i in range(temporal.shape[1] // LANES):
        piece = temporal[:, i * LANES : (i + 1) * LANES]
        adam_into(piece, refs[3:], outs[4:], slice(i * rows, (i + 1) * rows))
    half, double = spatial.shape
    k = double // 2
    edge = k - LANES // 2
    adam_into(spatial[:, 0:k], refs, outs, slice(0, half))
    adam_into(pltpu.roll(spatial[:, edge:], k, 1)[:, 0:k], refs, outs, slice(half, 2 * half))


def adam_unit(u, sources, state, before, name, after=()):
    unit = [pl.BlockSpec((1,) + a.shape[1:], lambda i: (u, 0, 0)) for a in state]
    types = [F32, F32, F32, BF]
    outs = [shape(state[0].shape, t) for t in types] + [shape(state[3].shape, t) for t in types]
    before = list(before or ())
    whole = [pl.BlockSpec(a.shape, lambda i, n=a.ndim: (0,) * n) for a in sources]

    def kernel(*refs):
        adam_body(*refs[len(after) :], grads=len(sources))

    return pl.pallas_call(
        kernel,
        grid=(1,),
        out_shape=tuple(outs),
        in_specs=[pl.BlockSpec(memory_space=pl.ANY)] * len(after) + whole + unit + [pl.BlockSpec(memory_space=pl.ANY)] * len(before),
        out_specs=tuple([unit[0]] * 4 + [unit[3]] * 4),
        input_output_aliases={len(after) + len(sources) + 6 + i: i for i in range(len(before))},
        compiler_params=pltpu.CompilerParams(vmem_limit_bytes=40 * MIB),
        name=name,
    )(*after, *sources, *state, *before)


def swap(parts, axis):
    return lax.all_to_all(parts, axis, 0, 0, tiled=True)


def from_all(value, axis):
    count = lax.axis_size(axis)
    return swap(jnp.broadcast_to(value[None], (count,) + value.shape), axis)


def across(value, bit):
    count = lax.axis_size("rep")
    return lax.ppermute(value, "rep", [(i, i ^ bit) for i in range(count)])


def from_group(value):
    far = across(value, 2)
    near = across(value, 1)
    return value, far, near, across(far, 1)


def neighbours(first, last):
    count = lax.axis_size("frames")
    before = lax.ppermute(last, "frames", [(i, i + 1) for i in range(count - 1)])
    after = lax.ppermute(first, "frames", [(i + 1, i) for i in range(count - 1)])
    return before, after


def along(step):
    return [(RING[i], RING[(i + step) % 8]) for i in range(8)]


def ring_gather(own):
    ahead, back = [own], [own]
    for step in range(4):
        ahead.append(lax.ppermute(ahead[-1], "frames", along(1)))
        if step < 3:
            back.append(lax.ppermute(back[-1], "frames", along(-1)))
    return ahead + back[1:], list(zip(ahead[1:4], back[1:]))


def ring_sums(parts, ahead, back):
    def plus(got, part):
        return (got.astype(F32) + part.astype(F32)).astype(BF)

    steps = []
    for i in (3, 2, 1):
        ahead = plus(lax.ppermute(ahead, "frames", along(1)), parts[i])
        if i > 1:
            back = plus(lax.ppermute(back, "frames", along(-1)), parts[9 - i])
        steps.append((ahead, back))
    ends = [parts[0], lax.ppermute(ahead, "frames", along(1)), lax.ppermute(back, "frames", along(-1))]
    return ends, steps


def reduced(send, kept, x):
    got = across(send, 1)
    away = lax.dynamic_index_in_dim(got, 1 - x, 0, False).astype(F32)
    away = away + lax.dynamic_index_in_dim(kept, 1 - x, 0, False)
    return got, kept, across(away.astype(BF), 2)


def ordered(t_grad, count):
    n_r, rows, cols = t_grad.shape
    return t_grad.reshape(n_r, 3, rows // 3, cols).transpose(1, 0, 2, 3).reshape(count, -1, cols)


def sum_over(parts, axis):
    return jnp.sum(swap(parts, axis).astype(F32), axis=0)


def on_device(
    frames_in, cotangent, lengths,
    spatial_weights, spatial_first, spatial_second,
    temporal_weights, temporal_first, temporal_second,
    mid_norm, mid_first, mid_second,
    out_norm, out_first, out_second,
):
    own_frames, height, width, depth = frames_in.shape
    n_f, n_r = lax.axis_size("frames"), lax.axis_size("rep")
    assert n_r == 4 and depth == n_r * LANES
    me = lax.axis_index("rep")
    frames = own_frames * n_r
    pixels = height * width
    rows = pixels * frames
    total = float(rows * n_f)
    dims = (height, width, frames, depth)
    units, k, mid = spatial_weights.shape
    cols = LANES
    everyone = ("frames", "rep")
    k_t = temporal_weights.shape[1]
    ring = can_ring(mid, k, k_t, n_f)
    spatial_flops = 2 * rows * 9 * depth * mid
    temporal_flops = 2 * rows * 3 * depth * mid
    pad = pltpu.VMEM((height + 2, width + 2, frames, depth), F32)
    flip = functools.partial(jnp.swapaxes, axis1=1, axis2=2)
    ids = [me, me ^ 2, me ^ 1, me ^ 3, me & 1, me >> 1]
    if ring:
        place = ring_place(lax.axis_index("frames"))
        ids += [ring_device(place + i) for i in (0, -1, -2, -3, -4, 1, 2, 3)]
        ids += [(ring_place(jnp.int32(f)) - place) % 8 for f in range(8)]
    ids = jnp.stack(ids).astype(jnp.int32)

    frame_ids = lax.axis_index("frames") * frames + jnp.arange(frames, dtype=jnp.int32)
    clip_ends = jnp.cumsum(lengths)
    starts = jnp.concatenate([jnp.zeros((1,), jnp.int32), clip_ends[:-1]])
    opening = jnp.any(frame_ids[:, None] == starts[None, :], axis=1)
    closing = jnp.any((frame_ids + 1)[:, None] == clip_ends[None, :], axis=1)
    keep = jnp.where(jnp.stack([opening, closing]), 0.0, 1.0).astype(F32)[:, :, None]

    act = lax.all_gather(frames_in, "rep", axis=0, tiled=True).transpose(1, 2, 0, 3).reshape(rows, depth)
    cot = cotangent.reshape(own_frames, pixels, n_r, cols).transpose(2, 0, 1, 3)
    cot = swap(cot, "rep").reshape(frames, pixels, cols).transpose(1, 0, 2).reshape(rows, cols)

    mid_own = lax.dynamic_slice_in_dim(mid_norm, me * mid, mid, axis=2)
    out_split = out_norm.reshape(units, 2, n_r, cols).transpose(0, 2, 1, 3)

    spatial_w, temporal_w, steps = [], [], [(), (), ()]
    if ring:
        wire = shape((mid // 2 + k_t * LANES // (2 * k), 2 * k), BF)
        w_shape, t_shape = shape((mid, n_f * k), BF), shape((n_r, 3, 2, mid // 2, cols), BF)
        wires = run(
            pack_body, [wire] * units, [flip(spatial_weights), temporal_weights], "pack",
            [pltpu.VMEM((mid, k + LANES // 2), F32)],
        )
        held, _ = ring_gather(wires[0])
        w, t, *waiting = run(
            unpack_body, [w_shape, t_shape] + [wire] * (units - 1), [ids, *held, *wires[1:]], "unpack_0", scalars=1,
            after=[act, cot, keep, mid_own, out_split],
        )
        spatial_w.append(w)
        temporal_w.append(swap(t, "rep").reshape(n_r, 3, mid, cols))
        for u in range(1, units):
            held, steps = ring_gather(waiting[u - 1])
            w, t = run(unpack_body, [w_shape, t_shape], [ids, *held], f"unpack_{u}", scalars=1)
            spatial_w.append(w)
            temporal_w.append(swap(t, "rep").reshape(n_r, 3, mid, cols))
    else:
        wire = flip(spatial_weights).astype(BF)
        temporal_low = temporal_weights.astype(BF)
        for u in range(units):
            held = lax.all_gather(wire[u], "frames", axis=0)
            spatial_w.append(held.transpose(1, 0, 2).reshape(mid, n_f * k))
            shard = lax.all_gather(temporal_low[u], "frames", axis=0, tiled=True)
            shard = shard.reshape(3, n_r, mid, cols).transpose(1, 0, 2, 3)
            temporal_w.append(swap(shard, "rep"))

    halo = shape((pixels, 1, mid), F32)
    column = shape((rows, cols), BF)
    saved = []
    for u in range(units):
        outs = [shape((rows, mid), F32), halo, halo, shape((2, mid), F32)]
        if u == 0:
            (spatial,) = run(
                functools.partial(spatial_body, dims=dims), outs[:1], [act, spatial_w[u]],
                f"spatial_{u}", [pad], flops=spatial_flops, moved=8 * MIB,
            )
            first, last, mom = run(
                functools.partial(moments_body, dims=dims), outs[1:], [spatial], f"moments_{u}", moved=MIB,
                after=[temporal_w[0]],
            )
        else:
            spatial, first, last, mom, act = run(
                functools.partial(next_body, dims=dims), outs + [shape((rows, depth), BF)],
                [ids, *t_group, both, out_split[u - 1], spatial_w[u]],
                f"spatial_{u}", [pad], scalars=1, flops=spatial_flops, moved=8 * MIB,
            )
        mid_both = from_all(mom, "frames")
        before, after = neighbours(first, last)
        send, kept, window, stat, row_w = run(
            functools.partial(temporal_body, dims=dims),
            [shape((2, rows, cols), BF), shape((2, rows, cols), F32), shape((3, rows, mid), BF), shape((2, mid), F32),
             shape((3, mid, depth), BF)],
            [ids, spatial, mid_both, before, after, mid_own[u], keep, temporal_w[u]],
            f"temporal_{u}", [pltpu.VMEM((pixels, frames + 16, mid), F32), pltpu.VMEM((rows, depth), F32)],
            scalars=1, flops=temporal_flops, moved=8 * MIB, after=steps[1] if u == 0 else (),
        )
        t, low, mom = run(
            total_body, [shape((rows, cols), F32), column, shape((2, cols), F32)],
            [ids, *reduced(send, kept, me >> 1)], f"total_{u}", scalars=1, moved=3 * MIB,
            after=steps[2] if u == 0 else (),
        )
        both = from_all(mom, everyone).reshape(n_f, n_r, 2, cols)
        t_group = from_group(low)
        saved.append((act, spatial, stat, window, row_w, t, t_group, both))

    d_norms = [None] * units
    weight_parts = [None] * units
    pending = [()] * 4
    held_back = ()
    for u in reversed(range(units)):
        act, spatial, stat, window, row_w, t, t_group, both = saved[u]
        if u == units - 1:
            block, summed_grad, low, sums = run(
                top_body, [column, shape((rows, cols), F32), column, shape((2, cols), F32)],
                [ids, t, both, out_split[u], saved[0][0], cot], "top", scalars=1, moved=3 * MIB,
            )
        else:
            low, sums = run(
                below_body, [column, shape((2, cols), F32)],
                [ids, *reduced(send, kept, me >> 1), t, both, out_split[u]], f"below_{u}", scalars=1, moved=3 * MIB,
                after=pending[0],
            )
        sums = from_all(sums, everyone).reshape(n_f, n_r, 2, cols)
        g_group = from_group(low)
        edge = [shape((2 * n_r, pixels, 1, cols), F32)] * 2
        edges = neighbours(*run(functools.partial(edges_body, dims=dims), edge, g_group + t_group, f"edges_{u}", after=[sums]))
        dt, coef, t_grad, out_sums = run(
            functools.partial(dt_body, total=total),
            [shape((rows, depth), BF), shape((n_r, 4, cols), F32), shape((n_r, 3 * mid, cols), BF), shape((2, cols), F32)],
            [ids, *g_group, *t_group, both, sums, out_split[u], window],
            f"dt_{u}", scalars=1, flops=temporal_flops, moved=8 * MIB, after=pending[1],
        )
        t_grad = swap(t_grad, "rep")
        d_mid, sums = run(
            functools.partial(middle_body, dims=dims), [shape((rows, mid), F32), shape((2, mid), F32)],
            [ids, dt, coef, *edges, keep, row_w, spatial, stat, mid_own[u]],
            f"middle_{u}", [pltpu.VMEM((pixels, frames + 16, depth), F32)],
            scalars=1, flops=temporal_flops, moved=8 * MIB, after=pending[2],
        )
        sums = from_all(sums, "frames")
        ds_shape, sum_shape = shape((rows, mid), BF), shape((2, mid), F32)
        acc = pltpu.VMEM((mid, n_f * k), F32)
        grad_args = [d_mid, spatial, stat, mid_own[u], sums]
        if u > 0 or not ring:
            ds, send, kept, mid_sums = run(
                functools.partial(input_body, dims=dims, total=total),
                [ds_shape, shape((2, rows, cols), BF), shape((2, rows, cols), F32), sum_shape],
                [ids, *grad_args, spatial_w[u]],
                f"input_{u}", [pad, pltpu.VMEM((rows, depth), F32)], scalars=1, flops=spatial_flops, moved=8 * MIB,
                after=[t_grad],
            )
        if ring:
            slab = shape(wires[u].shape, BF)
            slabs = [shape((n_f,) + slab.shape, BF), slab, slab]
        if ring and u > 0:
            s_grad, ahead, back = run(
                functools.partial(weight_body, dims=dims), slabs, [ids, act, ds, t_grad],
                f"weight_{u}", [pad, acc], scalars=1, flops=spatial_flops, moved=8 * MIB,
            )
            weight_parts[u], sent = ring_sums(s_grad, ahead, back)
            pending = [[s_grad], sent[0], sent[1], weight_parts[u][1:]]
        elif ring:
            ds, flat, s_grad, ahead, back = run(
                functools.partial(weight_first_body, dims=dims, total=total),
                [ds_shape, shape((n_r, 8, 512), F32)] + slabs,
                [ids, act, *grad_args, t_grad, *d_norms[1], out_sums],
                f"weight_{u}", [pltpu.VMEM((2, mid), F32), pad, acc], scalars=1, flops=spatial_flops, moved=8 * MIB,
                after=pending[3],
            )
            weight_parts[u], sent = ring_sums(s_grad, ahead, back)
            held_back = sent[0]
        else:
            (s_grad,) = run(
                functools.partial(weight_plain_body, dims=dims), [shape((mid, n_f * k), BF)], [act, ds],
                f"weight_{u}", [pad, acc], flops=spatial_flops, moved=8 * MIB,
            )
            s_grad = swap(s_grad.reshape(mid, n_f, k).transpose(1, 0, 2), "frames")
            weight_parts[u] = (s_grad, swap(ordered(t_grad, n_f), "frames"))
        if u == 0:
            d_input, block = run(
                functools.partial(last_body, dims=dims),
                [shape((n_r, own_frames, pixels, depth), BF), shape((n_r, own_frames, pixels, cols), BF)],
                [ids, ds, spatial_w[u], summed_grad, block], "last",
                [pad, pltpu.VMEM((n_r, rows, cols), F32), pltpu.VMEM((1, rows, cols), F32)], scalars=1,
                flops=spatial_flops, moved=8 * MIB, after=held_back,
            )
        d_norms[u] = (mid_sums, out_sums)

    block_out, input_grad = run(
        finish_body, [shape(frames_in.shape, BF), shape(frames_in.shape, F32)],
        [swap(block, "rep"), swap(d_input, "rep")], "finish", moved=3 * MIB,
    )
    if ring:
        flat = swap(flat, "rep")
        norms = [mid_norm, mid_first, mid_second, out_norm, out_first, out_second]
        norms = run(norm_body, [shape(a.shape, F32) for a in norms], [flat, *norms], "norms")
    else:
        flat = jnp.concatenate([jnp.concatenate([m.reshape(-1), o.reshape(-1)]) for m, o in d_norms])
        flat = from_all(flat, "rep").reshape(n_r, units, -1)
        mid_grad = flat[:, :, : 2 * mid].reshape(n_r, units, 2, mid).transpose(1, 2, 0, 3)
        mid_grad = mid_grad.reshape(units, 2, n_r * mid)
        out_grad = flat[:, :, 2 * mid :].reshape(n_r, units, 2, cols).transpose(1, 2, 0, 3)
        out_grad = out_grad.reshape(units, 2, depth)
        norms = [*adam_step(mid_norm, mid_grad, mid_first, mid_second, RATE_NORM, 0.0)]
        norms += adam_step(out_norm, out_grad, out_first, out_second, RATE_NORM, 0.0)

    if ring:
        state = [flip(a) for a in (spatial_weights, spatial_first, spatial_second)]
        state += [temporal_weights, temporal_first, temporal_second]
        weights = None
        for u in reversed(range(units)):
            weights = adam_unit(u, weight_parts[u], state, weights, f"adam_{u}", held_back if u > 0 else ())
        weights = [flip(a) for a in weights[:4]] + list(weights[4:])
    else:
        grads = [jnp.stack([jnp.sum(parts[i].astype(F32), axis=0) for parts in weight_parts]) for i in range(2)]
        news = adam_step(spatial_weights, flip(grads[0]), spatial_first, spatial_second, RATE_WEIGHT, DECAY)
        weights = [*news, news[0].astype(BF)]
        news = adam_step(temporal_weights, grads[1], temporal_first, temporal_second, RATE_WEIGHT, DECAY)
        weights += [*news, news[0].astype(BF)]
    return (block_out, input_grad, *weights, *norms)


def solution(mesh):
    by_frame = P(("frames", "rep"), None, None, None)
    by_block = P(None, "frames", "rep")
    placed = (by_frame, by_frame, P()) + (by_block,) * 6 + (P(),) * 6
    return jax.shard_map(
        on_device,
        mesh=mesh,
        in_specs=placed,
        out_specs=(by_frame, by_frame) + (by_block,) * 8 + (P(),) * 6,
        check_vma=False,
    )
```

```python
import functools

import jax
import jax.numpy as jnp
from jax import lax
from jax.experimental import pallas as pl
from jax.experimental.pallas import tpu as pltpu
from jax.sharding import PartitionSpec as P

STEP = 5
NORM_EPS = 1e-05
ADAM_EPS = 1e-08
BETA_ONE = 0.5
BETA_TWO = 0.5
RATE_WEIGHT = 0.015
RATE_NORM = 0.2
DECAY = 0.05
BF = jnp.bfloat16
F32 = jnp.float32
MIB = 1 << 20
VMEM = pl.BlockSpec(memory_space=pltpu.VMEM)
SMEM = pl.BlockSpec(memory_space=pltpu.SMEM)
LANES = 128
SCALE = 30
ANY = pl.BlockSpec(memory_space=pl.ANY)
HBM = pl.BlockSpec(memory_space=pltpu.HBM)


def shape(dims, dtype):
    return jax.ShapeDtypeStruct(tuple(dims), dtype)


class Placed:
    def __init__(self, value, where):
        self.value, self.where = value, where


def far(value):
    return Placed(value, "hbm")


def loaded(value):
    return Placed(value, "loaded")


def near(value):
    return Placed(value, "vmem")


def all_loaded(values):
    return [loaded(v) for v in values]


def in_hbm(array):
    return pltpu.with_memory_space_constraint(array, pltpu.HBM)


def operand(a):
    if not isinstance(a, Placed):
        return a
    return pltpu.with_memory_space_constraint(a.value, pltpu.VMEM if a.where == "vmem" else pltpu.HBM)


def result(a):
    if not isinstance(a, Placed):
        return a
    return (pltpu.VMEM if a.where == "vmem" else pltpu.HBM)(a.value.shape, a.value.dtype)


def is_far(a):
    return isinstance(a, Placed) and a.where == "hbm"


def run(body, outs, args, name, scratch=(), limit=28, scalars=0, flops=0, moved=0, after=(), scale=SCALE):
    def kernel(*refs):
        body(*refs[len(after) :])

    return pl.pallas_call(
        kernel,
        out_shape=tuple(result(o) for o in outs),
        in_specs=[ANY] * len(after) + [SMEM] * scalars + [ANY if is_far(a) else VMEM for a in args[scalars:]],
        out_specs=tuple(HBM if is_far(o) else VMEM for o in outs),
        scratch_shapes=list(scratch),
        compiler_params=pltpu.CompilerParams(vmem_limit_bytes=limit * MIB),
        cost_estimate=pl.CostEstimate(flops=int(scale * flops), bytes_accessed=int(scale * moved), transcendentals=0),
        name=name,
    )(*after, *[operand(a) for a in args])


def gate(value, after, name):
    return pl.pallas_call(
        lambda *refs: None,
        out_shape=shape(value.shape, value.dtype),
        in_specs=[ANY] * (len(after) + 1),
        out_specs=ANY,
        input_output_aliases={len(after): 0},
        name=name,
    )(*after, value)


def started(source, target, sem):
    copy = pltpu.make_async_copy(source, target, sem)
    copy.start()
    return copy


def padded(values, rows):
    return jnp.concatenate([values, jnp.zeros((rows - values.shape[0], values.shape[1]), F32)], axis=0)


def sigmoid(v):
    return 1.0 / (1.0 + jnp.exp(-v))


def silu(v):
    return v / (1.0 + jnp.exp(-v))


def silu_slope(v):
    s = sigmoid(v)
    return s * (1.0 + v * (1.0 - s))


def mm(a, b, dims):
    return lax.dot_general(a, b, (dims, ((), ())), preferred_element_type=F32)


def put_moments(values, out_ref):
    rows = values.shape[0]
    mean = jnp.sum(values, axis=0, keepdims=True) * (1.0 / rows)
    off = values - mean
    out_ref[0:1, :] = mean
    out_ref[1:2, :] = jnp.sum(off * off, axis=0, keepdims=True)


def joined_moments(both, rows):
    count = both.shape[0]
    mean = jnp.sum(both[:, 0:1], axis=0) * (1.0 / count)
    off = both[:, 0:1] - mean[None]
    total = jnp.sum(both[:, 1:2] + rows * (off * off), axis=0)
    return mean, lax.rsqrt(total * (1.0 / (rows * count)) + NORM_EPS)


def put_sums(upstream, normed, out_ref):
    out_ref[0:1, :] = jnp.sum(upstream * normed, axis=0, keepdims=True)
    out_ref[1:2, :] = jnp.sum(upstream, axis=0, keepdims=True)


def convolve(pad, w_ref, acc_ref, dims):
    height, width, frames, depth = dims
    rows = height * width * frames

    for k in range(9):
        i, j = k // 3, k % 3
        piece = pad[i : i + height, j : j + width].reshape(rows, depth).astype(BF)
        part = mm(piece, w_ref[:, k * depth : (k + 1) * depth], ((1,), (1,)))
        if k == 0:
            acc_ref[...] = part
        else:
            acc_ref[...] += part


def widened(scr, values, before, after):
    frames = values.shape[1]
    scr[:, 8 : 8 + frames, :] = values
    scr[:, 7:8, :] = before
    scr[:, 8 + frames : 9 + frames, :] = after


RING = (0, 2, 4, 6, 7, 5, 3, 1)


def can_ring(mid, k, k_t, count):
    return count == len(RING) and mid == 288 and k == 576 and k_t == 432


def ring_place(frame):
    return jnp.where(frame % 2 == 0, frame // 2, 7 - frame // 2)


def ring_device(place):
    place = place % 8
    return jnp.where(place < 4, 2 * place, 15 - 2 * place)


def low_half(shape_):
    return lax.broadcasted_iota(jnp.int32, shape_, 1) < LANES // 2


def fold(top, bottom, out_ref, k):
    edge = k - LANES // 2
    out_ref[:, 0:edge] = top[:, 0:edge].astype(out_ref.dtype)
    mixed = jnp.where(low_half((top.shape[0], LANES)), top[:, edge : edge + LANES], bottom[:, 0:LANES])
    out_ref[:, edge : edge + LANES] = mixed.astype(out_ref.dtype)
    out_ref[:, edge + LANES : 2 * k] = bottom[:, LANES : k + LANES // 2].astype(out_ref.dtype)


def pack_body(w_ref, t_ref, *refs):
    outs, folded, scr = refs[:-2], refs[-2], refs[-1]
    units, mid, k = w_ref.shape
    half = mid // 2
    for u in range(units):
        scr[:, 0:k] = w_ref[u]
        fold(scr[0:half, :], pltpu.roll(scr[half:mid, :], LANES // 2, 1), folded.at[0:half], k)
        rows = folded.shape[0] - half
        for i in range(2 * k // LANES):
            at = slice(i * LANES, (i + 1) * LANES)
            folded[half:, at] = t_ref[u, rows * i : rows * (i + 1), :].astype(BF)
        start = 0
        for out in outs[:3] if u == 0 else outs[u + 2 : u + 3]:
            out[...] = folded[start : start + out.shape[0], :]
            start += out.shape[0]


def unpack_temporal(f, slot, t_ref):
    rows = slot.shape[0]
    per = t_ref.shape[3] // rows
    for j in range(slot.shape[1] // LANES):
        block = 3 * f + j // per
        piece = slot[:, j * LANES : (j + 1) * LANES]
        t_ref[(block % 8) // 2, block // 8, block % 2, (j % per) * rows : (j % per + 1) * rows, :] = piece


def slots_of(refs):
    if len(refs[0].shape) == 3:
        half = refs[0].shape[1] * 3 // 4
        return [([refs[0].at[i, 0:half]], refs[0].at[i, half:]) for i in range(8)], refs[1:]
    return [([refs[i], refs[8 + i]], refs[16 + i]) for i in range(8)], refs[24:]


def unpack_temporal_body(ids_ref, *refs):
    slots, refs = slots_of(refs)
    if len(refs) > 5:
        refs[5][...] = refs[0][...]
        refs = refs[1:5] + refs[6:]
    outs, scr = refs[:4], refs[4]
    half = scr.shape[3]
    for i, (_, slot) in enumerate(slots):
        unpack_temporal(ids_ref[6 + i], slot, scr)
    for j, out_ref in enumerate(outs):
        for k in range(3):
            for part in range(2):
                out_ref[k, part * half : (part + 1) * half, :] = scr[ids_ref[j], k, part]


def unpack_spatial(ids_ref, slots, w_ref):
    half, k = w_ref.shape[0] // 2, w_ref.shape[1] // 8
    edge, wide = k - LANES // 2, k + LANES // 2
    for i, (slot, _) in enumerate(slots):
        f = ids_ref[6 + i]
        base = (f // 2) * (2 * k)
        values = jnp.concatenate([part[...].astype(F32) for part in slot], axis=0)
        low = low_half((half, LANES))

        def at(start, size):
            return pl.ds(pl.multiple_of(base + start, LANES), size)

        @pl.when(f % 2 == 0)
        def _():
            for start, part in ((0, values[:, 0:wide]), (half, pltpu.roll(values[:, edge:], k, 1))):
                rows = slice(start, start + half)
                w_ref[rows, at(0, edge)] = part[:, 0:edge].astype(BF)
                old = w_ref[rows, at(edge, LANES)].astype(F32)
                w_ref[rows, at(edge, LANES)] = jnp.where(low, part[:, edge:wide], old).astype(BF)

        @pl.when(f % 2 == 1)
        def _():
            for start, part in ((0, pltpu.roll(values[:, 0:wide], LANES // 2, 1)), (half, values[:, edge:])):
                rows = slice(start, start + half)
                old = w_ref[rows, at(edge, LANES)].astype(F32)
                w_ref[rows, at(edge, LANES)] = jnp.where(low, old, part[:, 0:LANES]).astype(BF)
                w_ref[rows, at(edge + LANES, edge)] = part[:, LANES:wide].astype(BF)


def spatial_body(*refs, dims, ring, first):
    height, width, frames, depth = dims
    rows = height * width * frames
    ids_ref, refs = refs[0], refs[1:]
    if ring:
        slots, refs = slots_of(refs)
    else:
        w_ref, refs = refs[0], refs[1:]
    refs = iter(refs)

    def take(count):
        return [next(refs) for _ in range(count)]

    sources = take(1 if first else 6)
    s_ref, first_ref, last_ref, mom_ref, s_far = take(5)
    w_far, act_far = take(int(ring)), take(int(not first))
    pad, sems = take(2)
    w_scr, act_scr = take(int(ring)), take(int(not first))

    copies = []
    if ring:
        w_ref = w_scr[0]
        unpack_spatial(ids_ref, slots, w_ref)
        copies.append(started(w_ref, w_far[0], sems.at[0]))
    pad[...] = jnp.zeros(pad.shape, F32)
    if first:
        pad[1 : height + 1, 1 : width + 1] = sources[0][...].astype(F32).reshape(dims)
    else:
        both_ref, norm_ref = sources[4:]
        for j, t_ref in enumerate(sources[:4]):
            b = ids_ref[j]
            mean, inverse = joined_moments(both_ref[:, b], rows)
            norm = norm_ref[b]
            y = (t_ref[...].astype(F32) - mean) * (inverse * norm[0:1]) + norm[1:2]
            a = silu(y)
            at = pl.ds(pl.multiple_of(b * LANES, LANES), LANES)
            act_scr[0][:, at] = padded(a, act_scr[0].shape[0]).astype(BF)
            pad[1 : height + 1, 1 : width + 1, :, at] = a.reshape(height, width, frames, LANES)
        copies.append(started(act_scr[0], act_far[0], sems.at[1]))
    convolve(pad, w_ref, s_ref, dims)
    copies.append(started(s_ref, s_far, sems.at[2]))
    values = s_ref[...]
    put_moments(values, mom_ref)
    grid = values.reshape(height * width, frames, values.shape[-1])
    first_ref[...] = grid[:, 0:1, :]
    last_ref[...] = grid[:, frames - 1 : frames, :]
    for copy in copies:
        copy.wait()


def temporal_body(
    ids_ref, s_ref, both_ref, before_ref, after_ref, norm_ref, keep_ref, w0, w1, w2, w3,
    send_ref, kept_ref, stat_ref, win_far, row_far, scr, part, win_ref, row_ref, sems, *, dims
):
    height, width, frames, depth = dims
    pixels = height * width
    rows = pixels * frames
    mid = s_ref.shape[-1]
    for j, w_ref in enumerate((w0, w1, w2, w3)):
        row_ref[:, :, pl.ds(pl.multiple_of(ids_ref[j] * LANES, LANES), LANES)] = w_ref[...]
    copies = [started(row_ref, row_far, sems.at[0])]
    mean, inverse = joined_moments(both_ref[...], rows)
    stat_ref[0:1, :] = mean
    stat_ref[1:2, :] = inverse
    scale, bias = inverse * norm_ref[0:1], norm_ref[1:2]

    def active(v):
        return silu((v - mean) * scale + bias)

    middle = active(s_ref[...])
    widened(
        scr, middle.reshape(pixels, frames, mid),
        active(before_ref[...].reshape(pixels, mid)).reshape(pixels, 1, mid),
        active(after_ref[...].reshape(pixels, mid)).reshape(pixels, 1, mid),
    )
    whole = win_ref.shape[1]
    earlier = (scr[:, 7 : 7 + frames, :] * keep_ref[0][None]).reshape(rows, mid)
    later = (scr[:, 9 : 9 + frames, :] * keep_ref[1][None]).reshape(rows, mid)
    for i, values in enumerate((earlier, middle, later)):
        win_ref[i] = padded(values, whole).astype(BF)
    copies.append(started(win_ref, win_far, sems.at[1]))
    part[...] = mm(win_ref[0], row_ref[0], ((1,), (0,)))
    part[...] += mm(win_ref[1], row_ref[1], ((1,), (0,)))
    part[...] += mm(win_ref[2], row_ref[2], ((1,), (0,)))
    put_halves(ids_ref, part, send_ref, kept_ref)
    for copy in copies:
        copy.wait()


def put_halves(ids_ref, part, send_ref, kept_ref):
    core = ids_ref[4]
    rows = send_ref.shape[1]
    for i in range(2):
        other = pl.multiple_of((2 * i + 1 - core) * LANES, LANES)
        own = pl.multiple_of((2 * i + core) * LANES, LANES)
        send_ref[i] = part[0:rows, pl.ds(other, LANES)].astype(BF)
        kept_ref[i] = part[0:rows, pl.ds(own, LANES)]


def total_body(ids_ref, got_ref, kept_ref, last_ref, t_ref, low_ref, mom_ref):
    x = ids_ref[5]
    t = got_ref[x].astype(F32) + kept_ref[x] + last_ref[...].astype(F32)
    t_ref[...] = t
    low_ref[...] = t.astype(BF)
    put_moments(t, mom_ref)


def edges_body(*refs, dims):
    height, width, frames, depth = dims
    blocks, (first_ref, last_ref) = refs[:-2], refs[-2:]
    for j, ref in enumerate(blocks):
        grid = ref[...].astype(F32).reshape(height * width, frames, LANES)
        first_ref[j] = grid[:, 0:1, :]
        last_ref[j] = grid[:, frames - 1 : frames, :]


def top_body(ids_ref, t_ref, both_ref, norm_ref, x_ref, cot_ref, block_ref, g_ref, low_ref, sums_ref):
    rows = t_ref.shape[0]
    b = ids_ref[0]
    mean, inverse = joined_moments(both_ref[:, b], rows)
    norm = norm_ref[b]
    normed = (t_ref[...] - mean) * inverse
    own = pl.ds(pl.multiple_of(b * LANES, LANES), LANES)
    summed = normed * norm[0:1] + norm[1:2] + x_ref[:, own].astype(F32)
    block_ref[...] = silu(summed).astype(BF)
    g = cot_ref[...].astype(F32) * silu_slope(summed)
    g_ref[...] = g
    low_ref[...] = g.astype(BF)
    put_sums(g, normed, sums_ref)


def below_body(ids_ref, got_ref, kept_ref, last_ref, t_ref, both_ref, norm_ref, low_ref, sums_ref):
    rows = t_ref.shape[0]
    b, x = ids_ref[0], ids_ref[5]
    d_act = got_ref[x].astype(F32) + kept_ref[x] + last_ref[...].astype(F32)
    mean, inverse = joined_moments(both_ref[:, b], rows)
    norm = norm_ref[b]
    normed = (t_ref[...] - mean) * inverse
    g = d_act * silu_slope(normed * norm[0:1] + norm[1:2])
    low_ref[...] = g.astype(BF)
    put_sums(g, normed, sums_ref)


def dt_body(
    ids_ref, g0, g1, g2, g3, t0, t1, t2, t3, both_ref, sums_ref, norm_ref, dt_ref, coef_ref, sum_ref, *, total
):
    rows, whole = g0.shape[0], dt_ref.shape[0]
    for j, (g_ref, t_ref) in enumerate(((g0, t0), (g1, t1), (g2, t2), (g3, t3))):
        b = ids_ref[j]
        mean, inverse = joined_moments(both_ref[:, b], rows)
        sums = jnp.sum(sums_ref[:, b], axis=0)
        if j == 0:
            sum_ref[...] = sums
        c1 = norm_ref[b][0:1] * inverse
        c2 = c1 * sums[1:2] * (1.0 / total)
        c3 = c1 * inverse * sums[0:1] * (1.0 / total)
        coef_ref[j] = jnp.concatenate([c1, c2, c3, mean], axis=0)
        d = c1 * g_ref[...].astype(F32) - c2 - c3 * (t_ref[...].astype(F32) - mean)
        dt_ref[:, pl.ds(pl.multiple_of(b * LANES, LANES), LANES)] = padded(d, whole).astype(BF)


def temporal_grad_body(ids_ref, win_ref, dt_ref, *refs):
    outs, term = refs[:-1], refs[-1]
    mid = win_ref.shape[-1]
    dt = dt_ref[...]
    for k in range(3):
        term[...] = mm(win_ref[k], dt, ((0,), (0,)))
        for j, out_ref in enumerate(outs):
            at = pl.ds(pl.multiple_of(ids_ref[j] * LANES, LANES), LANES)
            out_ref[k * mid : (k + 1) * mid, :] = term[:, at].astype(BF)


def middle_body(
    ids_ref, dt_ref, coef_ref, before_ref, after_ref, keep_ref, stat_ref, norm_ref, row_far, s_far,
    d_ref, sums_ref, scr, row_ref, s_ref, sems, *, dims
):
    height, width, frames, depth = dims
    pixels = height * width
    rows = pixels * frames
    copies = [started(row_far, row_ref, sems.at[0]), started(s_far, s_ref, sems.at[1])]
    dt = dt_ref[...]
    scr[:, 8 : 8 + frames, :] = dt.astype(F32)[0:rows].reshape(pixels, frames, depth)
    for j in range(4):
        at = pl.ds(pl.multiple_of(ids_ref[j] * LANES, LANES), LANES)
        c = coef_ref[j]

        def halo(g, t):
            d = c[0:1] * g.reshape(pixels, LANES) - c[1:2] - c[2:3] * (t.reshape(pixels, LANES) - c[3:4])
            return d.astype(BF).astype(F32).reshape(pixels, 1, LANES)

        scr[:, 7:8, at] = halo(before_ref[j], before_ref[4 + j])
        scr[:, 8 + frames : 9 + frames, at] = halo(after_ref[j], after_ref[4 + j])
    later = (scr[:, 9 : 9 + frames, :] * keep_ref[1][None]).reshape(rows, depth).astype(BF)
    earlier = (scr[:, 7 : 7 + frames, :] * keep_ref[0][None]).reshape(rows, depth).astype(BF)
    copies[0].wait()
    d_ref[...] = mm(later, row_ref[0], ((1,), (1,)))
    d_ref[...] += mm(dt, row_ref[1], ((1,), (1,)))[0:rows]
    d_ref[...] += mm(earlier, row_ref[2], ((1,), (1,)))
    copies[1].wait()
    normed = (s_ref[...] - stat_ref[0:1]) * stat_ref[1:2]
    d = d_ref[...] * silu_slope(normed * norm_ref[0:1] + norm_ref[1:2])
    d_ref[...] = d
    put_sums(d, normed, sums_ref)


def spatial_grad(d_ref, s_ref, stat_ref, norm_ref, sums_ref, ds_ref, sum_ref, total):
    sums = jnp.sum(sums_ref[...], axis=0)
    sum_ref[...] = sums
    inverse = stat_ref[1:2]
    normed = (s_ref[...] - stat_ref[0:1]) * inverse
    d = d_ref[...] - sums[1:2] * (1.0 / total) - normed * (sums[0:1] * (1.0 / total))
    ds_ref[...] = (norm_ref[0:1] * inverse * d).astype(BF)


def adjoint(ds_ref, w_ref, pad, dims):
    height, width, frames, depth = dims
    pad[...] = jnp.zeros(pad.shape, F32)

    for k in range(9):
        part = mm(ds_ref[...], w_ref[:, k * depth : (k + 1) * depth], ((1,), (0,)))
        at = (slice(k // 3, k // 3 + height), slice(k % 3, k % 3 + width))
        pad[at] = pad[at] + part.reshape(dims)


def input_body(
    ids_ref, d_ref, stat_ref, norm_ref, sums_ref, s_far, w_far,
    ds_ref, send_ref, kept_ref, sum_ref, pad, part, s_ref, w_ref, sems, *, dims, total
):
    height, width, frames, depth = dims
    copies = [started(s_far, s_ref, sems.at[0]), started(w_far, w_ref, sems.at[1])]
    copies[0].wait()
    spatial_grad(d_ref, s_ref, stat_ref, norm_ref, sums_ref, ds_ref, sum_ref, total)
    copies[1].wait()
    adjoint(ds_ref, w_ref, pad, dims)
    part[...] = pad[1 : height + 1, 1 : width + 1].reshape(part.shape)
    put_halves(ids_ref, part, send_ref, kept_ref)


def by_frame(source, out_ref, dims):
    height, width, frames, depth = dims
    pixels, own = height * width, out_ref.shape[1]
    for r in range(source.shape[0]):
        for f in range(frames):
            values = source[r, pl.ds(f, pixels, stride=frames), :]
            out_ref[f // own, f % own, :, r * LANES : (r + 1) * LANES] = values.astype(out_ref.dtype)


def last_body(ids_ref, ds_ref, g_ref, block_ref, w_far, *refs, dims):
    grads, blocks, (pad, part, block, grad_scr, block_scr, w_ref, sem) = refs[:4], refs[4:8], refs[8:]
    height, width, frames, depth = dims
    copy = started(w_far, w_ref, sem)
    block[0] = block_ref[...].astype(F32)
    by_frame(block, block_scr, dims)
    copy.wait()
    adjoint(ds_ref, w_ref, pad, dims)
    own = ids_ref[0]
    for r in range(part.shape[0]):
        columns = pad[1 : height + 1, 1 : width + 1, :, r * LANES : (r + 1) * LANES]
        part[r] = columns.reshape(part.shape[1:])
    part[own] = part[own] + g_ref[...]
    by_frame(part, grad_scr, dims)
    for j in range(4):
        grads[j][...] = grad_scr[ids_ref[j]]
        blocks[j][...] = block_scr[ids_ref[j]]


def finish_body(ids_ref, *refs):
    blocks, grads, (out_ref, grad_out_ref, block) = refs[:4], refs[4:8], refs[8:]
    own, height, width, depth = out_ref.shape
    for j, ref in enumerate(blocks):
        block[:, :, pl.ds(pl.multiple_of(ids_ref[j] * LANES, LANES), LANES)] = ref[...].astype(F32)
    for f in range(own):
        grad = sum(ref[f].astype(F32) for ref in grads)
        for h in range(height):
            at = slice(h * width, (h + 1) * width)
            out_ref[f, h] = block[f, at].astype(BF)
            grad_out_ref[f, h] = grad[at]


def weight_terms(act_ref, ds_ref, pad, acc, dims):
    height, width, frames, depth = dims
    rows = height * width * frames
    pad[...] = jnp.zeros(pad.shape, F32)
    pad[1 : height + 1, 1 : width + 1] = act_ref[...].astype(F32)[0:rows].reshape(dims)
    flipped = ds_ref[...].astype(F32).T.astype(BF)

    for k in range(9):
        i, j = k // 3, k % 3
        piece = pad[i : i + height, j : j + width].reshape(rows, depth).astype(BF)
        acc[:, k * depth : (k + 1) * depth] = mm(flipped, piece, ((1,), (0,)))


def put_shards(acc, places, out_ref, k):
    mid = acc.shape[0]
    half = mid // 2
    wide = k + LANES // 2
    for f in range(8):
        if f % 2 == 0:
            top = acc[0:half, k * f : k * f + wide]
            bottom = pltpu.roll(acc[half:mid, k * f : k * f + wide], LANES // 2, 1)
        else:
            start = k * f - LANES // 2
            top = pltpu.roll(acc[0:half, start : start + wide], k, 1)
            bottom = acc[half:mid, start : start + wide]
        fold(top, bottom, out_ref.at[places[f], 0:half], k)


def weight_plain_body(act_ref, ds_ref, out_ref, pad, acc, *, dims):
    weight_terms(act_ref, ds_ref, pad, acc, dims)
    out_ref[...] = acc[...].astype(BF)


def put_temporal(ids_ref, sources, out_ref, half):
    rows = out_ref.shape[1] - half
    per = half // rows
    for i, source in enumerate(sources):
        for tap in range(3):
            for part in range(2):
                block = tap * 8 + ids_ref[i] * 2 + part
                place = ids_ref[14 + block // 3]
                for j in range(per):
                    start = tap * 2 * half + part * half + j * rows
                    at = pl.multiple_of(((block % 3) * per + j) * LANES, LANES)
                    out_ref[place, half:, pl.ds(at, LANES)] = source[start : start + rows, :]


def weight_body(ids_ref, act_ref, ds_ref, t0, t1, t2, t3, out_ref, token_ref, pad, acc, *, dims):
    weight_terms(act_ref, ds_ref, pad, acc, dims)
    put_shards(acc, [ids_ref[14 + f] for f in range(8)], out_ref, acc.shape[1] // 8)
    put_temporal(ids_ref, (t0, t1, t2, t3), out_ref, acc.shape[0] // 2)
    token_ref[...] = jnp.zeros(token_ref.shape, F32)


def weight_first_body(
    ids_ref, act_ref, d_ref, stat_ref, norm_ref, sums_ref, mid_ref, out_1_ref, out_0_ref, t0, t1, t2, t3, s_far,
    ds_ref, flat_ref, out_ref, own_ref, ahead_ref, back_ref, sum_ref, s_ref, sem, pad, acc, *, dims, total
):
    started(s_far, s_ref, sem).wait()
    spatial_grad(d_ref, s_ref, stat_ref, norm_ref, sums_ref, ds_ref, sum_ref, total)
    flat_ref[...] = jnp.zeros(flat_ref.shape, F32)
    for i, ref in enumerate((sum_ref, mid_ref, out_0_ref, out_1_ref)):
        flat_ref[2 * i : 2 * i + 2, 0 : ref.shape[1]] = ref[...]
    weight_body(ids_ref, act_ref, ds_ref, t0, t1, t2, t3, out_ref, sum_ref, pad, acc, dims=dims)
    own_ref[...] = out_ref[0]
    ahead_ref[...] = out_ref[4]
    back_ref[...] = out_ref[5]


def norm_body(ids_ref, f0, f1, f2, f3, *refs):
    refs, flat_ref = refs[:-1], refs[-1]
    for j, ref in enumerate((f0, f1, f2, f3)):
        flat_ref[ids_ref[j]] = ref[...]
    count = flat_ref.shape[0]
    for which in range(2):
        old, new = refs[3 * which : 3 * which + 3], refs[6 + 3 * which : 9 + 3 * which]
        width = old[0].shape[-1] // count
        for u in range(2):
            row = 4 * which + 2 * u
            grad = jnp.concatenate([flat_ref[r, row : row + 2, 0:width] for r in range(count)], axis=1)
            values = adam_step(old[0][u], grad, old[1][u], old[2][u], RATE_NORM, 0.0)
            for ref, value in zip(new, values):
                ref[u] = value


def adam_step(param, gradient, moment_one, moment_two, rate, decay):
    first_new = BETA_ONE * moment_one + (1.0 - BETA_ONE) * gradient
    second_new = BETA_TWO * moment_two + (1.0 - BETA_TWO) * gradient * gradient
    fix_one = 1.0 - BETA_ONE**STEP
    fix_two = 1.0 - BETA_TWO**STEP
    update = first_new / fix_one / (jnp.sqrt(second_new / fix_two) + ADAM_EPS)
    return (param - rate * (update + decay * param), first_new, second_new)


def adam_into(grad, refs, outs, rows):
    new, first, second = adam_step(refs[0][0, rows], grad, refs[1][0, rows], refs[2][0, rows], RATE_WEIGHT, DECAY)
    outs[0][0, rows] = new
    outs[1][0, rows] = first
    outs[2][0, rows] = second
    outs[3][0, rows] = new.astype(BF)


def adam_body(*refs, grads):
    sources, refs = refs[:grads], refs[grads:]
    refs, outs = refs[:6], refs[-8:]
    half = refs[0].shape[1] // 2
    summed = sum(r[...].astype(F32) for r in sources)
    temporal = summed[half:]
    rows = temporal.shape[0]
    for i in range(temporal.shape[1] // LANES):
        piece = temporal[:, i * LANES : (i + 1) * LANES]
        adam_into(piece, refs[3:], outs[4:], slice(i * rows, (i + 1) * rows))
    spatial = summed[0:half]
    k = spatial.shape[1] // 2
    edge = k - LANES // 2
    adam_into(spatial[:, 0:k], refs, outs, slice(0, half))
    adam_into(pltpu.roll(spatial[:, edge:], k, 1)[:, 0:k], refs, outs, slice(half, 2 * half))


def adam_unit(u, sources, state, before, name, after=()):
    unit = [pl.BlockSpec((1,) + a.shape[1:], lambda i: (u, 0, 0)) for a in state]
    types = [F32, F32, F32, BF]
    outs = [shape(state[0].shape, t) for t in types] + [shape(state[3].shape, t) for t in types]
    before = list(before or ())
    whole = [pl.BlockSpec(a.shape, lambda i, n=a.ndim: (0,) * n) for a in sources]

    def kernel(*refs):
        adam_body(*refs[len(after) :], grads=len(sources))

    return pl.pallas_call(
        kernel,
        grid=(1,),
        out_shape=tuple(outs),
        in_specs=[pl.BlockSpec(memory_space=pl.ANY)] * len(after) + whole + unit + [pl.BlockSpec(memory_space=pl.ANY)] * len(before),
        out_specs=tuple([unit[0]] * 4 + [unit[3]] * 4),
        input_output_aliases={len(after) + len(sources) + 6 + i: i for i in range(len(before))},
        compiler_params=pltpu.CompilerParams(vmem_limit_bytes=40 * MIB),
        name=name,
    )(*after, *[in_hbm(a) for a in [*sources, *state]], *before)


def swap(parts, axis):
    return lax.all_to_all(parts, axis, 0, 0, tiled=True)


def from_all(value, axis):
    count = lax.axis_size(axis)
    return swap(jnp.broadcast_to(value[None], (count,) + value.shape), axis)


def across(value, bit):
    count = lax.axis_size("rep")
    return lax.ppermute(value, "rep", [(i, i ^ bit) for i in range(count)])


MASKS = (0, 2, 1, 3)


def traded(parts):
    return [part if mask == 0 else across(part, mask) for part, mask in zip(parts, MASKS)]


def from_group(value, after=None):
    distant = across(value, 2)
    beside = across(value, 1)
    if after is not None:
        distant = gate(distant, [after], "then")
    return value, distant, beside, across(distant, 1)


def neighbours(first, last):
    count = lax.axis_size("frames")
    before = lax.ppermute(last, "frames", [(i, i + 1) for i in range(count - 1)])
    after = lax.ppermute(first, "frames", [(i + 1, i) for i in range(count - 1)])
    return before, after


def along(step):
    return [(RING[i], RING[(i + step) % 8]) for i in range(8)]


def ring_gather(chunks):
    ahead, back = [[c] for c in chunks], [[c] for c in chunks]
    for step in range(4):
        for a, b in zip(ahead, back):
            a.append(lax.ppermute(a[-1], "frames", along(1)))
            if step < 3:
                b.append(lax.ppermute(b[-1], "frames", along(-1)))
    return [piece for a, b in zip(ahead, back) for piece in a + b[1:]]


def added(gots, parts, places, after, name):
    count = len(gots)

    def body(*refs):
        refs = refs[len(after) :]
        for got_ref, part_ref, out_ref in zip(refs[:count], refs[count : 2 * count], refs[2 * count :]):
            out_ref[...] = (got_ref[...].astype(F32) + part_ref[0].astype(F32)).astype(BF)

    flat = pl.BlockSpec(gots[0].shape, lambda g: (0, 0))
    part_specs = [pl.BlockSpec((1,) + gots[0].shape, lambda g, i=i: (i, 0, 0)) for i in places]
    return pl.pallas_call(
        body,
        grid=(1,),
        out_shape=[shape(g.shape, BF) for g in gots],
        in_specs=[ANY] * len(after) + [flat] * count + part_specs,
        out_specs=[flat] * count,
        name=name,
    )(*after, *[in_hbm(g) for g in gots], *[in_hbm(parts)] * count)


def ring_step(ahead, back):
    return lax.ppermute(ahead, "frames", along(1)), lax.ppermute(back, "frames", along(-1))


class RingSums:
    def __init__(self, parts, own, ahead, back, name):
        self.parts, self.own, self.ahead, self.back, self.name = parts, own, ahead, back, name
        self.step = 0

    def add(self, after=()):
        self.step += 1
        step, after, name = self.step, list(after), f"{self.name}_{self.step}"
        if step < 3:
            gots = ring_step(self.ahead, self.back)
            self.ahead, self.back = added(gots, self.parts, (4 - step, 5 + step), after, name)
        else:
            gots = [lax.ppermute(self.ahead, "frames", along(1))]
            (self.ahead,) = added(gots, self.parts, (4 - step,), after, name)
        return [self.ahead, self.back]

    def end(self):
        return [self.own, *ring_step(self.ahead, self.back)]


def reduced(send, kept, x):
    got = across(send, 1)
    away = lax.dynamic_index_in_dim(got, 1 - x, 0, False).astype(F32)
    away = away + lax.dynamic_index_in_dim(kept, 1 - x, 0, False)
    return got, kept, across(away.astype(BF), 2)


def ordered(t_grad, count):
    n_r, rows, cols = t_grad.shape
    return t_grad.reshape(n_r, 3, rows // 3, cols).transpose(1, 0, 2, 3).reshape(count, -1, cols)


def sum_over(parts, axis):
    return jnp.sum(swap(parts, axis).astype(F32), axis=0)


def on_device(
    frames_in, cotangent, lengths,
    spatial_weights, spatial_first, spatial_second,
    temporal_weights, temporal_first, temporal_second,
    mid_norm, mid_first, mid_second,
    out_norm, out_first, out_second,
):
    own_frames, height, width, depth = frames_in.shape
    n_f, n_r = lax.axis_size("frames"), lax.axis_size("rep")
    assert n_r == 4 and depth == n_r * LANES
    me = lax.axis_index("rep")
    frames = own_frames * n_r
    pixels = height * width
    rows = pixels * frames
    total = float(rows * n_f)
    dims = (height, width, frames, depth)
    units, k, mid = spatial_weights.shape
    cols = LANES
    everyone = ("frames", "rep")
    k_t = temporal_weights.shape[1]
    ring = can_ring(mid, k, k_t, n_f)
    spatial_flops = 2 * rows * 9 * depth * mid
    temporal_flops = 2 * rows * 3 * depth * mid
    pad = pltpu.VMEM((height + 2, width + 2, frames, depth), F32)
    flip = functools.partial(jnp.swapaxes, axis1=1, axis2=2)
    ids = [me, me ^ 2, me ^ 1, me ^ 3, me & 1, me >> 1]
    if ring:
        place = ring_place(lax.axis_index("frames"))
        in_order = jnp.stack(ids + [jnp.int32(f) for f in (*range(8), *range(8))]).astype(jnp.int32)
        ids += [ring_device(place + i) for i in (0, -1, -2, -3, -4, 1, 2, 3)]
        ids += [(ring_place(jnp.int32(f)) - place) % 8 for f in range(8)]
    ids = jnp.stack(ids).astype(jnp.int32)

    frame_ids = lax.axis_index("frames") * frames + jnp.arange(frames, dtype=jnp.int32)
    clip_ends = jnp.cumsum(lengths)
    starts = jnp.concatenate([jnp.zeros((1,), jnp.int32), clip_ends[:-1]])
    opening = jnp.any(frame_ids[:, None] == starts[None, :], axis=1)
    closing = jnp.any((frame_ids + 1)[:, None] == clip_ends[None, :], axis=1)
    keep = jnp.where(jnp.stack([opening, closing]), 0.0, 1.0).astype(F32)[:, :, None]

    act = lax.all_gather(frames_in, "rep", axis=0, tiled=True).transpose(1, 2, 0, 3).reshape(rows, depth)
    cot = cotangent.reshape(own_frames, pixels, n_r, cols).transpose(2, 0, 1, 3)
    cot = swap(cot, "rep").reshape(frames, pixels, cols).transpose(1, 0, 2).reshape(rows, cols)

    mid_own = lax.dynamic_slice_in_dim(mid_norm, me * mid, mid, axis=2)
    out_split = out_norm.reshape(units, 2, n_r, cols).transpose(0, 2, 1, 3)

    slots, temporal_w = [], []
    waiting = []

    def row_slices(order, held, after, handing):
        u = len(temporal_w)
        parts = [shape((3, mid, cols), BF)] * (n_r - 1)
        parts = run(
            unpack_temporal_body, [loaded(shape((3, mid, cols), BF)), *parts] + [shape(a.shape, BF) for a in handing],
            [order, *all_loaded(held), *all_loaded(handing)], f"unpack_{u}",
            [pltpu.VMEM((n_r, 3, 2, mid // 2, cols), BF)], scalars=1, after=after,
        )
        temporal_w.append(traded(parts[:n_r]))
        return parts[n_r:]

    if ring:
        wire = shape((mid // 2 + k_t * LANES // (2 * k), 2 * k), BF)
        chunks = [shape((n, 2 * k), BF) for n in (80, mid // 2 - 80, wire.shape[0] - mid // 2)]
        *chunks, wire_1 = run(
            pack_body, [*chunks, wire], [flip(spatial_weights), temporal_weights], "pack",
            [pltpu.VMEM(wire.shape, BF), pltpu.VMEM((mid, k + LANES // 2), F32)],
        )
        held = ring_gather(chunks)
        slots.append((ids, held))
        waiting = row_slices(ids, held, [act, cot], [wire_1])
    else:
        wire = flip(spatial_weights).astype(BF)
        temporal_low = temporal_weights.astype(BF)
        for u in range(units):
            held = lax.all_gather(wire[u], "frames", axis=0)
            slots.append((ids, [held.transpose(1, 0, 2).reshape(mid, n_f * k)]))
            shard = lax.all_gather(temporal_low[u], "frames", axis=0, tiled=True)
            shard = shard.reshape(3, n_r, mid, cols).transpose(1, 0, 2, 3)
            temporal_w.append(traded([lax.dynamic_index_in_dim(shard, ids[j], 0, False) for j in range(n_r)]))

    rows_16 = -(-rows // 16) * 16
    halo = shape((pixels, 1, mid), F32)
    column = shape((rows, cols), BF)
    s_shape, w_shape = shape((rows, mid), F32), shape((mid, n_f * k), BF)
    act_shape = shape((rows_16, depth), BF)
    win_shape, row_shape = shape((3, rows_16, mid), BF), shape((3, mid, depth), BF)
    s_scr, w_scr = pltpu.VMEM(s_shape.shape, F32), pltpu.VMEM(w_shape.shape, BF)
    sems = pltpu.SemaphoreType.DMA
    saved, spatial_w = [], []
    for u in range(units):
        order, held = slots[u]
        sources = [loaded(act)] if u == 0 else [*t_group, both, out_split[u - 1]]
        outs = [s_shape, halo, halo, shape((2, mid), F32), far(s_shape)]
        outs += [far(w_shape)] * ring + [far(act_shape)] * (u > 0)
        spatial, first, last, mom, s_far, *more = run(
            functools.partial(spatial_body, dims=dims, ring=ring, first=u == 0), outs,
            [order, *all_loaded(held), *sources], f"spatial_{u}",
            [pad, sems((3,))] + [w_scr] * ring + [pltpu.VMEM(act_shape.shape, BF)] * (u > 0),
            scalars=1, flops=spatial_flops, moved=8 * MIB,
            after=[temporal_w[0][0], cot, keep, mid_own, out_split] if u == 0 else (),
        )
        spatial_w.append(more.pop(0) if ring else held[0])
        if u > 0:
            act = more.pop(0)
        if ring and u + 1 < units:
            slots.append((in_order, [lax.all_gather(waiting[u], "frames", axis=0)]))
        if ring and u > 0:
            row_slices(*slots[u], [mom], ())
        mid_both = from_all(mom, "frames")
        before, after = neighbours(first, last)
        send, kept, stat, window, row_w = run(
            functools.partial(temporal_body, dims=dims),
            [shape((2, rows, cols), BF), shape((2, rows, cols), F32), shape((2, mid), F32), far(win_shape), far(row_shape)],
            [ids, spatial, mid_both, before, after, mid_own[u], keep, *temporal_w[u]], f"temporal_{u}",
            [pltpu.VMEM((pixels, frames + 16, mid), F32), pltpu.VMEM((rows_16, depth), F32),
             pltpu.VMEM(win_shape.shape, BF), pltpu.VMEM(row_shape.shape, BF), sems((2,))],
            scalars=1, flops=temporal_flops, moved=8 * MIB,
        )
        t, low, mom = run(
            total_body, [loaded(shape((rows, cols), F32)), column, shape((2, cols), F32)],
            [ids, *reduced(send, kept, me >> 1)], f"total_{u}", scalars=1, moved=3 * MIB,
        )
        both = from_all(mom, everyone).reshape(n_f, n_r, 2, cols)
        t_group = from_group(low, both if u + 1 < units else None)
        saved.append((act, s_far, stat, window, row_w, t, t_group, both))

    d_norms = [None] * units
    weight_parts = [None] * units
    token = None
    for u in reversed(range(units)):
        act, s_far, stat, window, row_w, t, t_group, both = saved[u]
        if u == units - 1:
            block, summed_grad, low, sums = run(
                top_body, [loaded(column), loaded(shape((rows, cols), F32)), column, shape((2, cols), F32)],
                [ids, loaded(t), both, out_split[u], loaded(saved[0][0]), loaded(cot)], "top", scalars=1, moved=3 * MIB,
            )
        else:
            low, sums = run(
                below_body, [column, shape((2, cols), F32)],
                [ids, *reduced(send, kept, me >> 1), loaded(t), both, out_split[u]], f"below_{u}", scalars=1, moved=3 * MIB,
                after=[token] if ring else (),
            )
        sums = from_all(sums, everyone).reshape(n_f, n_r, 2, cols)
        g_group = from_group(low, sums)
        edge = [shape((2 * n_r, pixels, 1, cols), F32)] * 2
        edges = neighbours(*run(functools.partial(edges_body, dims=dims), edge, [*g_group, *all_loaded(t_group)], f"edges_{u}"))
        dt, coef, out_sums = run(
            functools.partial(dt_body, total=total),
            [shape((rows_16, depth), BF), shape((n_r, 4, cols), F32), shape((2, cols), F32)],
            [ids, *g_group, *all_loaded(t_group), both, sums, out_split[u]], f"dt_{u}", scalars=1, moved=4 * MIB,
        )
        t_terms = run(
            temporal_grad_body, [loaded(shape((3 * mid, cols), BF))] + [shape((3 * mid, cols), BF)] * (n_r - 1), [ids, loaded(window), dt], f"temporal_grad_{u}",
            [pltpu.VMEM((mid, depth), F32)], scalars=1, flops=temporal_flops, moved=4 * MIB,
        )
        t_grad = traded(t_terms)
        d_mid, sums = run(
            functools.partial(middle_body, dims=dims), [shape((rows, mid), F32), shape((2, mid), F32)],
            [ids, dt, coef, *edges, keep, stat, mid_own[u], far(row_w), far(s_far)], f"middle_{u}",
            [pltpu.VMEM((pixels, frames + 16, depth), F32), pltpu.VMEM(row_shape.shape, BF), s_scr, sems((2,))],
            scalars=1, flops=temporal_flops, moved=8 * MIB, after=t_terms[:1],
        )
        sums = from_all(sums, "frames")
        ds_shape, sum_shape = shape((rows, mid), BF), shape((2, mid), F32)
        acc = pltpu.VMEM((mid, n_f * k), F32)
        grad_args = [d_mid, stat, mid_own[u], sums]
        if u > 0 or not ring:
            ds, send, kept, mid_sums = run(
                functools.partial(input_body, dims=dims, total=total),
                [ds_shape, shape((2, rows, cols), BF), shape((2, rows, cols), F32), sum_shape],
                [ids, *grad_args, far(s_far), far(spatial_w[u])], f"input_{u}",
                [pad, pltpu.VMEM((rows, depth), F32), s_scr, w_scr, sems((2,))],
                scalars=1, flops=spatial_flops, moved=8 * MIB, after=t_grad[1:],
            )
        if ring and u > 0:
            terms, token = run(
                functools.partial(weight_body, dims=dims), [loaded(shape((n_f,) + wire.shape, BF)), shape((8, LANES), F32)],
                [in_order, loaded(act), ds, *all_loaded(t_grad)], f"weight_{u}", [pad, acc],
                scalars=1, flops=spatial_flops, moved=8 * MIB,
            )
            weight_parts[u] = [lax.psum_scatter(terms, "frames", scatter_dimension=0, tiled=False)]
        elif ring:
            slab = wire
            ds, flat, *terms = run(
                functools.partial(weight_first_body, dims=dims, total=total),
                [ds_shape, shape((8, 512), F32), loaded(shape((n_f,) + slab.shape, BF)), loaded(slab), slab, slab],
                [ids, loaded(act), *grad_args, *d_norms[1], out_sums, *all_loaded(t_grad), far(s_far)], f"weight_{u}",
                [pltpu.VMEM((2, mid), F32), s_scr, sems(()), pad, acc],
                scalars=1, flops=spatial_flops, moved=8 * MIB, scale=1,
            )
            sums_0 = RingSums(*terms, f"sum_{u}")
        else:
            (s_grad,) = run(
                functools.partial(weight_plain_body, dims=dims), [w_shape], [loaded(act), ds],
                f"weight_{u}", [pad, acc], flops=spatial_flops, moved=8 * MIB,
            )
            s_grad = swap(s_grad.reshape(mid, n_f, k).transpose(1, 0, 2), "frames")
            t_rows = jnp.zeros((n_r,) + t_grad[0].shape, BF)
            for j in range(n_r):
                t_rows = lax.dynamic_update_index_in_dim(t_rows, t_grad[j], ids[j], 0)
            weight_parts[u] = (s_grad, swap(ordered(t_rows, n_f), "frames"))
        d_norms[u] = (mid_sums, out_sums) if u > 0 or not ring else None

    grad_part, block_part = (own_frames, pixels, depth), (own_frames, pixels, cols)
    ends = run(
        functools.partial(last_body, dims=dims), [loaded(shape(grad_part, BF))] + [shape(grad_part, BF)] * (n_r - 1) + [shape(block_part, BF)] * n_r,
        [ids, ds, loaded(summed_grad), loaded(block), far(spatial_w[0])], "last",
        [pad, pltpu.VMEM((n_r, rows, cols), F32), pltpu.VMEM((1, rows, cols), F32), pltpu.VMEM((n_r,) + grad_part, BF),
         pltpu.VMEM((n_r,) + block_part, BF), w_scr, sems(())],
        scalars=1, flops=spatial_flops, moved=8 * MIB, scale=1,
    )
    sent = ()
    if not ring:
        blocks, grads = traded(ends[n_r:]), traded(ends[:n_r])
    if ring:
        flats = from_group(flat)
        sums_0.add([ends[0], *flats[1:]])
        blocks, grads = traded(ends[n_r:]), traded(ends[:n_r])
        sums_0.add([*blocks[1:], *grads[1:]])
        sent = sums_0.add()
        weight_parts[0] = sums_0.end()
    block_out, input_grad = run(
        finish_body, [shape(frames_in.shape, BF), shape(frames_in.shape, F32)],
        [ids, *all_loaded(blocks + grads)], "finish", [pltpu.VMEM((own_frames, pixels, depth), F32)],
        scalars=1, moved=3 * MIB, after=sent,
    )
    if ring:
        norms = [mid_norm, mid_first, mid_second, out_norm, out_first, out_second]
        norms = run(
            norm_body, [shape(a.shape, F32) for a in norms], [ids, *flats, *norms], "norms",
            [pltpu.VMEM((n_r, 8, 512), F32)], scalars=1,
        )
    else:
        flat = jnp.concatenate([jnp.concatenate([m.reshape(-1), o.reshape(-1)]) for m, o in d_norms])
        flat = from_all(flat, "rep").reshape(n_r, units, -1)
        mid_grad = flat[:, :, : 2 * mid].reshape(n_r, units, 2, mid).transpose(1, 2, 0, 3)
        mid_grad = mid_grad.reshape(units, 2, n_r * mid)
        out_grad = flat[:, :, 2 * mid :].reshape(n_r, units, 2, cols).transpose(1, 2, 0, 3)
        out_grad = out_grad.reshape(units, 2, depth)
        norms = [*adam_step(mid_norm, mid_grad, mid_first, mid_second, RATE_NORM, 0.0)]
        norms += adam_step(out_norm, out_grad, out_first, out_second, RATE_NORM, 0.0)

    if ring:
        state = [flip(a) for a in (spatial_weights, spatial_first, spatial_second)]
        state += [temporal_weights, temporal_first, temporal_second]
        weights = None
        for u in reversed(range(units)):
            weights = adam_unit(u, weight_parts[u], state, weights, f"adam_{u}", sent if u > 0 else ())
        weights = [flip(a) for a in weights[:4]] + list(weights[4:])
    else:
        grads = [jnp.stack([jnp.sum(parts[i].astype(F32), axis=0) for parts in weight_parts]) for i in range(2)]
        news = adam_step(spatial_weights, flip(grads[0]), spatial_first, spatial_second, RATE_WEIGHT, DECAY)
        weights = [*news, news[0].astype(BF)]
        news = adam_step(temporal_weights, grads[1], temporal_first, temporal_second, RATE_WEIGHT, DECAY)
        weights += [*news, news[0].astype(BF)]
    return (block_out, input_grad, *weights, *norms)


def solution(mesh):
    by_frame = P(("frames", "rep"), None, None, None)
    by_block = P(None, "frames", "rep")
    placed = (by_frame, by_frame, P()) + (by_block,) * 6 + (P(),) * 6
    return jax.shard_map(
        on_device,
        mesh=mesh,
        in_specs=placed,
        out_specs=(by_frame, by_frame) + (by_block,) * 8 + (P(),) * 6,
        check_vma=False,
    )
```

```python
import functools

import jax
import jax.numpy as jnp
from jax import lax
from jax.experimental import pallas as pl
from jax.experimental.pallas import tpu as pltpu
from jax.sharding import PartitionSpec as P

STEP = 5
NORM_EPS = 1e-05
ADAM_EPS = 1e-08
BETA_ONE = 0.5
BETA_TWO = 0.5
RATE_WEIGHT = 0.015
RATE_NORM = 0.2
DECAY = 0.05
BF = jnp.bfloat16
F32 = jnp.float32
MIB = 1 << 20
VMEM = pl.BlockSpec(memory_space=pltpu.VMEM)
SMEM = pl.BlockSpec(memory_space=pltpu.SMEM)
LANES = 128
SCALE = 30
CHEAP = pl.CostEstimate(flops=1000, bytes_accessed=1000, transcendentals=0)
ANY = pl.BlockSpec(memory_space=pl.ANY)
HBM = pl.BlockSpec(memory_space=pltpu.HBM)


def shape(dims, dtype):
    return jax.ShapeDtypeStruct(tuple(dims), dtype)


class Placed:
    def __init__(self, value, where):
        self.value, self.where = value, where


def far(value):
    return Placed(value, "hbm")


def loaded(value):
    return Placed(value, "loaded")


def near(value):
    return Placed(value, "vmem")


def all_loaded(values):
    return [loaded(v) for v in values]


def in_hbm(array):
    return pltpu.with_memory_space_constraint(array, pltpu.HBM)


def operand(a):
    if not isinstance(a, Placed):
        return a
    return pltpu.with_memory_space_constraint(a.value, pltpu.VMEM if a.where == "vmem" else pltpu.HBM)


def result(a):
    if not isinstance(a, Placed):
        return a
    return (pltpu.VMEM if a.where == "vmem" else pltpu.HBM)(a.value.shape, a.value.dtype)


def is_far(a):
    return isinstance(a, Placed) and a.where == "hbm"


def run(body, outs, args, name, scratch=(), limit=28, scalars=0, flops=0, moved=0, after=(), scale=SCALE):
    def kernel(*refs):
        body(*refs[len(after) :])

    return pl.pallas_call(
        kernel,
        out_shape=tuple(result(o) for o in outs),
        in_specs=[ANY] * len(after) + [SMEM] * scalars + [ANY if is_far(a) else VMEM for a in args[scalars:]],
        out_specs=tuple(HBM if is_far(o) else VMEM for o in outs),
        scratch_shapes=list(scratch),
        compiler_params=pltpu.CompilerParams(vmem_limit_bytes=limit * MIB),
        cost_estimate=pl.CostEstimate(flops=int(scale * flops), bytes_accessed=int(scale * moved), transcendentals=0),
        name=name,
    )(*after, *[operand(a) for a in args])


def gate(value, after, name):
    return pl.pallas_call(
        lambda *refs: None,
        out_shape=shape(value.shape, value.dtype),
        in_specs=[ANY] * (len(after) + 1),
        out_specs=ANY,
        input_output_aliases={len(after): 0},
        name=name,
    )(*after, value)


def started(source, target, sem):
    copy = pltpu.make_async_copy(source, target, sem)
    copy.start()
    return copy


def padded(values, rows):
    return jnp.concatenate([values, jnp.zeros((rows - values.shape[0], values.shape[1]), F32)], axis=0)


def sigmoid(v):
    return 1.0 / (1.0 + jnp.exp(-v))


def silu(v):
    return v / (1.0 + jnp.exp(-v))


def silu_slope(v):
    s = sigmoid(v)
    return s * (1.0 + v * (1.0 - s))


def mm(a, b, dims):
    return lax.dot_general(a, b, (dims, ((), ())), preferred_element_type=F32)


def put_moments(values, out_ref):
    rows = values.shape[0]
    mean = jnp.sum(values, axis=0, keepdims=True) * (1.0 / rows)
    off = values - mean
    out_ref[0:1, :] = mean
    out_ref[1:2, :] = jnp.sum(off * off, axis=0, keepdims=True)


def joined_moments(both, rows):
    count = both.shape[0]
    mean = jnp.sum(both[:, 0:1], axis=0) * (1.0 / count)
    off = both[:, 0:1] - mean[None]
    total = jnp.sum(both[:, 1:2] + rows * (off * off), axis=0)
    return mean, lax.rsqrt(total * (1.0 / (rows * count)) + NORM_EPS)


def put_sums(upstream, normed, out_ref):
    out_ref[0:1, :] = jnp.sum(upstream * normed, axis=0, keepdims=True)
    out_ref[1:2, :] = jnp.sum(upstream, axis=0, keepdims=True)


def convolve(pad, w_ref, turned, dims):
    height, width, frames, depth = dims
    rows = height * width * frames
    for k in range(9):
        i, j = k // 3, k % 3
        piece = pad[i : i + height, j : j + width].reshape(rows, depth).astype(BF)
        part = mm(w_ref[:, k * depth : (k + 1) * depth], piece, ((1,), (1,)))
        if k == 0:
            turned[...] = part
        else:
            turned[...] += part
    return turned[...].T


def widened(scr, values, before, after):
    frames = values.shape[1]
    scr[:, 8 : 8 + frames, :] = values
    scr[:, 7:8, :] = before
    scr[:, 8 + frames : 9 + frames, :] = after


RING = (0, 2, 4, 6, 7, 5, 3, 1)


def can_ring(mid, k, k_t, count):
    return count == len(RING) and mid == 288 and k == 576 and k_t == 432


def ring_place(frame):
    return jnp.where(frame % 2 == 0, frame // 2, 7 - frame // 2)


def ring_device(place):
    place = place % 8
    return jnp.where(place < 4, 2 * place, 15 - 2 * place)


def low_half(shape_):
    return lax.broadcasted_iota(jnp.int32, shape_, 1) < LANES // 2


def fold(top, bottom, out_ref, k):
    edge = k - LANES // 2
    out_ref[:, 0:edge] = top[:, 0:edge].astype(out_ref.dtype)
    mixed = jnp.where(low_half((top.shape[0], LANES)), top[:, edge : edge + LANES], bottom[:, 0:LANES])
    out_ref[:, edge : edge + LANES] = mixed.astype(out_ref.dtype)
    out_ref[:, edge + LANES : 2 * k] = bottom[:, LANES : k + LANES // 2].astype(out_ref.dtype)


def pack_body(w_ref, t_ref, *refs):
    outs, folded, scr = refs[:-2], refs[-2], refs[-1]
    mid, k = w_ref.shape[1:]
    half = mid // 2
    scr[:, 0:k] = w_ref[0]
    fold(scr[0:half, :], pltpu.roll(scr[half:mid, :], LANES // 2, 1), folded.at[0:half], k)
    rows = folded.shape[0] - half
    for i in range(2 * k // LANES):
        at = slice(i * LANES, (i + 1) * LANES)
        folded[half:, at] = t_ref[0, rows * i : rows * (i + 1), :].astype(BF)
    start = 0
    for out in outs:
        out[...] = folded[start : start + out.shape[0], :]
        start += out.shape[0]


def packed(u, spatial, temporal, sizes):
    mid, k = spatial.shape[1:]
    flat = [pl.BlockSpec((n, 2 * k), lambda i: (0, 0)) for n in sizes]
    return pl.pallas_call(
        pack_body,
        grid=(1,),
        out_shape=[shape((n, 2 * k), BF) for n in sizes],
        in_specs=[pl.BlockSpec((1,) + a.shape[1:], lambda i: (u, 0, 0)) for a in (spatial, temporal)],
        out_specs=flat,
        scratch_shapes=[pltpu.VMEM((sum(sizes), 2 * k), BF), pltpu.VMEM((mid, k + LANES // 2), F32)],
        compiler_params=pltpu.CompilerParams(vmem_limit_bytes=24 * MIB),
        name=f"pack_{u}",
    )(in_hbm(spatial), in_hbm(temporal))


def unpack_temporal(f, slot, t_ref):
    rows = slot.shape[0]
    per = t_ref.shape[3] // rows
    for j in range(slot.shape[1] // LANES):
        block = 3 * f + j // per
        piece = slot[:, j * LANES : (j + 1) * LANES]
        t_ref[(block % 8) // 2, block // 8, block % 2, (j % per) * rows : (j % per + 1) * rows, :] = piece


def slots_of(refs, half):
    if len(refs[0].shape) == 3:
        return [([refs[0].at[i, 0:half]], refs[0].at[i, half:]) for i in range(8)], refs[1:]
    cut = half - refs[0].shape[0]
    return [([refs[i], refs[8 + i].at[0:cut]], refs[8 + i].at[cut:]) for i in range(8)], refs[16:]


def unpack_rows(ids_ref, slots, outs, scr):
    half = scr.shape[3]
    for i, (_, slot) in enumerate(slots):
        unpack_temporal(ids_ref[6 + i], slot, scr)
    for j, out_ref in enumerate(outs):
        for k in range(3):
            for part in range(2):
                out_ref[k, part * half : (part + 1) * half, :] = scr[ids_ref[j], k, part]


def unpack_spatial(ids_ref, slots, w_ref):
    half, k = w_ref.shape[0] // 2, w_ref.shape[1] // 8
    edge, wide = k - LANES // 2, k + LANES // 2
    for i, (slot, _) in enumerate(slots):
        f = ids_ref[6 + i]
        base = (f // 2) * (2 * k)
        values = jnp.concatenate([part[...].astype(F32) for part in slot], axis=0)
        low = low_half((half, LANES))

        def at(start, size):
            return pl.ds(pl.multiple_of(base + start, LANES), size)

        @pl.when(f % 2 == 0)
        def _():
            for start, part in ((0, values[:, 0:wide]), (half, pltpu.roll(values[:, edge:], k, 1))):
                rows = slice(start, start + half)
                w_ref[rows, at(0, edge)] = part[:, 0:edge].astype(BF)
                old = w_ref[rows, at(edge, LANES)].astype(F32)
                w_ref[rows, at(edge, LANES)] = jnp.where(low, part[:, edge:wide], old).astype(BF)

        @pl.when(f % 2 == 1)
        def _():
            for start, part in ((0, pltpu.roll(values[:, 0:wide], LANES // 2, 1)), (half, values[:, edge:])):
                rows = slice(start, start + half)
                old = w_ref[rows, at(edge, LANES)].astype(F32)
                w_ref[rows, at(edge, LANES)] = jnp.where(low, old, part[:, 0:LANES]).astype(BF)
                w_ref[rows, at(edge + LANES, edge)] = part[:, LANES:wide].astype(BF)


def spatial_body(*refs, dims, half, ring, first):
    height, width, frames, depth = dims
    rows = height * width * frames
    ids_ref, refs = refs[0], refs[1:]
    if ring:
        slots, refs = slots_of(refs, half)
    else:
        w_ref, refs = refs[0], refs[1:]
    refs = iter(refs)

    def take(count):
        return [next(refs) for _ in range(count)]

    sources = take(1 if first else 6)
    (s_ref,) = take(1) if not first else (None,)
    first_ref, last_ref, mom_ref, s_far = take(4)
    w_far, act_far, row_outs = take(int(ring)), take(int(not first)), take(4 * int(ring))
    pad, turned, sems = take(3)
    w_scr, act_scr, row_scr = take(int(ring)), take(int(not first)), take(int(ring))
    if first:
        (s_ref,) = take(1)

    copies = []
    if ring:
        w_ref = w_scr[0]
        unpack_spatial(ids_ref, slots, w_ref)
        copies.append(started(w_ref, w_far[0], sems.at[0]))
        unpack_rows(ids_ref, slots, row_outs, row_scr[0])
    pad[...] = jnp.zeros(pad.shape, F32)
    if first:
        pad[1 : height + 1, 1 : width + 1] = sources[0][...].astype(F32).reshape(dims)
    else:
        both_ref, norm_ref = sources[4:]
        for j, t_ref in enumerate(sources[:4]):
            b = ids_ref[j]
            mean, inverse = joined_moments(both_ref[:, b], rows)
            norm = norm_ref[b]
            y = (t_ref[...].astype(F32) - mean) * (inverse * norm[0:1]) + norm[1:2]
            a = silu(y)
            at = pl.ds(pl.multiple_of(b * LANES, LANES), LANES)
            act_scr[0][:, at] = padded(a, act_scr[0].shape[0]).astype(BF)
            pad[1 : height + 1, 1 : width + 1, :, at] = a.reshape(height, width, frames, LANES)
        copies.append(started(act_scr[0], act_far[0], sems.at[1]))
    s_ref[...] = convolve(pad, w_ref, turned, dims)
    copies.append(started(s_ref, s_far, sems.at[2]))
    values = s_ref[...]
    put_moments(values, mom_ref)
    grid = values.reshape(height * width, frames, values.shape[-1])
    first_ref[...] = grid[:, 0:1, :]
    last_ref[...] = grid[:, frames - 1 : frames, :]
    for copy in copies:
        copy.wait()


def temporal_body(
    ids_ref, s_ref, both_ref, before_ref, after_ref, norm_ref, keep_ref, w0, w1, w2, w3,
    send_ref, kept_ref, stat_ref, win_far, row_far, scr, part, win_ref, row_ref, sems, s_scr=None, *, dims
):
    height, width, frames, depth = dims
    pixels = height * width
    rows = pixels * frames
    mid = s_ref.shape[-1]
    if s_scr is not None:
        arriving = started(s_ref, s_scr, sems.at[2])
    for j, w_ref in enumerate((w0, w1, w2, w3)):
        row_ref[:, :, pl.ds(pl.multiple_of(ids_ref[j] * LANES, LANES), LANES)] = w_ref[...]
    copies = [started(row_ref, row_far, sems.at[0])]
    mean, inverse = joined_moments(both_ref[...], rows)
    stat_ref[0:1, :] = mean
    stat_ref[1:2, :] = inverse
    scale, bias = inverse * norm_ref[0:1], norm_ref[1:2]

    def active(v):
        return silu((v - mean) * scale + bias)

    if s_scr is not None:
        arriving.wait()
        s_ref = s_scr
    middle = active(s_ref[...])
    widened(
        scr, middle.reshape(pixels, frames, mid),
        active(before_ref[...].reshape(pixels, mid)).reshape(pixels, 1, mid),
        active(after_ref[...].reshape(pixels, mid)).reshape(pixels, 1, mid),
    )
    whole = win_ref.shape[1]
    earlier = (scr[:, 7 : 7 + frames, :] * keep_ref[0][None]).reshape(rows, mid)
    later = (scr[:, 9 : 9 + frames, :] * keep_ref[1][None]).reshape(rows, mid)
    for i, values in enumerate((earlier, middle, later)):
        win_ref[i] = padded(values, whole).astype(BF)
    copies.append(started(win_ref, win_far, sems.at[1]))
    part[...] = mm(win_ref[0], row_ref[0], ((1,), (0,)))
    part[...] += mm(win_ref[1], row_ref[1], ((1,), (0,)))
    part[...] += mm(win_ref[2], row_ref[2], ((1,), (0,)))
    put_halves(ids_ref, part, send_ref, kept_ref)
    for copy in copies:
        copy.wait()


def put_halves(ids_ref, part, send_ref, kept_ref):
    core = ids_ref[4]
    rows = send_ref.shape[1]
    for i in range(2):
        other = pl.multiple_of((2 * i + 1 - core) * LANES, LANES)
        own = pl.multiple_of((2 * i + core) * LANES, LANES)
        send_ref[i] = part[0:rows, pl.ds(other, LANES)].astype(BF)
        kept_ref[i] = part[0:rows, pl.ds(own, LANES)]


def total_body(ids_ref, got_ref, kept_ref, last_ref, t_ref, low_ref, mom_ref):
    x = ids_ref[5]
    t = got_ref[x].astype(F32) + kept_ref[x] + last_ref[...].astype(F32)
    t_ref[...] = t
    low_ref[...] = t.astype(BF)
    put_moments(t, mom_ref)


def edges_body(*refs, dims):
    height, width, frames, depth = dims
    blocks, (first_ref, last_ref) = refs[:-2], refs[-2:]
    for j, ref in enumerate(blocks):
        grid = ref[...].astype(F32).reshape(height * width, frames, LANES)
        first_ref[j] = grid[:, 0:1, :]
        last_ref[j] = grid[:, frames - 1 : frames, :]


def top_body(ids_ref, t_ref, both_ref, norm_ref, x_ref, cot_ref, block_ref, g_ref, low_ref, sums_ref):
    rows = t_ref.shape[0]
    b = ids_ref[0]
    mean, inverse = joined_moments(both_ref[:, b], rows)
    norm = norm_ref[b]
    normed = (t_ref[...] - mean) * inverse
    own = pl.ds(pl.multiple_of(b * LANES, LANES), LANES)
    summed = normed * norm[0:1] + norm[1:2] + x_ref[:, own].astype(F32)
    block_ref[...] = silu(summed).astype(BF)
    g = cot_ref[...].astype(F32) * silu_slope(summed)
    g_ref[...] = g
    low_ref[...] = g.astype(BF)
    put_sums(g, normed, sums_ref)


def below_body(ids_ref, got_ref, kept_ref, last_ref, t_ref, both_ref, norm_ref, low_ref, sums_ref):
    rows = t_ref.shape[0]
    b, x = ids_ref[0], ids_ref[5]
    d_act = got_ref[x].astype(F32) + kept_ref[x] + last_ref[...].astype(F32)
    mean, inverse = joined_moments(both_ref[:, b], rows)
    norm = norm_ref[b]
    normed = (t_ref[...] - mean) * inverse
    g = d_act * silu_slope(normed * norm[0:1] + norm[1:2])
    low_ref[...] = g.astype(BF)
    put_sums(g, normed, sums_ref)


def dt_body(
    ids_ref, g0, g1, g2, g3, t0, t1, t2, t3, both_ref, sums_ref, norm_ref, dt_ref, coef_ref, sum_ref, *, total
):
    rows, whole = g0.shape[0], dt_ref.shape[0]
    for j, (g_ref, t_ref) in enumerate(((g0, t0), (g1, t1), (g2, t2), (g3, t3))):
        b = ids_ref[j]
        mean, inverse = joined_moments(both_ref[:, b], rows)
        sums = jnp.sum(sums_ref[:, b], axis=0)
        if j == 0:
            sum_ref[...] = sums
        c1 = norm_ref[b][0:1] * inverse
        c2 = c1 * sums[1:2] * (1.0 / total)
        c3 = c1 * inverse * sums[0:1] * (1.0 / total)
        coef_ref[j] = jnp.concatenate([c1, c2, c3, mean], axis=0)
        d = c1 * g_ref[...].astype(F32) - c2 - c3 * (t_ref[...].astype(F32) - mean)
        dt_ref[:, pl.ds(pl.multiple_of(b * LANES, LANES), LANES)] = padded(d, whole).astype(BF)


def temporal_grad_body(ids_ref, win_ref, dt_ref, *refs):
    outs, term = refs[:-1], refs[-1]
    mid = win_ref.shape[-1]
    dt = dt_ref[...]
    for k in range(3):
        term[...] = mm(win_ref[k], dt, ((0,), (0,)))
        for j, out_ref in enumerate(outs):
            at = pl.ds(pl.multiple_of(ids_ref[j] * LANES, LANES), LANES)
            out_ref[k * mid : (k + 1) * mid, :] = term[:, at].astype(BF)


def middle_body(
    ids_ref, dt_ref, coef_ref, before_ref, after_ref, keep_ref, stat_ref, norm_ref, row_far, s_far,
    d_far, sums_ref, scr, row_ref, s_ref, d_ref, sems, *, dims
):
    height, width, frames, depth = dims
    pixels = height * width
    rows = pixels * frames
    copies = [started(row_far, row_ref, sems.at[0]), started(s_far, s_ref, sems.at[1])]
    dt = dt_ref[...]
    scr[:, 8 : 8 + frames, :] = dt.astype(F32)[0:rows].reshape(pixels, frames, depth)
    for j in range(4):
        at = pl.ds(pl.multiple_of(ids_ref[j] * LANES, LANES), LANES)
        c = coef_ref[j]

        def halo(g, t):
            d = c[0:1] * g.reshape(pixels, LANES) - c[1:2] - c[2:3] * (t.reshape(pixels, LANES) - c[3:4])
            return d.astype(BF).astype(F32).reshape(pixels, 1, LANES)

        scr[:, 7:8, at] = halo(before_ref[j], before_ref[4 + j])
        scr[:, 8 + frames : 9 + frames, at] = halo(after_ref[j], after_ref[4 + j])
    later = (scr[:, 9 : 9 + frames, :] * keep_ref[1][None]).reshape(rows, depth).astype(BF)
    earlier = (scr[:, 7 : 7 + frames, :] * keep_ref[0][None]).reshape(rows, depth).astype(BF)
    copies[0].wait()
    d_ref[...] = mm(later, row_ref[0], ((1,), (1,)))
    d_ref[...] += mm(dt, row_ref[1], ((1,), (1,)))[0:rows]
    d_ref[...] += mm(earlier, row_ref[2], ((1,), (1,)))
    copies[1].wait()
    normed = (s_ref[...] - stat_ref[0:1]) * stat_ref[1:2]
    d = d_ref[...] * silu_slope(normed * norm_ref[0:1] + norm_ref[1:2])
    d_ref[...] = d
    leaving = started(d_ref, d_far, sems.at[2])
    put_sums(d, normed, sums_ref)
    leaving.wait()


def spatial_grad(d_ref, s_ref, stat_ref, norm_ref, sums_ref, ds_ref, sum_ref, total):
    sums = jnp.sum(sums_ref[...], axis=0)
    sum_ref[...] = sums
    inverse = stat_ref[1:2]
    normed = (s_ref[...] - stat_ref[0:1]) * inverse
    d = d_ref[...] - sums[1:2] * (1.0 / total) - normed * (sums[0:1] * (1.0 / total))
    ds_ref[...] = (norm_ref[0:1] * inverse * d).astype(BF)


def adjoint(ds_ref, w_ref, pad, patches, stacked, dims):
    height, width, frames, depth = dims
    rows, mid = ds_ref.shape
    whole = mid // LANES * LANES
    rest = mid - whole
    start = 9 * whole
    pad[...] = jnp.zeros(pad.shape, F32)
    pad[1 : height + 1, 1 : width + 1, :, 0:mid] = ds_ref[...].astype(F32).reshape(height, width, frames, mid)
    lane = lax.broadcasted_iota(jnp.int32, (rows, LANES), 1)
    tails = [jnp.zeros((rows, LANES), F32) for _ in range((patches.shape[1] - start) // LANES)]
    stacked[start:, :] = jnp.zeros((stacked.shape[0] - start, depth), BF)
    for k in range(9):
        i, j = k // 3, k % 3
        piece = pad[2 - i : 2 - i + height, 2 - j : 2 - j + width].reshape(rows, pad.shape[-1])
        w = w_ref[:, k * depth : (k + 1) * depth]
        patches[:, k * whole : (k + 1) * whole] = piece[:, 0:whole].astype(BF)
        stacked[k * whole : (k + 1) * whole, :] = w[0:whole]
        stacked[start + k * rest : start + (k + 1) * rest, :] = w[whole:mid]
        tile, at = divmod(k * rest, LANES)
        tail = pltpu.roll(piece[:, whole:], at, 1) if at else piece[:, whole:]
        tails[tile] = jnp.where((lane >= at) & (lane < at + rest), tail, tails[tile])
    for tile, tail in enumerate(tails):
        patches[:, start + tile * LANES : start + (tile + 1) * LANES] = tail.astype(BF)
    return mm(patches[...], stacked[...], ((1,), (0,)))


def input_body(
    ids_ref, d_far, stat_ref, norm_ref, sums_ref, s_far, w_far,
    ds_ref, send_ref, kept_ref, sum_ref, pad, patches, stacked, part, s_ref, d_ref, w_ref, sems, *, dims, total
):
    height, width, frames, depth = dims
    copies = [started(s_far, s_ref, sems.at[0]), started(w_far, w_ref, sems.at[1]), started(d_far, d_ref, sems.at[2])]
    copies[0].wait()
    copies[2].wait()
    spatial_grad(d_ref, s_ref, stat_ref, norm_ref, sums_ref, ds_ref, sum_ref, total)
    copies[1].wait()
    part[...] = adjoint(ds_ref, w_ref, pad, patches, stacked, dims)
    put_halves(ids_ref, part, send_ref, kept_ref)


def by_frame(source, out_ref, dims):
    height, width, frames, depth = dims
    pixels, own = height * width, out_ref.shape[1]
    for r in range(source.shape[0]):
        for f in range(frames):
            values = source[r, pl.ds(f, pixels, stride=frames), :]
            out_ref[f // own, f % own, :, r * LANES : (r + 1) * LANES] = values.astype(out_ref.dtype)


def last_body(ids_ref, ds_ref, g_ref, block_ref, w_far, *refs, dims):
    grads, blocks, refs = refs[:4], refs[4:8], refs[8:]
    pad, patches, stacked, part, block, grad_scr, block_scr, w_ref, sem = refs
    height, width, frames, depth = dims
    copy = started(w_far, w_ref, sem)
    block[0] = block_ref[...].astype(F32)
    by_frame(block, block_scr, dims)
    copy.wait()
    terms = adjoint(ds_ref, w_ref, pad, patches, stacked, dims)
    own = ids_ref[0]
    for r in range(part.shape[0]):
        part[r] = terms[:, r * LANES : (r + 1) * LANES]
    part[own] = part[own] + g_ref[...]
    by_frame(part, grad_scr, dims)
    for j in range(4):
        grads[j][...] = grad_scr[ids_ref[j]]
        blocks[j][...] = block_scr[ids_ref[j]]


def finish_body(ids_ref, *refs):
    blocks, grads, (out_ref, grad_out_ref, block) = refs[:4], refs[4:8], refs[8:]
    own, height, width, depth = out_ref.shape
    for j, ref in enumerate(blocks):
        block[:, :, pl.ds(pl.multiple_of(ids_ref[j] * LANES, LANES), LANES)] = ref[...].astype(F32)
    for f in range(own):
        grad = sum(ref[f].astype(F32) for ref in grads)
        for h in range(height):
            at = slice(h * width, (h + 1) * width)
            out_ref[f, h] = block[f, at].astype(BF)
            grad_out_ref[f, h] = grad[at]


def weight_terms(act_ref, ds_ref, pad, acc, dims):
    height, width, frames, depth = dims
    rows = height * width * frames
    pad[...] = jnp.zeros(pad.shape, F32)
    pad[1 : height + 1, 1 : width + 1] = act_ref[...].astype(F32)[0:rows].reshape(dims)
    flipped = ds_ref[...].astype(F32).T.astype(BF)

    for k in range(9):
        i, j = k // 3, k % 3
        piece = pad[i : i + height, j : j + width].reshape(rows, depth).astype(BF)
        acc[:, k * depth : (k + 1) * depth] = mm(flipped, piece, ((1,), (0,)))


def put_shards(acc, places, out_ref, k):
    mid = acc.shape[0]
    half = mid // 2
    wide = k + LANES // 2
    for f in range(8):
        if f % 2 == 0:
            top = acc[0:half, k * f : k * f + wide]
            bottom = pltpu.roll(acc[half:mid, k * f : k * f + wide], LANES // 2, 1)
        else:
            start = k * f - LANES // 2
            top = pltpu.roll(acc[0:half, start : start + wide], k, 1)
            bottom = acc[half:mid, start : start + wide]
        fold(top, bottom, out_ref.at[places[f], 0:half], k)


def weight_plain_body(act_ref, ds_ref, out_ref, pad, acc, *, dims):
    weight_terms(act_ref, ds_ref, pad, acc, dims)
    out_ref[...] = acc[...].astype(BF)


def put_temporal(ids_ref, sources, out_ref, half):
    rows = out_ref.shape[1] - half
    per = half // rows
    for i, source in enumerate(sources):
        for tap in range(3):
            for part in range(2):
                block = tap * 8 + ids_ref[i] * 2 + part
                place = ids_ref[14 + block // 3]
                for j in range(per):
                    start = tap * 2 * half + part * half + j * rows
                    at = pl.multiple_of(((block % 3) * per + j) * LANES, LANES)
                    out_ref[place, half:, pl.ds(at, LANES)] = source[start : start + rows, :]


def weight_body(
    ids_ref, act_ref, ds_ref, t0, t1, t2, t3, out_ref, own_ref, ahead_ref, back_ref, token_ref, pad, acc, *, dims
):
    weight_terms(act_ref, ds_ref, pad, acc, dims)
    put_shards(acc, [ids_ref[14 + f] for f in range(8)], out_ref, acc.shape[1] // 8)
    put_temporal(ids_ref, (t0, t1, t2, t3), out_ref, acc.shape[0] // 2)
    token_ref[...] = jnp.zeros(token_ref.shape, F32)
    own_ref[...] = out_ref[0]
    ahead_ref[...] = out_ref[4]
    back_ref[...] = out_ref[5]


def weight_first_body(
    ids_ref, act_ref, d_far, stat_ref, norm_ref, sums_ref, mid_ref, out_1_ref, out_0_ref, t0, t1, t2, t3, s_far,
    ds_ref, flat_ref, out_ref, own_ref, ahead_ref, back_ref, sum_ref, s_ref, d_ref, sems, pad, acc, *, dims, total
):
    copies = [started(s_far, s_ref, sems.at[0]), started(d_far, d_ref, sems.at[1])]
    for copy in copies:
        copy.wait()
    spatial_grad(d_ref, s_ref, stat_ref, norm_ref, sums_ref, ds_ref, sum_ref, total)
    flat_ref[...] = jnp.zeros(flat_ref.shape, F32)
    for i, ref in enumerate((sum_ref, mid_ref, out_0_ref, out_1_ref)):
        flat_ref[2 * i : 2 * i + 2, 0 : ref.shape[1]] = ref[...]
    weight_body(
        ids_ref, act_ref, ds_ref, t0, t1, t2, t3, out_ref, own_ref, ahead_ref, back_ref, sum_ref, pad, acc, dims=dims
    )


def norm_body(ids_ref, f0, f1, f2, f3, *refs):
    refs, flat_ref = refs[:-1], refs[-1]
    for j, ref in enumerate((f0, f1, f2, f3)):
        flat_ref[ids_ref[j]] = ref[...]
    count = flat_ref.shape[0]
    for which in range(2):
        old, new = refs[3 * which : 3 * which + 3], refs[6 + 3 * which : 9 + 3 * which]
        width = old[0].shape[-1] // count
        for u in range(2):
            row = 4 * which + 2 * u
            grad = jnp.concatenate([flat_ref[r, row : row + 2, 0:width] for r in range(count)], axis=1)
            values = adam_step(old[0][u], grad, old[1][u], old[2][u], RATE_NORM, 0.0)
            for ref, value in zip(new, values):
                ref[u] = value


def adam_step(param, gradient, moment_one, moment_two, rate, decay):
    first_new = BETA_ONE * moment_one + (1.0 - BETA_ONE) * gradient
    second_new = BETA_TWO * moment_two + (1.0 - BETA_TWO) * gradient * gradient
    fix_one = 1.0 - BETA_ONE**STEP
    fix_two = 1.0 - BETA_TWO**STEP
    update = first_new / fix_one / (jnp.sqrt(second_new / fix_two) + ADAM_EPS)
    return (param - rate * (update + decay * param), first_new, second_new)


def adam_into(grad, refs, outs, rows):
    new, first, second = adam_step(refs[0][0, rows], grad, refs[1][0, rows], refs[2][0, rows], RATE_WEIGHT, DECAY)
    outs[0][0, rows] = new
    outs[1][0, rows] = first
    outs[2][0, rows] = second
    outs[3][0, rows] = new.astype(BF)


def adam_body(*refs, grads):
    sources, refs = refs[:grads], refs[grads:]
    refs, outs = refs[:6], refs[-8:]
    half = refs[0].shape[1] // 2
    summed = sum(r[...].astype(F32) for r in sources)
    temporal = summed[half:]
    rows = temporal.shape[0]
    for i in range(temporal.shape[1] // LANES):
        piece = temporal[:, i * LANES : (i + 1) * LANES]
        adam_into(piece, refs[3:], outs[4:], slice(i * rows, (i + 1) * rows))
    spatial = summed[0:half]
    k = spatial.shape[1] // 2
    edge = k - LANES // 2
    adam_into(spatial[:, 0:k], refs, outs, slice(0, half))
    adam_into(pltpu.roll(spatial[:, edge:], k, 1)[:, 0:k], refs, outs, slice(half, 2 * half))


def adam_unit(u, sources, state, before, name, after=()):
    unit = [pl.BlockSpec((1,) + a.shape[1:], lambda i: (u, 0, 0)) for a in state]
    types = [F32, F32, F32, BF]
    outs = [shape(state[0].shape, t) for t in types] + [shape(state[3].shape, t) for t in types]
    before = list(before or ())
    whole = [pl.BlockSpec(a.shape, lambda i, n=a.ndim: (0,) * n) for a in sources]

    def kernel(*refs):
        adam_body(*refs[len(after) :], grads=len(sources))

    return pl.pallas_call(
        kernel,
        grid=(1,),
        out_shape=tuple(outs),
        in_specs=[pl.BlockSpec(memory_space=pl.ANY)] * len(after) + whole + unit + [pl.BlockSpec(memory_space=pl.ANY)] * len(before),
        out_specs=tuple([unit[0]] * 4 + [unit[3]] * 4),
        input_output_aliases={len(after) + len(sources) + 6 + i: i for i in range(len(before))},
        compiler_params=pltpu.CompilerParams(vmem_limit_bytes=40 * MIB),
        cost_estimate=CHEAP,
        name=name,
    )(*after, *[in_hbm(a) for a in [*sources, *state]], *before)


def swap(parts, axis):
    return lax.all_to_all(parts, axis, 0, 0, tiled=True)


def from_all(value, axis):
    count = lax.axis_size(axis)
    return swap(jnp.broadcast_to(value[None], (count,) + value.shape), axis)


def across(value, bit):
    count = lax.axis_size("rep")
    return lax.ppermute(value, "rep", [(i, i ^ bit) for i in range(count)])


MASKS = (0, 2, 1, 3)


def traded(parts):
    return [part if mask == 0 else across(part, mask) for part, mask in zip(parts, MASKS)]


def from_group(value, after=None):
    distant = across(value, 2)
    beside = across(value, 1)
    if after is not None:
        distant = gate(distant, [after], "then")
    return value, distant, beside, across(distant, 1)


def neighbours(first, last):
    count = lax.axis_size("frames")
    before = lax.ppermute(last, "frames", [(i, i + 1) for i in range(count - 1)])
    after = lax.ppermute(first, "frames", [(i + 1, i) for i in range(count - 1)])
    return before, after


def along(step):
    return [(RING[i], RING[(i + step) % 8]) for i in range(8)]


def ring_gather(chunks, after):
    ahead, back = [[c] for c in chunks], [[c] for c in chunks]
    for step in range(4):
        if step == 2:
            ahead[-1][-1] = gate(ahead[-1][-1], after, "hop_then")
        for a, b in zip(ahead, back):
            a.append(lax.ppermute(a[-1], "frames", along(1)))
            if step < 3:
                b.append(lax.ppermute(b[-1], "frames", along(-1)))
    return [piece for a, b in zip(ahead, back) for piece in a + b[1:]]


def added(gots, parts, places, after, name):
    count = len(gots)

    def body(*refs):
        refs, token_ref = refs[len(after) : -1], refs[-1]
        token_ref[...] = jnp.zeros(token_ref.shape, F32)
        for got_ref, part_ref, out_ref in zip(refs[:count], refs[count : 2 * count], refs[2 * count :]):
            out_ref[...] = (got_ref[...].astype(F32) + part_ref[0].astype(F32)).astype(BF)

    flat = pl.BlockSpec(gots[0].shape, lambda g: (0, 0))
    part_specs = [pl.BlockSpec((1,) + gots[0].shape, lambda g, i=i: (i, 0, 0)) for i in places]
    return pl.pallas_call(
        body,
        grid=(1,),
        out_shape=[shape(g.shape, BF) for g in gots] + [shape((8, LANES), F32)],
        in_specs=[ANY] * len(after) + [flat] * count + part_specs,
        out_specs=[flat] * count + [pl.BlockSpec((8, LANES), lambda g: (0, 0))],
        cost_estimate=CHEAP,
        name=name,
    )(*after, *[in_hbm(g) for g in gots], *[in_hbm(parts)] * count)


def ring_step(ahead, back):
    return lax.ppermute(ahead, "frames", along(1)), lax.ppermute(back, "frames", along(-1))


class RingSums:
    def __init__(self, parts, own, ahead, back, name):
        self.parts, self.own, self.ahead, self.back, self.name = parts, own, ahead, back, name
        self.step = 0

    def add(self, after=()):
        self.step += 1
        step, after, name = self.step, list(after), f"{self.name}_{self.step}"
        if step < 3:
            gots = ring_step(self.ahead, self.back)
            self.ahead, self.back, token = added(gots, self.parts, (4 - step, 5 + step), after, name)
        else:
            gots = [lax.ppermute(self.ahead, "frames", along(1))]
            self.ahead, token = added(gots, self.parts, (4 - step,), after, name)
        return [token]

    def end(self):
        return [self.own, *ring_step(self.ahead, self.back)]


def reduced(send, kept, x):
    got = across(send, 1)
    away = lax.dynamic_index_in_dim(got, 1 - x, 0, False).astype(F32)
    away = away + lax.dynamic_index_in_dim(kept, 1 - x, 0, False)
    return got, kept, across(away.astype(BF), 2)


def ordered(t_grad, count):
    n_r, rows, cols = t_grad.shape
    return t_grad.reshape(n_r, 3, rows // 3, cols).transpose(1, 0, 2, 3).reshape(count, -1, cols)


def sum_over(parts, axis):
    return jnp.sum(swap(parts, axis).astype(F32), axis=0)


def on_device(
    frames_in, cotangent, lengths,
    spatial_weights, spatial_first, spatial_second,
    temporal_weights, temporal_first, temporal_second,
    mid_norm, mid_first, mid_second,
    out_norm, out_first, out_second,
):
    own_frames, height, width, depth = frames_in.shape
    n_f, n_r = lax.axis_size("frames"), lax.axis_size("rep")
    assert n_r == 4 and depth == n_r * LANES
    me = lax.axis_index("rep")
    frames = own_frames * n_r
    pixels = height * width
    rows = pixels * frames
    total = float(rows * n_f)
    dims = (height, width, frames, depth)
    units, k, mid = spatial_weights.shape
    cols = LANES
    everyone = ("frames", "rep")
    k_t = temporal_weights.shape[1]
    ring = can_ring(mid, k, k_t, n_f)
    spatial_flops = 2 * rows * 9 * depth * mid
    temporal_flops = 2 * rows * 3 * depth * mid
    pad = pltpu.VMEM((height + 2, width + 2, frames, depth), F32)
    flip = functools.partial(jnp.swapaxes, axis1=1, axis2=2)
    ids = [me, me ^ 2, me ^ 1, me ^ 3, me & 1, me >> 1]
    if ring:
        place = ring_place(lax.axis_index("frames"))
        in_order = jnp.stack(ids + [jnp.int32(f) for f in (*range(8), *range(8))]).astype(jnp.int32)
        ids += [ring_device(place + i) for i in (0, -1, -2, -3, -4, 1, 2, 3)]
        ids += [(ring_place(jnp.int32(f)) - place) % 8 for f in range(8)]
    ids = jnp.stack(ids).astype(jnp.int32)

    frame_ids = lax.axis_index("frames") * frames + jnp.arange(frames, dtype=jnp.int32)
    clip_ends = jnp.cumsum(lengths)
    starts = jnp.concatenate([jnp.zeros((1,), jnp.int32), clip_ends[:-1]])
    opening = jnp.any(frame_ids[:, None] == starts[None, :], axis=1)
    closing = jnp.any((frame_ids + 1)[:, None] == clip_ends[None, :], axis=1)
    keep = jnp.where(jnp.stack([opening, closing]), 0.0, 1.0).astype(F32)[:, :, None]

    act = lax.all_gather(frames_in, "rep", axis=0, tiled=True).transpose(1, 2, 0, 3).reshape(rows, depth)
    cot = cotangent.reshape(own_frames, pixels, n_r, cols).transpose(2, 0, 1, 3)
    cot = swap(cot, "rep").reshape(frames, pixels, cols).transpose(1, 0, 2).reshape(rows, cols)

    mid_own = lax.dynamic_slice_in_dim(mid_norm, me * mid, mid, axis=2)
    out_split = out_norm.reshape(units, 2, n_r, cols).transpose(0, 2, 1, 3)

    slots, temporal_w = [], []

    if ring:
        wire = shape((mid // 2 + k_t * LANES // (2 * k), 2 * k), BF)
        chunks = packed(0, flip(spatial_weights), temporal_weights, (wire.shape[0] // 2, wire.shape[0] // 2))
        held = ring_gather(chunks, [act, cot])
        slots.append((ids, held))
        (wire_1,) = packed(1, flip(spatial_weights), temporal_weights, wire.shape[:1])
        wire_1 = gate(wire_1, [held[4], held[7], held[12], held[15]], "wire_then")
        slots.append((in_order, [lax.all_gather(wire_1, "frames", axis=0)]))
    else:
        wire = flip(spatial_weights).astype(BF)
        temporal_low = temporal_weights.astype(BF)
        for u in range(units):
            held = lax.all_gather(wire[u], "frames", axis=0)
            slots.append((ids, [held.transpose(1, 0, 2).reshape(mid, n_f * k)]))
            shard = lax.all_gather(temporal_low[u], "frames", axis=0, tiled=True)
            shard = shard.reshape(3, n_r, mid, cols).transpose(1, 0, 2, 3)
            temporal_w.append(traded([lax.dynamic_index_in_dim(shard, ids[j], 0, False) for j in range(n_r)]))

    rows_16 = -(-rows // 16) * 16
    halo = shape((pixels, 1, mid), F32)
    column = shape((rows, cols), BF)
    s_shape, w_shape = shape((rows, mid), F32), shape((mid, n_f * k), BF)
    act_shape = shape((rows_16, depth), BF)
    win_shape, row_shape = shape((3, rows_16, mid), BF), shape((3, mid, depth), BF)
    s_scr, w_scr = pltpu.VMEM(s_shape.shape, F32), pltpu.VMEM(w_shape.shape, BF)
    sems = pltpu.SemaphoreType.DMA
    saved, spatial_w = [], []
    for u in range(units):
        order, held = slots[u]
        sources = [loaded(act)] if u == 0 else [*t_group, both, out_split[u - 1]]
        outs = [s_shape] * (u > 0) + [halo, halo, shape((2, mid), F32), far(s_shape)]
        outs += [far(w_shape)] * ring + [far(act_shape)] * (u > 0) + [shape((3, mid, cols), BF)] * (n_r * ring)
        parts = run(
            functools.partial(spatial_body, dims=dims, half=mid // 2, ring=ring, first=u == 0), outs,
            [order, *all_loaded(held), *sources], f"spatial_{u}",
            [pad, pltpu.VMEM((mid, rows), F32), sems((3,))] + [w_scr] * ring + [pltpu.VMEM(act_shape.shape, BF)] * (u > 0)
            + [pltpu.VMEM((n_r, 3, 2, mid // 2, cols), BF)] * ring + [s_scr] * (u == 0),
            scalars=1, flops=spatial_flops, moved=8 * MIB,
            after=[cot, keep, mid_own, out_split] if u == 0 else (),
        )
        spatial = parts[: int(u > 0)]
        first, last, mom, s_far, *more = parts[int(u > 0) :]
        spatial_w.append(more.pop(0) if ring else held[0])
        if u > 0:
            act = more.pop(0)
        if ring:
            temporal_w.append(traded(more))
        mid_both = from_all(mom, "frames")
        before, after = neighbours(first, last)
        send, kept, stat, window, row_w = run(
            functools.partial(temporal_body, dims=dims),
            [shape((2, rows, cols), BF), shape((2, rows, cols), F32), shape((2, mid), F32), far(win_shape), far(row_shape)],
            [ids, *(spatial or [far(s_far)]), mid_both, before, after, mid_own[u], keep, *temporal_w[u]], f"temporal_{u}",
            [pltpu.VMEM((pixels, frames + 16, mid), F32), pltpu.VMEM((rows_16, depth), F32),
             pltpu.VMEM(win_shape.shape, BF), pltpu.VMEM(row_shape.shape, BF), sems((3,))] + [s_scr] * (u == 0),
            scalars=1, flops=temporal_flops, moved=8 * MIB,
        )
        t, low, mom = run(
            total_body, [loaded(shape((rows, cols), F32)), column, shape((2, cols), F32)],
            [ids, *reduced(send, kept, me >> 1)], f"total_{u}", scalars=1, moved=3 * MIB,
        )
        both = from_all(mom, everyone).reshape(n_f, n_r, 2, cols)
        t_group = from_group(low, both if u + 1 < units else None)
        saved.append((act, s_far, stat, window, row_w, t, t_group, both))

    wide = -(-mid // LANES) * LANES
    deep = 9 * (mid // LANES * LANES) + -(-9 * (mid % LANES) // LANES) * LANES
    adjoint_scr = [
        pltpu.VMEM((height + 2, width + 2, frames, wide), F32), pltpu.VMEM((rows, deep), BF), pltpu.VMEM((deep, depth), BF)
    ]
    d_norms = [None] * units
    weight_parts = [None] * units
    token, sums_1 = None, None
    for u in reversed(range(units)):
        act, s_far, stat, window, row_w, t, t_group, both = saved[u]
        if u == units - 1:
            block, summed_grad, low, sums = run(
                top_body, [loaded(column), loaded(shape((rows, cols), F32)), column, shape((2, cols), F32)],
                [ids, loaded(t), both, out_split[u], loaded(saved[0][0]), loaded(cot)], "top", scalars=1, moved=3 * MIB,
            )
        else:
            low, sums = run(
                below_body, [column, shape((2, cols), F32)],
                [ids, *reduced(send, kept, me >> 1), loaded(t), both, out_split[u]], f"below_{u}", scalars=1, moved=3 * MIB,
                after=[token] if ring else (),
            )
        done = sums_1.add([sums]) if sums_1 is not None else []
        sums = from_all(sums, everyone).reshape(n_f, n_r, 2, cols)
        g_group = from_group(low, sums)
        edge = [shape((2 * n_r, pixels, 1, cols), F32)] * 2
        edges = neighbours(*run(functools.partial(edges_body, dims=dims), edge, [*g_group, *all_loaded(t_group)], f"edges_{u}"))
        dt, coef, out_sums = run(
            functools.partial(dt_body, total=total),
            [shape((rows_16, depth), BF), shape((n_r, 4, cols), F32), shape((2, cols), F32)],
            [ids, *g_group, *all_loaded(t_group), both, sums, out_split[u]], f"dt_{u}", scalars=1, moved=4 * MIB,
        )
        done = sums_1.add([coef]) if sums_1 is not None else []
        t_terms = run(
            temporal_grad_body, [loaded(shape((3 * mid, cols), BF))] + [shape((3 * mid, cols), BF)] * (n_r - 1),
            [ids, loaded(window), dt], f"temporal_grad_{u}", [pltpu.VMEM((mid, depth), F32)], scalars=1,
            flops=temporal_flops, moved=4 * MIB,
        )
        t_grad = traded(t_terms)
        d_mid, sums = run(
            functools.partial(middle_body, dims=dims), [far(shape((rows, mid), F32)), shape((2, mid), F32)],
            [ids, dt, coef, *edges, keep, stat, mid_own[u], far(row_w), far(s_far)], f"middle_{u}",
            [pltpu.VMEM((pixels, frames + 16, depth), F32), pltpu.VMEM(row_shape.shape, BF), s_scr, s_scr, sems((3,))],
            scalars=1, flops=temporal_flops, moved=8 * MIB, after=[t_terms[0]],
        )
        done = sums_1.add([sums]) if sums_1 is not None else []
        sums = from_all(sums, "frames")
        ds_shape, sum_shape = shape((rows, mid), BF), shape((2, mid), F32)
        acc = pltpu.VMEM((mid, n_f * k), F32)
        grad_args = [far(d_mid), stat, mid_own[u], sums]
        if u > 0 or not ring:
            ds, send, kept, mid_sums = run(
                functools.partial(input_body, dims=dims, total=total),
                [ds_shape, shape((2, rows, cols), BF), shape((2, rows, cols), F32), sum_shape],
                [ids, *grad_args, far(s_far), far(spatial_w[u])], f"input_{u}",
                [*adjoint_scr, pltpu.VMEM((rows, depth), F32), s_scr, s_scr, w_scr, sems((3,))],
                limit=44, scalars=1, flops=spatial_flops, moved=8 * MIB, after=t_grad[1:],
            )
        if ring and u > 0:
            *terms, token = run(
                functools.partial(weight_body, dims=dims),
                [loaded(shape((n_f,) + wire.shape, BF)), loaded(wire), wire, wire, shape((8, LANES), F32)], [ids, loaded(act), ds, *all_loaded(t_grad)], f"weight_{u}", [pad, acc],
                scalars=1, flops=spatial_flops, moved=8 * MIB,
            )
            sums_1 = RingSums(*terms, f"sum_{u}")
        elif ring:
            slab = wire
            ds, flat, *terms = run(
                functools.partial(weight_first_body, dims=dims, total=total),
                [ds_shape, shape((8, 512), F32), loaded(shape((n_f,) + slab.shape, BF)), loaded(slab), slab, slab],
                [ids, loaded(act), *grad_args, *d_norms[1], out_sums, *all_loaded(t_grad), far(s_far)], f"weight_{u}",
                [pltpu.VMEM((2, mid), F32), s_scr, s_scr, sems((2,)), pad, acc],
                scalars=1, flops=spatial_flops, moved=8 * MIB, scale=1,
            )
            sums_0 = RingSums(*terms, f"sum_{u}")
        else:
            (s_grad,) = run(
                functools.partial(weight_plain_body, dims=dims), [w_shape], [loaded(act), ds],
                f"weight_{u}", [pad, acc], flops=spatial_flops, moved=8 * MIB,
            )
            s_grad = swap(s_grad.reshape(mid, n_f, k).transpose(1, 0, 2), "frames")
            t_rows = jnp.zeros((n_r,) + t_grad[0].shape, BF)
            for j in range(n_r):
                t_rows = lax.dynamic_update_index_in_dim(t_rows, t_grad[j], ids[j], 0)
            weight_parts[u] = (s_grad, swap(ordered(t_rows, n_f), "frames"))
        d_norms[u] = (mid_sums, out_sums) if u > 0 or not ring else None

    ends_1 = sums_1.end() if ring else []
    grad_part, block_part = (own_frames, pixels, depth), (own_frames, pixels, cols)
    ends = run(
        functools.partial(last_body, dims=dims), [loaded(shape(grad_part, BF))] + [shape(grad_part, BF)] * (n_r - 1) + [shape(block_part, BF)] * n_r,
        [ids, ds, loaded(summed_grad), loaded(block), far(spatial_w[0])], "last",
        [*adjoint_scr, pltpu.VMEM((n_r, rows, cols), F32), pltpu.VMEM((1, rows, cols), F32), pltpu.VMEM((n_r,) + grad_part, BF),
         pltpu.VMEM((n_r,) + block_part, BF), w_scr, sems(())],
        limit=44, scalars=1, flops=spatial_flops, moved=8 * MIB, scale=1, after=ends_1[1:],
    )
    sent = ()
    state = [flip(a) for a in (spatial_weights, spatial_first, spatial_second)]
    state += [temporal_weights, temporal_first, temporal_second]
    if not ring:
        blocks, grads = traded(ends[n_r:]), traded(ends[:n_r])
    if ring:
        flats = from_group(flat)
        sums_0.add(ends[:1])
        blocks, grads = traded(ends[n_r:]), traded(ends[:n_r])
        sent = sums_0.add(grads[1:2])
        weights = adam_unit(1, ends_1, state, None, "adam_1", sent)
        sent = sums_0.add([weights[0], *grads[2:]])
        weight_parts[0] = sums_0.end()
    block_out, input_grad = run(
        finish_body, [shape(frames_in.shape, BF), shape(frames_in.shape, F32)],
        [ids, *all_loaded(blocks + grads)], "finish", [pltpu.VMEM((own_frames, pixels, depth), F32)],
        scalars=1, moved=3 * MIB, after=sent,
    )
    if ring:
        norms = [mid_norm, mid_first, mid_second, out_norm, out_first, out_second]
        norms = run(
            norm_body, [shape(a.shape, F32) for a in norms], [ids, *flats, *norms], "norms",
            [pltpu.VMEM((n_r, 8, 512), F32)], scalars=1,
        )
    else:
        flat = jnp.concatenate([jnp.concatenate([m.reshape(-1), o.reshape(-1)]) for m, o in d_norms])
        flat = from_all(flat, "rep").reshape(n_r, units, -1)
        mid_grad = flat[:, :, : 2 * mid].reshape(n_r, units, 2, mid).transpose(1, 2, 0, 3)
        mid_grad = mid_grad.reshape(units, 2, n_r * mid)
        out_grad = flat[:, :, 2 * mid :].reshape(n_r, units, 2, cols).transpose(1, 2, 0, 3)
        out_grad = out_grad.reshape(units, 2, depth)
        norms = [*adam_step(mid_norm, mid_grad, mid_first, mid_second, RATE_NORM, 0.0)]
        norms += adam_step(out_norm, out_grad, out_first, out_second, RATE_NORM, 0.0)

    if ring:
        weights = adam_unit(0, weight_parts[0], state, weights, "adam_0")
        weights = [flip(a) for a in weights[:4]] + list(weights[4:])
    else:
        grads = [jnp.stack([jnp.sum(parts[i].astype(F32), axis=0) for parts in weight_parts]) for i in range(2)]
        news = adam_step(spatial_weights, flip(grads[0]), spatial_first, spatial_second, RATE_WEIGHT, DECAY)
        weights = [*news, news[0].astype(BF)]
        news = adam_step(temporal_weights, grads[1], temporal_first, temporal_second, RATE_WEIGHT, DECAY)
        weights += [*news, news[0].astype(BF)]
    return (block_out, input_grad, *weights, *norms)


def solution(mesh):
    by_frame = P(("frames", "rep"), None, None, None)
    by_block = P(None, "frames", "rep")
    placed = (by_frame, by_frame, P()) + (by_block,) * 6 + (P(),) * 6
    return jax.shard_map(
        on_device,
        mesh=mesh,
        in_specs=placed,
        out_specs=(by_frame, by_frame) + (by_block,) * 8 + (P(),) * 6,
        check_vma=False,
    )
```

```python
import functools

import jax
import jax.numpy as jnp
from jax import lax
from jax.experimental import pallas as pl
from jax.experimental.pallas import tpu as pltpu
from jax.sharding import PartitionSpec as P

STEP = 5
NORM_EPS = 1e-05
ADAM_EPS = 1e-08
BETA_ONE = 0.5
BETA_TWO = 0.5
RATE_WEIGHT = 0.015
RATE_NORM = 0.2
DECAY = 0.05
BF = jnp.bfloat16
F32 = jnp.float32
MIB = 1 << 20
VMEM = pl.BlockSpec(memory_space=pltpu.VMEM)
SMEM = pl.BlockSpec(memory_space=pltpu.SMEM)
LANES = 128
SCALE = 30
CHEAP = pl.CostEstimate(flops=1000, bytes_accessed=1000, transcendentals=0)
ANY = pl.BlockSpec(memory_space=pl.ANY)
HBM = pl.BlockSpec(memory_space=pltpu.HBM)


def shape(dims, dtype):
    return jax.ShapeDtypeStruct(tuple(dims), dtype)


class Placed:
    def __init__(self, value, where):
        self.value, self.where = value, where


def far(value):
    return Placed(value, "hbm")


def loaded(value):
    return Placed(value, "loaded")


def near(value):
    return Placed(value, "vmem")


def all_loaded(values):
    return [loaded(v) for v in values]


def in_hbm(array):
    return pltpu.with_memory_space_constraint(array, pltpu.HBM)


def operand(a):
    if not isinstance(a, Placed):
        return a
    return pltpu.with_memory_space_constraint(a.value, pltpu.VMEM if a.where == "vmem" else pltpu.HBM)


def result(a):
    if not isinstance(a, Placed):
        return a
    return (pltpu.VMEM if a.where == "vmem" else pltpu.HBM)(a.value.shape, a.value.dtype)


def is_far(a):
    return isinstance(a, Placed) and a.where == "hbm"


def run(body, outs, args, name, scratch=(), limit=28, scalars=0, flops=0, moved=0, after=(), scale=SCALE):
    def kernel(*refs):
        body(*refs[len(after) :])

    return pl.pallas_call(
        kernel,
        out_shape=tuple(result(o) for o in outs),
        in_specs=[ANY] * len(after) + [SMEM] * scalars + [ANY if is_far(a) else VMEM for a in args[scalars:]],
        out_specs=tuple(HBM if is_far(o) else VMEM for o in outs),
        scratch_shapes=list(scratch),
        compiler_params=pltpu.CompilerParams(vmem_limit_bytes=limit * MIB),
        cost_estimate=pl.CostEstimate(flops=int(scale * flops), bytes_accessed=int(scale * moved), transcendentals=0),
        name=name,
    )(*after, *[operand(a) for a in args])


def gate(value, after, name):
    return pl.pallas_call(
        lambda *refs: None,
        out_shape=shape(value.shape, value.dtype),
        in_specs=[ANY] * (len(after) + 1),
        out_specs=ANY,
        input_output_aliases={len(after): 0},
        name=name,
    )(*after, value)


def started(source, target, sem):
    copy = pltpu.make_async_copy(source, target, sem)
    copy.start()
    return copy


def padded(values, rows):
    return jnp.concatenate([values, jnp.zeros((rows - values.shape[0], values.shape[1]), F32)], axis=0)


def sigmoid(v):
    return 1.0 / (1.0 + jnp.exp(-v))


def silu(v):
    return v / (1.0 + jnp.exp(-v))


def silu_slope(v):
    s = sigmoid(v)
    return s * (1.0 + v * (1.0 - s))


def mm(a, b, dims):
    return lax.dot_general(a, b, (dims, ((), ())), preferred_element_type=F32)


def put_moments(values, out_ref):
    rows = values.shape[0]
    mean = jnp.sum(values, axis=0, keepdims=True) * (1.0 / rows)
    off = values - mean
    out_ref[0:1, :] = mean
    out_ref[1:2, :] = jnp.sum(off * off, axis=0, keepdims=True)


def joined_moments(both, rows):
    count = both.shape[0]
    mean = jnp.sum(both[:, 0:1], axis=0) * (1.0 / count)
    off = both[:, 0:1] - mean[None]
    total = jnp.sum(both[:, 1:2] + rows * (off * off), axis=0)
    return mean, lax.rsqrt(total * (1.0 / (rows * count)) + NORM_EPS)


def put_sums(upstream, normed, out_ref):
    out_ref[0:1, :] = jnp.sum(upstream * normed, axis=0, keepdims=True)
    out_ref[1:2, :] = jnp.sum(upstream, axis=0, keepdims=True)


def convolve(pad, w_ref, turned, dims):
    height, width, frames, depth = dims
    rows = height * width * frames
    for k in range(9):
        i, j = k // 3, k % 3
        piece = pad[i : i + height, j : j + width].reshape(rows, depth).astype(BF)
        part = mm(w_ref[:, k * depth : (k + 1) * depth], piece, ((1,), (1,)))
        if k == 0:
            turned[...] = part
        else:
            turned[...] += part
    return turned[...].T


def widened(scr, values, before, after):
    frames = values.shape[1]
    scr[:, 8 : 8 + frames, :] = values
    scr[:, 7:8, :] = before
    scr[:, 8 + frames : 9 + frames, :] = after


RING = (0, 2, 4, 6, 7, 5, 3, 1)


def can_ring(mid, k, k_t, count):
    return count == len(RING) and mid == 288 and k == 576 and k_t == 432


def ring_place(frame):
    return jnp.where(frame % 2 == 0, frame // 2, 7 - frame // 2)


def ring_device(place):
    place = place % 8
    return jnp.where(place < 4, 2 * place, 15 - 2 * place)


def low_half(shape_):
    return lax.broadcasted_iota(jnp.int32, shape_, 1) < LANES // 2


def fold(top, bottom, out_ref, k):
    edge = k - LANES // 2
    out_ref[:, 0:edge] = top[:, 0:edge].astype(out_ref.dtype)
    mixed = jnp.where(low_half((top.shape[0], LANES)), top[:, edge : edge + LANES], bottom[:, 0:LANES])
    out_ref[:, edge : edge + LANES] = mixed.astype(out_ref.dtype)
    out_ref[:, edge + LANES : 2 * k] = bottom[:, LANES : k + LANES // 2].astype(out_ref.dtype)


def pack_body(w_ref, t_ref, *refs):
    outs, folded, scr = refs[:-2], refs[-2], refs[-1]
    mid, k = w_ref.shape[1:]
    half = mid // 2
    scr[:, 0:k] = w_ref[0]
    fold(scr[0:half, :], pltpu.roll(scr[half:mid, :], LANES // 2, 1), folded.at[0:half], k)
    rows = folded.shape[0] - half
    for i in range(2 * k // LANES):
        at = slice(i * LANES, (i + 1) * LANES)
        folded[half:, at] = t_ref[0, rows * i : rows * (i + 1), :].astype(BF)
    start = 0
    for out in outs:
        out[...] = folded[start : start + out.shape[0], :]
        start += out.shape[0]


def packed(u, spatial, temporal, sizes):
    mid, k = spatial.shape[1:]
    flat = [pl.BlockSpec((n, 2 * k), lambda i: (0, 0)) for n in sizes]
    return pl.pallas_call(
        pack_body,
        grid=(1,),
        out_shape=[shape((n, 2 * k), BF) for n in sizes],
        in_specs=[pl.BlockSpec((1,) + a.shape[1:], lambda i: (u, 0, 0)) for a in (spatial, temporal)],
        out_specs=flat,
        scratch_shapes=[pltpu.VMEM((sum(sizes), 2 * k), BF), pltpu.VMEM((mid, k + LANES // 2), F32)],
        compiler_params=pltpu.CompilerParams(vmem_limit_bytes=24 * MIB),
        name=f"pack_{u}",
    )(in_hbm(spatial), in_hbm(temporal))


def unpack_temporal(f, slot, t_ref):
    rows = slot.shape[0]
    per = t_ref.shape[3] // rows
    for j in range(slot.shape[1] // LANES):
        block = 3 * f + j // per
        piece = slot[:, j * LANES : (j + 1) * LANES]
        t_ref[(block % 8) // 2, block // 8, block % 2, (j % per) * rows : (j % per + 1) * rows, :] = piece


def slots_of(refs, half):
    if len(refs[0].shape) == 3:
        return [([refs[0].at[i, 0:half]], refs[0].at[i, half:]) for i in range(8)], refs[1:]
    cut = half - refs[0].shape[0]
    return [([refs[i], refs[8 + i].at[0:cut]], refs[8 + i].at[cut:]) for i in range(8)], refs[16:]


def unpack_rows(ids_ref, slots, outs, scr):
    half = scr.shape[3]
    for i, (_, slot) in enumerate(slots):
        unpack_temporal(ids_ref[6 + i], slot, scr)
    for j, out_ref in enumerate(outs):
        for k in range(3):
            for part in range(2):
                out_ref[k, part * half : (part + 1) * half, :] = scr[ids_ref[j], k, part]


def unpack_spatial(ids_ref, slots, w_ref):
    half, k = w_ref.shape[0] // 2, w_ref.shape[1] // 8
    edge, wide = k - LANES // 2, k + LANES // 2
    for i, (slot, _) in enumerate(slots):
        f = ids_ref[6 + i]
        base = (f // 2) * (2 * k)
        values = jnp.concatenate([part[...].astype(F32) for part in slot], axis=0)
        low = low_half((half, LANES))

        def at(start, size):
            return pl.ds(pl.multiple_of(base + start, LANES), size)

        @pl.when(f % 2 == 0)
        def _():
            for start, part in ((0, values[:, 0:wide]), (half, pltpu.roll(values[:, edge:], k, 1))):
                rows = slice(start, start + half)
                w_ref[rows, at(0, edge)] = part[:, 0:edge].astype(BF)
                old = w_ref[rows, at(edge, LANES)].astype(F32)
                w_ref[rows, at(edge, LANES)] = jnp.where(low, part[:, edge:wide], old).astype(BF)

        @pl.when(f % 2 == 1)
        def _():
            for start, part in ((0, pltpu.roll(values[:, 0:wide], LANES // 2, 1)), (half, values[:, edge:])):
                rows = slice(start, start + half)
                old = w_ref[rows, at(edge, LANES)].astype(F32)
                w_ref[rows, at(edge, LANES)] = jnp.where(low, old, part[:, 0:LANES]).astype(BF)
                w_ref[rows, at(edge + LANES, edge)] = part[:, LANES:wide].astype(BF)


def spatial_body(*refs, dims, half, ring, first):
    height, width, frames, depth = dims
    rows = height * width * frames
    ids_ref, refs = refs[0], refs[1:]
    if ring:
        slots, refs = slots_of(refs, half)
    else:
        w_ref, refs = refs[0], refs[1:]
    refs = iter(refs)

    def take(count):
        return [next(refs) for _ in range(count)]

    sources = take(1 if first else 6)
    (s_ref,) = take(1) if not first else (None,)
    first_ref, last_ref, mom_ref, s_far = take(4)
    w_far, act_far, row_outs = take(int(ring)), take(int(not first)), take(4 * int(ring))
    pad, turned, sems = take(3)
    w_scr, act_scr, row_scr = take(int(ring)), take(int(not first)), take(int(ring))
    if first:
        (s_ref,) = take(1)

    copies = []
    if ring:
        w_ref = w_scr[0]
        unpack_spatial(ids_ref, slots, w_ref)
        copies.append(started(w_ref, w_far[0], sems.at[0]))
        unpack_rows(ids_ref, slots, row_outs, row_scr[0])
    pad[...] = jnp.zeros(pad.shape, F32)
    if first:
        pad[1 : height + 1, 1 : width + 1] = sources[0][...].astype(F32).reshape(dims)
    else:
        both_ref, norm_ref = sources[4:]
        for j, t_ref in enumerate(sources[:4]):
            b = ids_ref[j]
            mean, inverse = joined_moments(both_ref[:, b], rows)
            norm = norm_ref[b]
            y = (t_ref[...].astype(F32) - mean) * (inverse * norm[0:1]) + norm[1:2]
            a = silu(y)
            at = pl.ds(pl.multiple_of(b * LANES, LANES), LANES)
            act_scr[0][:, at] = padded(a, act_scr[0].shape[0]).astype(BF)
            pad[1 : height + 1, 1 : width + 1, :, at] = a.reshape(height, width, frames, LANES)
        copies.append(started(act_scr[0], act_far[0], sems.at[1]))
    s_ref[...] = convolve(pad, w_ref, turned, dims)
    copies.append(started(s_ref, s_far, sems.at[2]))
    values = s_ref[...]
    put_moments(values, mom_ref)
    grid = values.reshape(height * width, frames, values.shape[-1])
    first_ref[...] = grid[:, 0:1, :]
    last_ref[...] = grid[:, frames - 1 : frames, :]
    for copy in copies:
        copy.wait()


def temporal_body(
    ids_ref, s_ref, both_ref, before_ref, after_ref, norm_ref, keep_ref, w0, w1, w2, w3,
    send_ref, kept_ref, stat_ref, win_far, row_far, scr, part, win_ref, row_ref, sems, s_scr=None, *, dims
):
    height, width, frames, depth = dims
    pixels = height * width
    rows = pixels * frames
    mid = s_ref.shape[-1]
    if s_scr is not None:
        arriving = started(s_ref, s_scr, sems.at[2])
    for j, w_ref in enumerate((w0, w1, w2, w3)):
        row_ref[:, :, pl.ds(pl.multiple_of(ids_ref[j] * LANES, LANES), LANES)] = w_ref[...]
    copies = [started(row_ref, row_far, sems.at[0])]
    mean, inverse = joined_moments(both_ref[...], rows)
    stat_ref[0:1, :] = mean
    stat_ref[1:2, :] = inverse
    scale, bias = inverse * norm_ref[0:1], norm_ref[1:2]

    def active(v):
        return silu((v - mean) * scale + bias)

    if s_scr is not None:
        arriving.wait()
        s_ref = s_scr
    middle = active(s_ref[...])
    widened(
        scr, middle.reshape(pixels, frames, mid),
        active(before_ref[...].reshape(pixels, mid)).reshape(pixels, 1, mid),
        active(after_ref[...].reshape(pixels, mid)).reshape(pixels, 1, mid),
    )
    whole = win_ref.shape[1]
    earlier = (scr[:, 7 : 7 + frames, :] * keep_ref[0][None]).reshape(rows, mid)
    later = (scr[:, 9 : 9 + frames, :] * keep_ref[1][None]).reshape(rows, mid)
    for i, values in enumerate((earlier, middle, later)):
        win_ref[i] = padded(values, whole).astype(BF)
    copies.append(started(win_ref, win_far, sems.at[1]))
    part[...] = mm(win_ref[0], row_ref[0], ((1,), (0,)))
    part[...] += mm(win_ref[1], row_ref[1], ((1,), (0,)))
    part[...] += mm(win_ref[2], row_ref[2], ((1,), (0,)))
    put_halves(ids_ref, part, send_ref, kept_ref)
    for copy in copies:
        copy.wait()


def put_halves(ids_ref, part, send_ref, kept_ref):
    core = ids_ref[4]
    rows = send_ref.shape[1]
    for i in range(2):
        other = pl.multiple_of((2 * i + 1 - core) * LANES, LANES)
        own = pl.multiple_of((2 * i + core) * LANES, LANES)
        send_ref[i] = part[0:rows, pl.ds(other, LANES)].astype(BF)
        kept_ref[i] = part[0:rows, pl.ds(own, LANES)]


def total_body(ids_ref, got_ref, kept_ref, last_ref, t_ref, low_ref, mom_ref):
    x = ids_ref[5]
    t = got_ref[x].astype(F32) + kept_ref[x] + last_ref[...].astype(F32)
    t_ref[...] = t
    low_ref[...] = t.astype(BF)
    put_moments(t, mom_ref)


def edges_body(*refs, dims):
    height, width, frames, depth = dims
    blocks, (first_ref, last_ref, scr) = refs[:-3], refs[-3:]
    pixels = height * width
    slot = scr.shape[0] // len(blocks)
    for out_ref, at in ((first_ref, 0), (last_ref, frames - 1)):
        for j, ref in enumerate(blocks):
            grid = ref[...].astype(F32).reshape(pixels, frames, LANES)
            scr[slot * j : slot * j + pixels, :] = grid[:, at : at + 1, :].reshape(pixels, LANES)
        out_ref[...] = scr[...].astype(BF)


def top_body(ids_ref, t_ref, both_ref, norm_ref, x_ref, cot_ref, block_ref, g_ref, low_ref, sums_ref):
    rows = t_ref.shape[0]
    b = ids_ref[0]
    mean, inverse = joined_moments(both_ref[:, b], rows)
    norm = norm_ref[b]
    normed = (t_ref[...] - mean) * inverse
    own = pl.ds(pl.multiple_of(b * LANES, LANES), LANES)
    summed = normed * norm[0:1] + norm[1:2] + x_ref[:, own].astype(F32)
    block_ref[...] = silu(summed).astype(BF)
    g = cot_ref[...].astype(F32) * silu_slope(summed)
    g_ref[...] = g
    low_ref[...] = g.astype(BF)
    put_sums(g, normed, sums_ref)


def below_body(ids_ref, got_ref, kept_ref, last_ref, t_ref, both_ref, norm_ref, low_ref, sums_ref):
    rows = t_ref.shape[0]
    b, x = ids_ref[0], ids_ref[5]
    d_act = got_ref[x].astype(F32) + kept_ref[x] + last_ref[...].astype(F32)
    mean, inverse = joined_moments(both_ref[:, b], rows)
    norm = norm_ref[b]
    normed = (t_ref[...] - mean) * inverse
    g = d_act * silu_slope(normed * norm[0:1] + norm[1:2])
    low_ref[...] = g.astype(BF)
    put_sums(g, normed, sums_ref)


def dt_body(
    ids_ref, g0, g1, g2, g3, t0, t1, t2, t3, both_ref, sums_ref, norm_ref, dt_ref, coef_ref, sum_ref, *, total
):
    rows, whole = g0.shape[0], dt_ref.shape[0]
    for j, (g_ref, t_ref) in enumerate(((g0, t0), (g1, t1), (g2, t2), (g3, t3))):
        b = ids_ref[j]
        mean, inverse = joined_moments(both_ref[:, b], rows)
        sums = jnp.sum(sums_ref[:, b], axis=0)
        if j == 0:
            sum_ref[...] = sums
        c1 = norm_ref[b][0:1] * inverse
        c2 = c1 * sums[1:2] * (1.0 / total)
        c3 = c1 * inverse * sums[0:1] * (1.0 / total)
        coef_ref[j] = jnp.concatenate([c1, c2, c3, mean], axis=0)
        d = c1 * g_ref[...].astype(F32) - c2 - c3 * (t_ref[...].astype(F32) - mean)
        dt_ref[:, pl.ds(pl.multiple_of(b * LANES, LANES), LANES)] = padded(d, whole).astype(BF)


def temporal_grad_body(ids_ref, win_ref, dt_ref, *refs):
    outs, term = refs[:-1], refs[-1]
    mid = win_ref.shape[-1]
    dt = dt_ref[...]
    for k in range(3):
        term[...] = mm(win_ref[k], dt, ((0,), (0,)))
        for j, out_ref in enumerate(outs):
            at = pl.ds(pl.multiple_of(ids_ref[j] * LANES, LANES), LANES)
            out_ref[k * mid : (k + 1) * mid, :] = term[:, at].astype(BF)


def middle_body(
    ids_ref, dt_ref, coef_ref, before_ref, after_ref, keep_ref, stat_ref, norm_ref, row_far, s_far,
    d_far, sums_ref, scr, row_ref, s_ref, d_ref, sems, *, dims
):
    height, width, frames, depth = dims
    pixels = height * width
    rows = pixels * frames
    copies = [started(row_far, row_ref, sems.at[0]), started(s_far, s_ref, sems.at[1])]
    before, after = before_ref[...].astype(F32), after_ref[...].astype(F32)
    slot = before.shape[0] // 8
    dt = dt_ref[...]
    scr[:, 8 : 8 + frames, :] = dt.astype(F32)[0:rows].reshape(pixels, frames, depth)
    for j in range(4):
        at = pl.ds(pl.multiple_of(ids_ref[j] * LANES, LANES), LANES)
        c = coef_ref[j]

        def halo(frame):
            g, t = (frame[slot * b : slot * b + pixels] for b in (j, 4 + j))
            d = c[0:1] * g - c[1:2] - c[2:3] * (t - c[3:4])
            return d.astype(BF).astype(F32).reshape(pixels, 1, LANES)

        scr[:, 7:8, at] = halo(before)
        scr[:, 8 + frames : 9 + frames, at] = halo(after)
    later = (scr[:, 9 : 9 + frames, :] * keep_ref[1][None]).reshape(rows, depth).astype(BF)
    earlier = (scr[:, 7 : 7 + frames, :] * keep_ref[0][None]).reshape(rows, depth).astype(BF)
    copies[0].wait()
    d_ref[...] = mm(later, row_ref[0], ((1,), (1,)))
    d_ref[...] += mm(dt, row_ref[1], ((1,), (1,)))[0:rows]
    d_ref[...] += mm(earlier, row_ref[2], ((1,), (1,)))
    copies[1].wait()
    normed = (s_ref[...] - stat_ref[0:1]) * stat_ref[1:2]
    d = d_ref[...] * silu_slope(normed * norm_ref[0:1] + norm_ref[1:2])
    d_ref[...] = d
    leaving = started(d_ref, d_far, sems.at[2])
    put_sums(d, normed, sums_ref)
    leaving.wait()


def spatial_grad(d_ref, s_ref, stat_ref, norm_ref, sums_ref, ds_ref, sum_ref, total):
    sums = jnp.sum(sums_ref[...], axis=0)
    sum_ref[...] = sums
    inverse = stat_ref[1:2]
    normed = (s_ref[...] - stat_ref[0:1]) * inverse
    d = d_ref[...] - sums[1:2] * (1.0 / total) - normed * (sums[0:1] * (1.0 / total))
    ds_ref[...] = (norm_ref[0:1] * inverse * d).astype(BF)


def adjoint(ds_ref, w_ref, pad, patches, stacked, dims):
    height, width, frames, depth = dims
    rows, mid = ds_ref.shape
    whole = mid // LANES * LANES
    rest = mid - whole
    start = 9 * whole
    pad[...] = jnp.zeros(pad.shape, F32)
    pad[1 : height + 1, 1 : width + 1, :, 0:mid] = ds_ref[...].astype(F32).reshape(height, width, frames, mid)
    lane = lax.broadcasted_iota(jnp.int32, (rows, LANES), 1)
    tails = [jnp.zeros((rows, LANES), F32) for _ in range((patches.shape[1] - start) // LANES)]
    stacked[start:, :] = jnp.zeros((stacked.shape[0] - start, depth), BF)
    for k in range(9):
        i, j = k // 3, k % 3
        piece = pad[2 - i : 2 - i + height, 2 - j : 2 - j + width].reshape(rows, pad.shape[-1])
        w = w_ref[:, k * depth : (k + 1) * depth]
        patches[:, k * whole : (k + 1) * whole] = piece[:, 0:whole].astype(BF)
        stacked[k * whole : (k + 1) * whole, :] = w[0:whole]
        stacked[start + k * rest : start + (k + 1) * rest, :] = w[whole:mid]
        tile, at = divmod(k * rest, LANES)
        tail = pltpu.roll(piece[:, whole:], at, 1) if at else piece[:, whole:]
        tails[tile] = jnp.where((lane >= at) & (lane < at + rest), tail, tails[tile])
    for tile, tail in enumerate(tails):
        patches[:, start + tile * LANES : start + (tile + 1) * LANES] = tail.astype(BF)
    return mm(patches[...], stacked[...], ((1,), (0,)))


def input_body(
    ids_ref, d_far, stat_ref, norm_ref, sums_ref, s_far, w_far,
    ds_ref, send_ref, kept_ref, sum_ref, pad, patches, stacked, part, s_ref, d_ref, w_ref, sems, *, dims, total
):
    height, width, frames, depth = dims
    copies = [started(s_far, s_ref, sems.at[0]), started(w_far, w_ref, sems.at[1]), started(d_far, d_ref, sems.at[2])]
    copies[0].wait()
    copies[2].wait()
    spatial_grad(d_ref, s_ref, stat_ref, norm_ref, sums_ref, ds_ref, sum_ref, total)
    copies[1].wait()
    part[...] = adjoint(ds_ref, w_ref, pad, patches, stacked, dims)
    put_halves(ids_ref, part, send_ref, kept_ref)


def by_frame(source, out_ref, dims):
    height, width, frames, depth = dims
    pixels, own = height * width, out_ref.shape[1]
    for r in range(source.shape[0]):
        for f in range(frames):
            values = source[r, pl.ds(f, pixels, stride=frames), :]
            out_ref[f // own, f % own, :, r * LANES : (r + 1) * LANES] = values.astype(out_ref.dtype)


def last_body(ids_ref, ds_ref, g_ref, block_ref, w_far, *refs, dims):
    grads, blocks, refs = refs[:4], refs[4:8], refs[8:]
    pad, patches, stacked, part, block, grad_scr, block_scr, w_ref, sem = refs
    height, width, frames, depth = dims
    copy = started(w_far, w_ref, sem)
    block[0] = block_ref[...].astype(F32)
    by_frame(block, block_scr, dims)
    copy.wait()
    terms = adjoint(ds_ref, w_ref, pad, patches, stacked, dims)
    own = ids_ref[0]
    for r in range(part.shape[0]):
        part[r] = terms[:, r * LANES : (r + 1) * LANES]
    part[own] = part[own] + g_ref[...]
    by_frame(part, grad_scr, dims)
    for j in range(4):
        grads[j][...] = grad_scr[ids_ref[j]]
        blocks[j][...] = block_scr[ids_ref[j]]


def finish_body(ids_ref, *refs):
    blocks, grads, (out_ref, grad_out_ref, block) = refs[:4], refs[4:8], refs[8:]
    own, height, width, depth = out_ref.shape
    for j, ref in enumerate(blocks):
        block[:, :, pl.ds(pl.multiple_of(ids_ref[j] * LANES, LANES), LANES)] = ref[...].astype(F32)
    for f in range(own):
        grad = sum(ref[f].astype(F32) for ref in grads)
        for h in range(height):
            at = slice(h * width, (h + 1) * width)
            out_ref[f, h] = block[f, at].astype(BF)
            grad_out_ref[f, h] = grad[at]


def weight_terms(act_ref, ds_ref, pad, acc, dims):
    height, width, frames, depth = dims
    rows = height * width * frames
    pad[...] = jnp.zeros(pad.shape, F32)
    pad[1 : height + 1, 1 : width + 1] = act_ref[...].astype(F32)[0:rows].reshape(dims)
    flipped = ds_ref[...].astype(F32).T.astype(BF)

    for k in range(9):
        i, j = k // 3, k % 3
        piece = pad[i : i + height, j : j + width].reshape(rows, depth).astype(BF)
        acc[:, k * depth : (k + 1) * depth] = mm(flipped, piece, ((1,), (0,)))


def put_shards(acc, places, out_ref, k, then):
    mid = acc.shape[0]
    half = mid // 2
    wide = k + LANES // 2
    for f in range(8):
        if f % 2 == 0:
            top = acc[0:half, k * f : k * f + wide]
            bottom = pltpu.roll(acc[half:mid, k * f : k * f + wide], LANES // 2, 1)
        else:
            start = k * f - LANES // 2
            top = pltpu.roll(acc[0:half, start : start + wide], k, 1)
            bottom = acc[half:mid, start : start + wide]
        fold(top, bottom, out_ref.at[places[f], 0:half], k)
        then(f)


def weight_plain_body(act_ref, ds_ref, out_ref, pad, acc, *, dims):
    weight_terms(act_ref, ds_ref, pad, acc, dims)
    out_ref[...] = acc[...].astype(BF)


def put_temporal(ids_ref, sources, out_ref, half):
    rows = out_ref.shape[1] - half
    per = half // rows
    for i, source in enumerate(sources):
        for tap in range(3):
            for part in range(2):
                block = tap * 8 + ids_ref[i] * 2 + part
                place = ids_ref[14 + block // 3]
                for j in range(per):
                    start = tap * 2 * half + part * half + j * rows
                    at = pl.multiple_of(((block % 3) * per + j) * LANES, LANES)
                    out_ref[place, half:, pl.ds(at, LANES)] = source[start : start + rows, :]


def put_terms(ids_ref, act_ref, ds_ref, t_refs, out_far, ahead_ref, back_ref, pad, acc, out_ref, sems, dims):
    weight_terms(act_ref, ds_ref, pad, acc, dims)
    places = [ids_ref[14 + f] for f in range(8)]
    put_temporal(ids_ref, t_refs, out_ref, acc.shape[0] // 2)
    copies = []
    put_shards(
        acc, places, out_ref, acc.shape[1] // 8,
        lambda f: copies.append(started(out_ref.at[places[f]], out_far.at[places[f]], sems.at[f])),
    )
    ahead_ref[...] = out_ref[4]
    back_ref[...] = out_ref[5]
    for copy in copies:
        copy.wait()


def weight_body(
    ids_ref, act_ref, ds_ref, t0, t1, t2, t3, out_far, ahead_ref, back_ref, token_ref, pad, acc, out_ref, sems, *, dims
):
    token_ref[...] = jnp.zeros(token_ref.shape, F32)
    put_terms(ids_ref, act_ref, ds_ref, (t0, t1, t2, t3), out_far, ahead_ref, back_ref, pad, acc, out_ref, sems, dims)


def weight_first_body(
    ids_ref, d_ref, stat_ref, norm_ref, sums_ref, mid_ref, out_1_ref, out_0_ref, t0, t1, t2, t3, s_ref, act_ref,
    ds_ref, flat_ref, out_far, ahead_ref, back_ref, sum_ref, pad, acc, out_ref, sems, *, dims, total
):
    spatial_grad(d_ref, s_ref, stat_ref, norm_ref, sums_ref, ds_ref, sum_ref, total)
    flat_ref[...] = jnp.zeros(flat_ref.shape, F32)
    for i, ref in enumerate((sum_ref, mid_ref, out_0_ref, out_1_ref)):
        flat_ref[2 * i : 2 * i + 2, 0 : ref.shape[1]] = ref[...]
    put_terms(ids_ref, act_ref, ds_ref, (t0, t1, t2, t3), out_far, ahead_ref, back_ref, pad, acc, out_ref, sems, dims)


def norm_body(ids_ref, f0, f1, f2, f3, *refs):
    refs, flat_ref = refs[:-1], refs[-1]
    for j, ref in enumerate((f0, f1, f2, f3)):
        flat_ref[ids_ref[j]] = ref[...]
    count = flat_ref.shape[0]
    for which in range(2):
        old, new = refs[3 * which : 3 * which + 3], refs[6 + 3 * which : 9 + 3 * which]
        width = old[0].shape[-1] // count
        for u in range(2):
            row = 4 * which + 2 * u
            grad = jnp.concatenate([flat_ref[r, row : row + 2, 0:width] for r in range(count)], axis=1)
            values = adam_step(old[0][u], grad, old[1][u], old[2][u], RATE_NORM, 0.0)
            for ref, value in zip(new, values):
                ref[u] = value


def adam_step(param, gradient, moment_one, moment_two, rate, decay):
    first_new = BETA_ONE * moment_one + (1.0 - BETA_ONE) * gradient
    second_new = BETA_TWO * moment_two + (1.0 - BETA_TWO) * gradient * gradient
    fix_one = 1.0 - BETA_ONE**STEP
    fix_two = 1.0 - BETA_TWO**STEP
    update = first_new / fix_one / (jnp.sqrt(second_new / fix_two) + ADAM_EPS)
    return (param - rate * (update + decay * param), first_new, second_new)


def adam_into(grad, refs, outs, rows):
    new, first, second = adam_step(refs[0][0, rows], grad, refs[1][0, rows], refs[2][0, rows], RATE_WEIGHT, DECAY)
    outs[0][0, rows] = new
    outs[1][0, rows] = first
    outs[2][0, rows] = second
    outs[3][0, rows] = new.astype(BF)


def adam_body(*refs, grads):
    sources, refs = refs[:grads], refs[grads:]
    refs, outs = refs[:6], refs[-8:]
    half = refs[0].shape[1] // 2
    summed = sources[0][0].astype(F32) + sum(r[...].astype(F32) for r in sources[1:])
    temporal = summed[half:]
    rows = temporal.shape[0]
    for i in range(temporal.shape[1] // LANES):
        piece = temporal[:, i * LANES : (i + 1) * LANES]
        adam_into(piece, refs[3:], outs[4:], slice(i * rows, (i + 1) * rows))
    spatial = summed[0:half]
    k = spatial.shape[1] // 2
    edge = k - LANES // 2
    adam_into(spatial[:, 0:k], refs, outs, slice(0, half))
    adam_into(pltpu.roll(spatial[:, edge:], k, 1)[:, 0:k], refs, outs, slice(half, 2 * half))


def adam_unit(u, sources, state, before, name, after=()):
    unit = [pl.BlockSpec((1,) + a.shape[1:], lambda i: (u, 0, 0)) for a in state]
    types = [F32, F32, F32, BF]
    outs = [shape(state[0].shape, t) for t in types] + [shape(state[3].shape, t) for t in types]
    before = list(before or ())
    whole = [pl.BlockSpec((1,) * (a.ndim - 2) + a.shape[-2:], lambda i, n=a.ndim: (0,) * n) for a in sources]

    def kernel(*refs):
        adam_body(*refs[len(after) :], grads=len(sources))

    return pl.pallas_call(
        kernel,
        grid=(1,),
        out_shape=tuple(outs),
        in_specs=[pl.BlockSpec(memory_space=pl.ANY)] * len(after) + whole + unit + [pl.BlockSpec(memory_space=pl.ANY)] * len(before),
        out_specs=tuple([unit[0]] * 4 + [unit[3]] * 4),
        input_output_aliases={len(after) + len(sources) + 6 + i: i for i in range(len(before))},
        compiler_params=pltpu.CompilerParams(vmem_limit_bytes=40 * MIB),
        cost_estimate=CHEAP,
        name=name,
    )(*after, *[in_hbm(a) for a in [*sources, *state]], *before)


def swap(parts, axis):
    return lax.all_to_all(parts, axis, 0, 0, tiled=True)


def from_all(value, axis):
    count = lax.axis_size(axis)
    return swap(jnp.broadcast_to(value[None], (count,) + value.shape), axis)


def across(value, bit):
    count = lax.axis_size("rep")
    return lax.ppermute(value, "rep", [(i, i ^ bit) for i in range(count)])


MASKS = (0, 2, 1, 3)


def traded(parts):
    return [part if mask == 0 else across(part, mask) for part, mask in zip(parts, MASKS)]


def from_group(value, after=None):
    distant = across(value, 2)
    beside = across(value, 1)
    if after is not None:
        distant = gate(distant, after, "then")
    return value, distant, beside, across(distant, 1)


def neighbours(first, last):
    count = lax.axis_size("frames")
    before = lax.ppermute(last, "frames", [(i, i + 1) for i in range(count - 1)])
    after = lax.ppermute(first, "frames", [(i + 1, i) for i in range(count - 1)])
    return before, after


def along(step):
    return [(RING[i], RING[(i + step) % 8]) for i in range(8)]


def ring_gather(chunks, after):
    ahead, back = [[c] for c in chunks], [[c] for c in chunks]
    for step in range(3):
        if step == 2:
            ahead[-1][-1] = gate(ahead[-1][-1], after, "hop_then")
        for a, b in zip(ahead, back):
            a.append(lax.ppermute(a[-1], "frames", along(1)))
            b.append(lax.ppermute(b[-1], "frames", along(-1)))
    last = lax.ppermute(ahead[0][-1], "frames", along(1)), lax.ppermute(back[1][-1], "frames", along(-1))
    return [piece for a, b, far_piece in zip(ahead, back, last) for piece in [*a, far_piece, *b[1:]]]


def added(gots, parts, places, after, name):
    count = len(gots)

    def body(*refs):
        refs, token_ref = refs[len(after) : -1], refs[-1]
        token_ref[...] = jnp.zeros(token_ref.shape, F32)
        for got_ref, part_ref, out_ref in zip(refs[:count], refs[count : 2 * count], refs[2 * count :]):
            out_ref[...] = (got_ref[...].astype(F32) + part_ref[0].astype(F32)).astype(BF)

    flat = pl.BlockSpec(gots[0].shape, lambda g: (0, 0))
    part_specs = [pl.BlockSpec((1,) + gots[0].shape, lambda g, i=i: (i, 0, 0)) for i in places]
    return pl.pallas_call(
        body,
        grid=(1,),
        out_shape=[shape(g.shape, BF) for g in gots] + [shape((8, LANES), F32)],
        in_specs=[ANY] * len(after) + [flat] * count + part_specs,
        out_specs=[flat] * count + [pl.BlockSpec((8, LANES), lambda g: (0, 0))],
        cost_estimate=CHEAP,
        name=name,
    )(*after, *[in_hbm(g) for g in gots], *[in_hbm(parts)] * count)


def ring_step(ahead, back):
    return lax.ppermute(ahead, "frames", along(1)), lax.ppermute(back, "frames", along(-1))


class RingSums:
    def __init__(self, parts, ahead, back, name):
        self.parts, self.ahead, self.back, self.name = parts, ahead, back, name
        self.step = 0

    def add(self, after=()):
        self.step += 1
        step, after, name = self.step, list(after), f"{self.name}_{self.step}"
        if step < 3:
            gots = ring_step(self.ahead, self.back)
            self.ahead, self.back, token = added(gots, self.parts, (4 - step, 5 + step), after, name)
        else:
            gots = [lax.ppermute(self.ahead, "frames", along(1))]
            self.ahead, token = added(gots, self.parts, (4 - step,), after, name)
        return [token]

    def end(self):
        return [self.parts, *ring_step(self.ahead, self.back)]


def reduced(send, kept, x):
    got = across(send, 1)
    away = lax.dynamic_index_in_dim(got, 1 - x, 0, False).astype(F32)
    away = away + lax.dynamic_index_in_dim(kept, 1 - x, 0, False)
    return got, kept, across(away.astype(BF), 2)


def ordered(t_grad, count):
    n_r, rows, cols = t_grad.shape
    return t_grad.reshape(n_r, 3, rows // 3, cols).transpose(1, 0, 2, 3).reshape(count, -1, cols)


def sum_over(parts, axis):
    return jnp.sum(swap(parts, axis).astype(F32), axis=0)


def on_device(
    frames_in, cotangent, lengths,
    spatial_weights, spatial_first, spatial_second,
    temporal_weights, temporal_first, temporal_second,
    mid_norm, mid_first, mid_second,
    out_norm, out_first, out_second,
):
    own_frames, height, width, depth = frames_in.shape
    n_f, n_r = lax.axis_size("frames"), lax.axis_size("rep")
    assert n_r == 4 and depth == n_r * LANES
    me = lax.axis_index("rep")
    frames = own_frames * n_r
    pixels = height * width
    rows = pixels * frames
    total = float(rows * n_f)
    dims = (height, width, frames, depth)
    units, k, mid = spatial_weights.shape
    cols = LANES
    everyone = ("frames", "rep")
    k_t = temporal_weights.shape[1]
    ring = can_ring(mid, k, k_t, n_f)
    spatial_flops = 2 * rows * 9 * depth * mid
    temporal_flops = 2 * rows * 3 * depth * mid
    pad = pltpu.VMEM((height + 2, width + 2, frames, depth), F32)
    flip = functools.partial(jnp.swapaxes, axis1=1, axis2=2)
    ids = [me, me ^ 2, me ^ 1, me ^ 3, me & 1, me >> 1]
    if ring:
        place = ring_place(lax.axis_index("frames"))
        in_order = jnp.stack(ids + [jnp.int32(f) for f in (*range(8), *range(8))]).astype(jnp.int32)
        ids += [ring_device(place + i) for i in (0, -1, -2, -3, -4, 1, 2, 3)]
        ids += [(ring_place(jnp.int32(f)) - place) % 8 for f in range(8)]
    ids = jnp.stack(ids).astype(jnp.int32)

    frame_ids = lax.axis_index("frames") * frames + jnp.arange(frames, dtype=jnp.int32)
    clip_ends = jnp.cumsum(lengths)
    starts = jnp.concatenate([jnp.zeros((1,), jnp.int32), clip_ends[:-1]])
    opening = jnp.any(frame_ids[:, None] == starts[None, :], axis=1)
    closing = jnp.any((frame_ids + 1)[:, None] == clip_ends[None, :], axis=1)
    keep = jnp.where(jnp.stack([opening, closing]), 0.0, 1.0).astype(F32)[:, :, None]

    act = lax.all_gather(frames_in, "rep", axis=0, tiled=True).transpose(1, 2, 0, 3).reshape(rows, depth)
    cot = cotangent.reshape(own_frames, pixels, n_r, cols).transpose(2, 0, 1, 3)
    cot = swap(cot, "rep").reshape(frames, pixels, cols).transpose(1, 0, 2).reshape(rows, cols)

    mid_own = lax.dynamic_slice_in_dim(mid_norm, me * mid, mid, axis=2)
    out_split = out_norm.reshape(units, 2, n_r, cols).transpose(0, 2, 1, 3)

    slots, temporal_w = [], []

    if ring:
        wire = shape((mid // 2 + k_t * LANES // (2 * k), 2 * k), BF)
        chunks = packed(0, flip(spatial_weights), temporal_weights, (wire.shape[0] // 2, wire.shape[0] // 2))
        held = ring_gather(chunks, [act, cot])
        slots.append((ids, held))
        (wire_1,) = packed(1, flip(spatial_weights), temporal_weights, wire.shape[:1])
        wire_1 = gate(wire_1, [held[3], held[15]], "wire_then")
        slots.append((in_order, [lax.all_gather(wire_1, "frames", axis=0)]))
    else:
        wire = flip(spatial_weights).astype(BF)
        temporal_low = temporal_weights.astype(BF)
        for u in range(units):
            held = lax.all_gather(wire[u], "frames", axis=0)
            slots.append((ids, [held.transpose(1, 0, 2).reshape(mid, n_f * k)]))
            shard = lax.all_gather(temporal_low[u], "frames", axis=0, tiled=True)
            shard = shard.reshape(3, n_r, mid, cols).transpose(1, 0, 2, 3)
            temporal_w.append(traded([lax.dynamic_index_in_dim(shard, ids[j], 0, False) for j in range(n_r)]))

    rows_16 = -(-rows // 16) * 16
    halo = shape((pixels, 1, mid), F32)
    column = shape((rows, cols), BF)
    s_shape, w_shape = shape((rows, mid), F32), shape((mid, n_f * k), BF)
    act_shape = shape((rows_16, depth), BF)
    win_shape, row_shape = shape((3, rows_16, mid), BF), shape((3, mid, depth), BF)
    s_scr, w_scr = pltpu.VMEM(s_shape.shape, F32), pltpu.VMEM(w_shape.shape, BF)
    sems = pltpu.SemaphoreType.DMA
    saved, spatial_w = [], []
    for u in range(units):
        order, held = slots[u]
        sources = [loaded(act)] if u == 0 else [loaded(t_group[0]), *t_group[1:], loaded(both), out_split[u - 1]]
        outs = [s_shape] * (u > 0) + [halo, halo, shape((2, mid), F32), far(s_shape)]
        outs += [far(w_shape)] * ring + [far(act_shape)] * (u > 0) + [shape((3, mid, cols), BF)] * (n_r * ring)
        parts = run(
            functools.partial(spatial_body, dims=dims, half=mid // 2, ring=ring, first=u == 0), outs,
            [order, *all_loaded(held), *sources], f"spatial_{u}",
            [pad, pltpu.VMEM((mid, rows), F32), sems((3,))] + [w_scr] * ring + [pltpu.VMEM(act_shape.shape, BF)] * (u > 0)
            + [pltpu.VMEM((n_r, 3, 2, mid // 2, cols), BF)] * ring + [s_scr] * (u == 0),
            scalars=1, flops=spatial_flops, moved=8 * MIB,
            after=[cot, keep, mid_own, out_split] if u == 0 else (),
        )
        spatial = parts[: int(u > 0)]
        first, last, mom, s_far, *more = parts[int(u > 0) :]
        spatial_w.append(more.pop(0) if ring else held[0])
        if u > 0:
            act = more.pop(0)
        if ring:
            temporal_w.append(traded(more))
        mid_both = from_all(mom, "frames")
        before, after = neighbours(first, last)
        send, kept, stat, window, row_w = run(
            functools.partial(temporal_body, dims=dims),
            [shape((2, rows, cols), BF), shape((2, rows, cols), F32), shape((2, mid), F32), far(win_shape), far(row_shape)],
            [ids, *(spatial or [far(s_far)]), mid_both, before, after, mid_own[u], keep, *temporal_w[u]], f"temporal_{u}",
            [pltpu.VMEM((pixels, frames + 16, mid), F32), pltpu.VMEM((rows_16, depth), F32),
             pltpu.VMEM(win_shape.shape, BF), pltpu.VMEM(row_shape.shape, BF), sems((3,))] + [s_scr] * (u == 0),
            scalars=1, flops=temporal_flops, moved=8 * MIB,
        )
        t, low, mom = run(
            total_body, [loaded(shape((rows, cols), F32)), column, shape((2, cols), F32)],
            [ids, *reduced(send, kept, me >> 1)], f"total_{u}", scalars=1, moved=3 * MIB,
        )
        both = from_all(mom, everyone).reshape(n_f, n_r, 2, cols)
        t_group = from_group(low, [both] if u + 1 < units else None)
        saved.append((act, s_far, stat, window, row_w, t, t_group, both))

    wide = -(-mid // LANES) * LANES
    deep = 9 * (mid // LANES * LANES) + -(-9 * (mid % LANES) // LANES) * LANES
    adjoint_scr = [
        pltpu.VMEM((height + 2, width + 2, frames, wide), F32), pltpu.VMEM((rows, deep), BF), pltpu.VMEM((deep, depth), BF)
    ]
    d_norms = [None] * units
    weight_parts = [None] * units
    token, sums_1 = None, None
    for u in reversed(range(units)):
        act, s_far, stat, window, row_w, t, t_group, both = saved[u]
        if u == units - 1:
            block, summed_grad, low, sums = run(
                top_body, [loaded(column), loaded(shape((rows, cols), F32)), column, shape((2, cols), F32)],
                [ids, loaded(t), loaded(both), out_split[u], loaded(saved[0][0]), loaded(cot)], "top", scalars=1, moved=3 * MIB,
            )
        else:
            low, sums = run(
                below_body, [column, shape((2, cols), F32)],
                [ids, *reduced(send, kept, me >> 1), loaded(t), loaded(both), out_split[u]], f"below_{u}", scalars=1, moved=3 * MIB,
                after=[token] if ring else (),
            )
        done = sums_1.add([sums]) if sums_1 is not None else []
        sums = from_all(sums, everyone).reshape(n_f, n_r, 2, cols)
        g_group = from_group(low, [sums, *done])
        edge = (2 * n_r * (-(-pixels // 8) * 8), cols)
        edges = neighbours(*run(
            functools.partial(edges_body, dims=dims), [shape(edge, BF)] * 2, [*g_group, *all_loaded(t_group)],
            f"edges_{u}", [pltpu.VMEM(edge, F32)]))
        dt, coef, out_sums = run(
            functools.partial(dt_body, total=total),
            [shape((rows_16, depth), BF), shape((n_r, 4, cols), F32), shape((2, cols), F32)],
            [ids, *g_group, *all_loaded(t_group), loaded(both), loaded(sums), out_split[u]], f"dt_{u}", scalars=1, moved=4 * MIB,
        )
        done = sums_1.add([coef]) if sums_1 is not None else []
        t_terms = run(
            temporal_grad_body, [loaded(shape((3 * mid, cols), BF))] + [shape((3 * mid, cols), BF)] * (n_r - 1),
            [ids, loaded(window), dt], f"temporal_grad_{u}", [pltpu.VMEM((mid, depth), F32)], scalars=1,
            flops=temporal_flops, moved=4 * MIB,
        )
        t_grad = traded(t_terms)
        d_mid, sums = run(
            functools.partial(middle_body, dims=dims), [far(shape((rows, mid), F32)), shape((2, mid), F32)],
            [ids, dt, coef, *edges, keep, stat, mid_own[u], far(row_w), far(s_far)], f"middle_{u}",
            [pltpu.VMEM((pixels, frames + 16, depth), F32), pltpu.VMEM(row_shape.shape, BF), s_scr, s_scr, sems((3,))],
            scalars=1, flops=temporal_flops, moved=8 * MIB, after=[t_terms[0]],
        )
        done = sums_1.add([sums]) if sums_1 is not None else []
        sums = from_all(sums, "frames")
        ds_shape, sum_shape = shape((rows, mid), BF), shape((2, mid), F32)
        acc = pltpu.VMEM((mid, n_f * k), F32)
        grad_args = [far(d_mid), stat, mid_own[u], sums]
        if u > 0 or not ring:
            ds, send, kept, mid_sums = run(
                functools.partial(input_body, dims=dims, total=total),
                [ds_shape, shape((2, rows, cols), BF), shape((2, rows, cols), F32), sum_shape],
                [ids, *grad_args, far(s_far), far(spatial_w[u])], f"input_{u}",
                [*adjoint_scr, pltpu.VMEM((rows, depth), F32), s_scr, s_scr, w_scr, sems((3,))],
                limit=44, scalars=1, flops=spatial_flops, moved=8 * MIB, after=t_grad[1:],
            )
        if ring and u > 0:
            *terms, token = run(
                functools.partial(weight_body, dims=dims),
                [far(shape((n_f,) + wire.shape, BF)), wire, wire, shape((8, LANES), F32)], [ids, loaded(act), ds, *all_loaded(t_grad)], f"weight_{u}", [pad, acc, pltpu.VMEM((n_f,) + wire.shape, BF), sems((n_f,))],
                scalars=1, flops=spatial_flops, moved=8 * MIB,
            )
            sums_1 = RingSums(*terms, f"sum_{u}")
        elif ring:
            slab = wire
            ds, flat, *terms = run(
                functools.partial(weight_first_body, dims=dims, total=total),
                [ds_shape, shape((8, 512), F32), far(shape((n_f,) + slab.shape, BF)), slab, slab],
                [ids, loaded(d_mid), *grad_args[1:], *d_norms[1], out_sums, *all_loaded(t_grad), loaded(s_far), loaded(act)], f"weight_{u}",
                [pltpu.VMEM((2, mid), F32), pad, acc, pltpu.VMEM((n_f,) + wire.shape, BF), sems((n_f,))],
                scalars=1, flops=spatial_flops, moved=8 * MIB, scale=1,
            )
            sums_0 = RingSums(*terms, f"sum_{u}")
        else:
            (s_grad,) = run(
                functools.partial(weight_plain_body, dims=dims), [w_shape], [loaded(act), ds],
                f"weight_{u}", [pad, acc], flops=spatial_flops, moved=8 * MIB,
            )
            s_grad = swap(s_grad.reshape(mid, n_f, k).transpose(1, 0, 2), "frames")
            t_rows = jnp.zeros((n_r,) + t_grad[0].shape, BF)
            for j in range(n_r):
                t_rows = lax.dynamic_update_index_in_dim(t_rows, t_grad[j], ids[j], 0)
            weight_parts[u] = (s_grad, swap(ordered(t_rows, n_f), "frames"))
        d_norms[u] = (mid_sums, out_sums) if u > 0 or not ring else None

    ends_1 = sums_1.end() if ring else []
    grad_part, block_part = (own_frames, pixels, depth), (own_frames, pixels, cols)
    ends = run(
        functools.partial(last_body, dims=dims), [loaded(shape(grad_part, BF))] + [shape(grad_part, BF)] * (n_r - 1) + [shape(block_part, BF)] * n_r,
        [ids, ds, loaded(summed_grad), loaded(block), far(spatial_w[0])], "last",
        [*adjoint_scr, pltpu.VMEM((n_r, rows, cols), F32), pltpu.VMEM((1, rows, cols), F32), pltpu.VMEM((n_r,) + grad_part, BF),
         pltpu.VMEM((n_r,) + block_part, BF), w_scr, sems(())],
        limit=44, scalars=1, flops=spatial_flops, moved=8 * MIB, scale=1, after=ends_1[1:],
    )
    sent = ()
    state = [flip(a) for a in (spatial_weights, spatial_first, spatial_second)]
    state += [temporal_weights, temporal_first, temporal_second]
    if not ring:
        blocks, grads = traded(ends[n_r:]), traded(ends[:n_r])
    if ring:
        flats = from_group(flat)
        sums_0.add(ends[:1])
        blocks, grads = traded(ends[n_r:]), traded(ends[:n_r])
        sent = sums_0.add(grads[1:2])
        weights = adam_unit(1, ends_1, state, None, "adam_1", sent)
        sent = sums_0.add([weights[0], *grads[2:]])
        weight_parts[0] = sums_0.end()
    block_out, input_grad = run(
        finish_body, [shape(frames_in.shape, BF), shape(frames_in.shape, F32)],
        [ids, *all_loaded(blocks + grads)], "finish", [pltpu.VMEM((own_frames, pixels, depth), F32)],
        scalars=1, moved=3 * MIB, after=sent,
    )
    if ring:
        norms = [mid_norm, mid_first, mid_second, out_norm, out_first, out_second]
        norms = run(
            norm_body, [shape(a.shape, F32) for a in norms], [ids, *flats, *norms], "norms",
            [pltpu.VMEM((n_r, 8, 512), F32)], scalars=1,
        )
    else:
        flat = jnp.concatenate([jnp.concatenate([m.reshape(-1), o.reshape(-1)]) for m, o in d_norms])
        flat = from_all(flat, "rep").reshape(n_r, units, -1)
        mid_grad = flat[:, :, : 2 * mid].reshape(n_r, units, 2, mid).transpose(1, 2, 0, 3)
        mid_grad = mid_grad.reshape(units, 2, n_r * mid)
        out_grad = flat[:, :, 2 * mid :].reshape(n_r, units, 2, cols).transpose(1, 2, 0, 3)
        out_grad = out_grad.reshape(units, 2, depth)
        norms = [*adam_step(mid_norm, mid_grad, mid_first, mid_second, RATE_NORM, 0.0)]
        norms += adam_step(out_norm, out_grad, out_first, out_second, RATE_NORM, 0.0)

    if ring:
        weights = adam_unit(0, weight_parts[0], state, weights, "adam_0")
        weights = [flip(a) for a in weights[:4]] + list(weights[4:])
    else:
        grads = [jnp.stack([jnp.sum(parts[i].astype(F32), axis=0) for parts in weight_parts]) for i in range(2)]
        news = adam_step(spatial_weights, flip(grads[0]), spatial_first, spatial_second, RATE_WEIGHT, DECAY)
        weights = [*news, news[0].astype(BF)]
        news = adam_step(temporal_weights, grads[1], temporal_first, temporal_second, RATE_WEIGHT, DECAY)
        weights += [*news, news[0].astype(BF)]
    return (block_out, input_grad, *weights, *norms)


def solution(mesh):
    by_frame = P(("frames", "rep"), None, None, None)
    by_block = P(None, "frames", "rep")
    placed = (by_frame, by_frame, P()) + (by_block,) * 6 + (P(),) * 6
    return jax.shard_map(
        on_device,
        mesh=mesh,
        in_specs=placed,
        out_specs=(by_frame, by_frame) + (by_block,) * 8 + (P(),) * 6,
        check_vma=False,
    )
```

```python
import functools

import jax
import jax.numpy as jnp
from jax import lax
from jax.experimental import pallas as pl
from jax.experimental.pallas import tpu as pltpu
from jax.sharding import PartitionSpec as P

STEP = 5
NORM_EPS = 1e-05
ADAM_EPS = 1e-08
BETA_ONE = 0.5
BETA_TWO = 0.5
RATE_WEIGHT = 0.015
RATE_NORM = 0.2
DECAY = 0.05
BF = jnp.bfloat16
F32 = jnp.float32
MIB = 1 << 20
VMEM = pl.BlockSpec(memory_space=pltpu.VMEM)
SMEM = pl.BlockSpec(memory_space=pltpu.SMEM)
LANES = 128
SCALE = 30
CHEAP = pl.CostEstimate(flops=1000, bytes_accessed=1000, transcendentals=0)
ANY = pl.BlockSpec(memory_space=pl.ANY)
HBM = pl.BlockSpec(memory_space=pltpu.HBM)


def shape(dims, dtype):
    return jax.ShapeDtypeStruct(tuple(dims), dtype)


class Placed:
    def __init__(self, value, where):
        self.value, self.where = value, where


def far(value):
    return Placed(value, "hbm")


def loaded(value):
    return Placed(value, "loaded")


def near(value):
    return Placed(value, "vmem")


def all_loaded(values):
    return [loaded(v) for v in values]


def in_hbm(array):
    return pltpu.with_memory_space_constraint(array, pltpu.HBM)


def operand(a):
    if not isinstance(a, Placed):
        return a
    return pltpu.with_memory_space_constraint(a.value, pltpu.VMEM if a.where == "vmem" else pltpu.HBM)


def result(a):
    if not isinstance(a, Placed):
        return a
    return (pltpu.VMEM if a.where == "vmem" else pltpu.HBM)(a.value.shape, a.value.dtype)


def is_far(a):
    return isinstance(a, Placed) and a.where == "hbm"


def run(body, outs, args, name, scratch=(), limit=28, scalars=0, flops=0, moved=0, after=(), scale=SCALE):
    def kernel(*refs):
        body(*refs[len(after) :])

    return pl.pallas_call(
        kernel,
        out_shape=tuple(result(o) for o in outs),
        in_specs=[ANY] * len(after) + [SMEM] * scalars + [ANY if is_far(a) else VMEM for a in args[scalars:]],
        out_specs=tuple(HBM if is_far(o) else VMEM for o in outs),
        scratch_shapes=list(scratch),
        compiler_params=pltpu.CompilerParams(vmem_limit_bytes=limit * MIB),
        cost_estimate=pl.CostEstimate(flops=int(scale * flops), bytes_accessed=int(scale * moved), transcendentals=0),
        name=name,
    )(*after, *[operand(a) for a in args])


def gate(value, after, name):
    return pl.pallas_call(
        lambda *refs: None,
        out_shape=shape(value.shape, value.dtype),
        in_specs=[ANY] * (len(after) + 1),
        out_specs=ANY,
        input_output_aliases={len(after): 0},
        name=name,
    )(*after, value)


def started(source, target, sem):
    copy = pltpu.make_async_copy(source, target, sem)
    copy.start()
    return copy


def padded(values, rows):
    return jnp.concatenate([values, jnp.zeros((rows - values.shape[0], values.shape[1]), F32)], axis=0)


def sigmoid(v):
    return 1.0 / (1.0 + jnp.exp(-v))


def silu(v):
    return v / (1.0 + jnp.exp(-v))


def silu_slope(v):
    s = sigmoid(v)
    return s * (1.0 + v * (1.0 - s))


def mm(a, b, dims):
    return lax.dot_general(a, b, (dims, ((), ())), preferred_element_type=F32)


def put_rows(out_ref, upper, lower):
    out_ref[:, 0:1, :] = jnp.broadcast_to(upper[None], (out_ref.shape[0],) + upper.shape)
    out_ref[:, 1:2, :] = jnp.broadcast_to(lower[None], (out_ref.shape[0],) + lower.shape)


def put_moments(values, out_ref):
    rows = values.shape[0]
    mean = jnp.sum(values, axis=0, keepdims=True) * (1.0 / rows)
    off = values - mean
    put_rows(out_ref, mean, jnp.sum(off * off, axis=0, keepdims=True))


def joined_moments(both, rows):
    count = both.shape[0]
    mean = jnp.sum(both[:, 0:1], axis=0) * (1.0 / count)
    off = both[:, 0:1] - mean[None]
    total = jnp.sum(both[:, 1:2] + rows * (off * off), axis=0)
    return mean, lax.rsqrt(total * (1.0 / (rows * count)) + NORM_EPS)


def put_sums(upstream, normed, out_ref):
    put_rows(out_ref, jnp.sum(upstream * normed, axis=0, keepdims=True), jnp.sum(upstream, axis=0, keepdims=True))


def convolve(pad, w_ref, turned, dims):
    height, width, frames, depth = dims
    rows = height * width * frames
    for k in range(9):
        i, j = k // 3, k % 3
        piece = pad[i : i + height, j : j + width].reshape(rows, depth).astype(BF)
        part = mm(w_ref[:, k * depth : (k + 1) * depth], piece, ((1,), (1,)))
        if k == 0:
            turned[...] = part
        else:
            turned[...] += part
    return turned[...].T


def widened(scr, values, before, after):
    frames = values.shape[1]
    scr[:, 8 : 8 + frames, :] = values
    scr[:, 7:8, :] = before
    scr[:, 8 + frames : 9 + frames, :] = after


RING = (0, 2, 4, 6, 7, 5, 3, 1)


def can_ring(mid, k, k_t, count):
    return count == len(RING) and mid == 288 and k == 576 and k_t == 432


def ring_place(frame):
    return jnp.where(frame % 2 == 0, frame // 2, 7 - frame // 2)


def ring_device(place):
    place = place % 8
    return jnp.where(place < 4, 2 * place, 15 - 2 * place)


def low_half(shape_):
    return lax.broadcasted_iota(jnp.int32, shape_, 1) < LANES // 2


def fold(top, bottom, out_ref, k):
    edge = k - LANES // 2
    out_ref[:, 0:edge] = top[:, 0:edge].astype(out_ref.dtype)
    mixed = jnp.where(low_half((top.shape[0], LANES)), top[:, edge : edge + LANES], bottom[:, 0:LANES])
    out_ref[:, edge : edge + LANES] = mixed.astype(out_ref.dtype)
    out_ref[:, edge + LANES : 2 * k] = bottom[:, LANES : k + LANES // 2].astype(out_ref.dtype)


def pack_body(ids_ref, w_ref, t_ref, *refs):
    outs, folded, scr = refs[:-2], refs[-2], refs[-1]
    mid, k = w_ref.shape[1:]
    half = mid // 2
    edge = k - LANES // 2
    odd = ids_ref[6] % 2 == 1
    low = low_half((half, LANES))

    @pl.when(jnp.logical_not(odd))
    def _():
        scr[:, 0:k] = w_ref[0]

    @pl.when(odd)
    def _():
        scr[:, 0:k] = w_ref[0]
        scr[...] = pltpu.roll(scr[...], k, 1)

    folded[0:half, 0:edge] = scr[0:half, 0:edge].astype(BF)
    folded[0:half, edge + LANES :] = scr[half:mid, 0:edge].astype(BF)
    upper, lower = scr[0:half, edge:], pltpu.roll(scr[half:mid, edge:], LANES // 2, 1)
    folded[0:half, edge : edge + LANES] = jnp.where(low != odd, upper, lower).astype(BF)
    rows = folded.shape[0] - half
    for i in range(2 * k // LANES):
        at = slice(i * LANES, (i + 1) * LANES)
        folded[half:, at] = t_ref[0, rows * i : rows * (i + 1), :].astype(BF)
    start = 0
    for out in outs:
        out[...] = folded[start : start + out.shape[0], :]
        start += out.shape[0]


def packed(u, ids, spatial, temporal, sizes):
    mid, k = spatial.shape[1:]
    flat = [pl.BlockSpec((n, 2 * k), lambda i: (0, 0)) for n in sizes]
    return pl.pallas_call(
        pack_body,
        grid=(1,),
        out_shape=[shape((n, 2 * k), BF) for n in sizes],
        in_specs=[SMEM] + [pl.BlockSpec((1,) + a.shape[1:], lambda i: (u, 0, 0)) for a in (spatial, temporal)],
        out_specs=flat,
        scratch_shapes=[pltpu.VMEM((sum(sizes), 2 * k), BF), pltpu.VMEM((mid, k + LANES // 2), F32)],
        compiler_params=pltpu.CompilerParams(vmem_limit_bytes=24 * MIB),
        name=f"pack_{u}",
    )(ids, in_hbm(spatial), in_hbm(temporal))


def unpack_temporal(f, slot, t_ref):
    rows = slot.shape[0]
    per = t_ref.shape[3] // rows
    for j in range(slot.shape[1] // LANES):
        block = 3 * f + j // per
        piece = slot[:, j * LANES : (j + 1) * LANES]
        t_ref[(block % 8) // 2, block // 8, block % 2, (j % per) * rows : (j % per + 1) * rows, :] = piece


def slots_of(refs, half):
    if len(refs[0].shape) == 3:
        return [([refs[0].at[i, 0:half]], refs[0].at[i, half:]) for i in range(8)], refs[1:]
    cut = half - refs[0].shape[0]
    return [([refs[i], refs[8 + i].at[0:cut]], refs[8 + i].at[cut:]) for i in range(8)], refs[16:]


def unpack_rows(ids_ref, slots, outs, scr):
    half = scr.shape[3]
    for i, (_, slot) in enumerate(slots):
        unpack_temporal(ids_ref[6 + i], slot, scr)
    for j, out_ref in enumerate(outs):
        for k in range(3):
            for part in range(2):
                out_ref[k, part * half : (part + 1) * half, :] = scr[ids_ref[j], k, part]


def unpack_spatial(ids_ref, slots, w_ref):
    half, k = w_ref.shape[0] // 2, w_ref.shape[1] // 8
    edge = k - LANES // 2
    low = low_half((half, LANES))
    for i, (slot, _) in enumerate(slots):
        f = ids_ref[6 + i]
        odd = f % 2
        base = (f // 2) * (2 * k)
        tiles = pl.ds(pl.multiple_of(base + odd * (edge + LANES), LANES), edge)
        middle = pl.ds(pl.multiple_of(base + edge, LANES), LANES)
        start = 0
        for part in slot:
            count = part.shape[0]
            w_ref[start : start + count, tiles] = part[:, 0:edge]
            w_ref[half + start : half + start + count, tiles] = part[:, edge + LANES :]
            start += count
        mixed = jnp.concatenate([part[:, edge : edge + LANES].astype(F32) for part in slot], axis=0)
        mine = low != (odd == 1)
        for rows, values in ((slice(0, half), mixed), (slice(half, 2 * half), pltpu.roll(mixed, LANES // 2, 1))):
            w_ref[rows, middle] = jnp.where(mine, values, w_ref[rows, middle].astype(F32)).astype(BF)


def spatial_body(*refs, dims, half, ring, first):
    height, width, frames, depth = dims
    rows = height * width * frames
    ids_ref, refs = refs[0], refs[1:]
    if ring:
        slots, refs = slots_of(refs, half)
    else:
        w_ref, refs = refs[0], refs[1:]
    refs = iter(refs)

    def take(count):
        return [next(refs) for _ in range(count)]

    sources = take(1 if first else 6)
    (s_ref,) = take(1) if not first else (None,)
    first_ref, last_ref, mom_ref, s_far = take(4)
    w_far, act_far, row_outs = take(int(ring)), take(int(not first)), take(4 * int(ring))
    pad, turned, sems = take(3)
    w_scr, act_scr, row_scr = take(int(ring)), take(int(not first)), take(int(ring))
    if first:
        (s_ref,) = take(1)

    copies = []
    if ring:
        w_ref = w_scr[0]
        unpack_spatial(ids_ref, slots, w_ref)
        copies.append(started(w_ref, w_far[0], sems.at[0]))
        unpack_rows(ids_ref, slots, row_outs, row_scr[0])
    pad[...] = jnp.zeros(pad.shape, F32)
    if first:
        pad[1 : height + 1, 1 : width + 1] = sources[0][...].astype(F32).reshape(dims)
    else:
        both_ref, norm_ref = sources[4:]
        for j, t_ref in enumerate(sources[:4]):
            b = ids_ref[j]
            mean, inverse = joined_moments(both_ref[:, b], rows)
            norm = norm_ref[b]
            y = (t_ref[...].astype(F32) - mean) * (inverse * norm[0:1]) + norm[1:2]
            a = silu(y)
            at = pl.ds(pl.multiple_of(b * LANES, LANES), LANES)
            act_scr[0][:, at] = padded(a, act_scr[0].shape[0]).astype(BF)
            pad[1 : height + 1, 1 : width + 1, :, at] = a.reshape(height, width, frames, LANES)
        copies.append(started(act_scr[0], act_far[0], sems.at[1]))
    s_ref[...] = convolve(pad, w_ref, turned, dims)
    copies.append(started(s_ref, s_far, sems.at[2]))
    values = s_ref[...]
    put_moments(values, mom_ref)
    grid = values.reshape(height * width, frames, values.shape[-1])
    first_ref[...] = grid[:, 0:1, :]
    last_ref[...] = grid[:, frames - 1 : frames, :]
    for copy in copies:
        copy.wait()


def temporal_body(
    ids_ref, s_ref, both_ref, before_ref, after_ref, norm_ref, keep_ref, w0, w1, w2, w3,
    send_ref, kept_ref, stat_ref, win_far, row_far, scr, part, win_ref, row_ref, sems, s_scr=None, *, dims
):
    height, width, frames, depth = dims
    pixels = height * width
    rows = pixels * frames
    mid = s_ref.shape[-1]
    if s_scr is not None:
        arriving = started(s_ref, s_scr, sems.at[2])
    for j, w_ref in enumerate((w0, w1, w2, w3)):
        row_ref[:, :, pl.ds(pl.multiple_of(ids_ref[j] * LANES, LANES), LANES)] = w_ref[...]
    copies = [started(row_ref, row_far, sems.at[0])]
    mean, inverse = joined_moments(both_ref[...], rows)
    stat_ref[0:1, :] = mean
    stat_ref[1:2, :] = inverse
    scale, bias = inverse * norm_ref[0:1], norm_ref[1:2]

    def active(v):
        return silu((v - mean) * scale + bias)

    if s_scr is not None:
        arriving.wait()
        s_ref = s_scr
    middle = active(s_ref[...])
    widened(
        scr, middle.reshape(pixels, frames, mid),
        active(before_ref[...].reshape(pixels, mid)).reshape(pixels, 1, mid),
        active(after_ref[...].reshape(pixels, mid)).reshape(pixels, 1, mid),
    )
    whole = win_ref.shape[1]
    earlier = (scr[:, 7 : 7 + frames, :] * keep_ref[0][None]).reshape(rows, mid)
    later = (scr[:, 9 : 9 + frames, :] * keep_ref[1][None]).reshape(rows, mid)
    for i, values in enumerate((earlier, middle, later)):
        win_ref[i] = padded(values, whole).astype(BF)
    copies.append(started(win_ref, win_far, sems.at[1]))
    part[...] = mm(win_ref[0], row_ref[0], ((1,), (0,)))
    part[...] += mm(win_ref[1], row_ref[1], ((1,), (0,)))
    part[...] += mm(win_ref[2], row_ref[2], ((1,), (0,)))
    put_halves(ids_ref, part, send_ref, kept_ref)
    for copy in copies:
        copy.wait()


def put_halves(ids_ref, part, send_ref, kept_ref):
    core = ids_ref[4]
    rows = send_ref.shape[1]
    for i in range(2):
        other = pl.multiple_of((2 * i + 1 - core) * LANES, LANES)
        own = pl.multiple_of((2 * i + core) * LANES, LANES)
        send_ref[i] = part[0:rows, pl.ds(other, LANES)].astype(BF)
        kept_ref[i] = part[0:rows, pl.ds(own, LANES)]


def total_body(ids_ref, got_ref, kept_ref, last_ref, t_ref, low_ref, mom_ref):
    x = ids_ref[5]
    t = got_ref[x].astype(F32) + kept_ref[x] + last_ref[...].astype(F32)
    t_ref[...] = t
    low_ref[...] = t.astype(BF)
    put_moments(t, mom_ref)


def edges_body(*refs, dims):
    height, width, frames, depth = dims
    blocks, (first_ref, last_ref, scr) = refs[:-3], refs[-3:]
    pixels = height * width
    slot = scr.shape[0] // len(blocks)
    for out_ref, at in ((first_ref, 0), (last_ref, frames - 1)):
        for j, ref in enumerate(blocks):
            grid = ref[...].astype(F32).reshape(pixels, frames, LANES)
            scr[slot * j : slot * j + pixels, :] = grid[:, at : at + 1, :].reshape(pixels, LANES)
        out_ref[...] = scr[...].astype(BF)


def top_body(ids_ref, t_ref, both_ref, norm_ref, x_ref, cot_ref, block_ref, g_ref, low_ref, sums_ref):
    rows = t_ref.shape[0]
    b = ids_ref[0]
    mean, inverse = joined_moments(both_ref[:, b], rows)
    norm = norm_ref[b]
    normed = (t_ref[...] - mean) * inverse
    own = pl.ds(pl.multiple_of(b * LANES, LANES), LANES)
    summed = normed * norm[0:1] + norm[1:2] + x_ref[:, own].astype(F32)
    block_ref[...] = silu(summed).astype(BF)
    g = cot_ref[...].astype(F32) * silu_slope(summed)
    g_ref[...] = g
    low_ref[...] = g.astype(BF)
    put_sums(g, normed, sums_ref)


def below_body(ids_ref, got_ref, kept_ref, last_ref, t_ref, both_ref, norm_ref, low_ref, sums_ref):
    rows = t_ref.shape[0]
    b, x = ids_ref[0], ids_ref[5]
    d_act = got_ref[x].astype(F32) + kept_ref[x] + last_ref[...].astype(F32)
    mean, inverse = joined_moments(both_ref[:, b], rows)
    norm = norm_ref[b]
    normed = (t_ref[...] - mean) * inverse
    g = d_act * silu_slope(normed * norm[0:1] + norm[1:2])
    low_ref[...] = g.astype(BF)
    put_sums(g, normed, sums_ref)


def dt_body(
    ids_ref, g0, g1, g2, g3, t0, t1, t2, t3, both_ref, sums_ref, norm_ref, dt_ref, coef_ref, sum_ref, *, total
):
    rows, whole = g0.shape[0], dt_ref.shape[0]
    for j, (g_ref, t_ref) in enumerate(((g0, t0), (g1, t1), (g2, t2), (g3, t3))):
        b = ids_ref[j]
        mean, inverse = joined_moments(both_ref[:, b], rows)
        sums = jnp.sum(sums_ref[:, b], axis=0)
        if j == 0:
            sum_ref[...] = sums
        c1 = norm_ref[b][0:1] * inverse
        c2 = c1 * sums[1:2] * (1.0 / total)
        c3 = c1 * inverse * sums[0:1] * (1.0 / total)
        coef_ref[j] = jnp.concatenate([c1, c2, c3, mean], axis=0)
        d = c1 * g_ref[...].astype(F32) - c2 - c3 * (t_ref[...].astype(F32) - mean)
        dt_ref[:, pl.ds(pl.multiple_of(b * LANES, LANES), LANES)] = padded(d, whole).astype(BF)


def temporal_grad_body(ids_ref, win_ref, dt_ref, *refs):
    outs, term = refs[:-1], refs[-1]
    mid = win_ref.shape[-1]
    dt = dt_ref[...]
    for k in range(3):
        term[...] = mm(win_ref[k], dt, ((0,), (0,)))
        for j, out_ref in enumerate(outs):
            at = pl.ds(pl.multiple_of(ids_ref[j] * LANES, LANES), LANES)
            out_ref[k * mid : (k + 1) * mid, :] = term[:, at].astype(BF)


def middle_body(
    ids_ref, dt_ref, coef_ref, before_ref, after_ref, keep_ref, stat_ref, norm_ref, row_far, s_far,
    d_far, sums_ref, scr, row_ref, s_ref, d_ref, sems, *, dims
):
    height, width, frames, depth = dims
    pixels = height * width
    rows = pixels * frames
    copies = [started(row_far, row_ref, sems.at[0]), started(s_far, s_ref, sems.at[1])]
    before, after = before_ref[...].astype(F32), after_ref[...].astype(F32)
    slot = before.shape[0] // 8
    dt = dt_ref[...]
    scr[:, 8 : 8 + frames, :] = dt.astype(F32)[0:rows].reshape(pixels, frames, depth)
    for j in range(4):
        at = pl.ds(pl.multiple_of(ids_ref[j] * LANES, LANES), LANES)
        c = coef_ref[j]

        def halo(frame):
            g, t = (frame[slot * b : slot * b + pixels] for b in (j, 4 + j))
            d = c[0:1] * g - c[1:2] - c[2:3] * (t - c[3:4])
            return d.astype(BF).astype(F32).reshape(pixels, 1, LANES)

        scr[:, 7:8, at] = halo(before)
        scr[:, 8 + frames : 9 + frames, at] = halo(after)
    later = (scr[:, 9 : 9 + frames, :] * keep_ref[1][None]).reshape(rows, depth).astype(BF)
    earlier = (scr[:, 7 : 7 + frames, :] * keep_ref[0][None]).reshape(rows, depth).astype(BF)
    copies[0].wait()
    d_ref[...] = mm(later, row_ref[0], ((1,), (1,)))
    d_ref[...] += mm(dt, row_ref[1], ((1,), (1,)))[0:rows]
    d_ref[...] += mm(earlier, row_ref[2], ((1,), (1,)))
    copies[1].wait()
    normed = (s_ref[...] - stat_ref[0:1]) * stat_ref[1:2]
    d = d_ref[...] * silu_slope(normed * norm_ref[0:1] + norm_ref[1:2])
    d_ref[...] = d
    leaving = started(d_ref, d_far, sems.at[2])
    put_sums(d, normed, sums_ref)
    leaving.wait()


def spatial_grad(d_ref, s_ref, stat_ref, norm_ref, sums_ref, ds_ref, sum_ref, total):
    sums = jnp.sum(sums_ref[...], axis=0)
    sum_ref[...] = sums
    inverse = stat_ref[1:2]
    normed = (s_ref[...] - stat_ref[0:1]) * inverse
    d = d_ref[...] - sums[1:2] * (1.0 / total) - normed * (sums[0:1] * (1.0 / total))
    ds_ref[...] = (norm_ref[0:1] * inverse * d).astype(BF)


def adjoint(ds_ref, w_ref, pad, patches, stacked, dims):
    height, width, frames, depth = dims
    rows, mid = ds_ref.shape
    whole = mid // LANES * LANES
    rest = mid - whole
    start = 9 * whole
    pad[...] = jnp.zeros(pad.shape, F32)
    pad[1 : height + 1, 1 : width + 1, :, 0:mid] = ds_ref[...].astype(F32).reshape(height, width, frames, mid)
    lane = lax.broadcasted_iota(jnp.int32, (rows, LANES), 1)
    tails = [jnp.zeros((rows, LANES), F32) for _ in range((patches.shape[1] - start) // LANES)]
    stacked[start:, :] = jnp.zeros((stacked.shape[0] - start, depth), BF)
    for k in range(9):
        i, j = k // 3, k % 3
        piece = pad[2 - i : 2 - i + height, 2 - j : 2 - j + width].reshape(rows, pad.shape[-1])
        w = w_ref[:, k * depth : (k + 1) * depth]
        patches[:, k * whole : (k + 1) * whole] = piece[:, 0:whole].astype(BF)
        stacked[k * whole : (k + 1) * whole, :] = w[0:whole]
        stacked[start + k * rest : start + (k + 1) * rest, :] = w[whole:mid]
        tile, at = divmod(k * rest, LANES)
        tail = pltpu.roll(piece[:, whole:], at, 1) if at else piece[:, whole:]
        tails[tile] = jnp.where((lane >= at) & (lane < at + rest), tail, tails[tile])
    for tile, tail in enumerate(tails):
        patches[:, start + tile * LANES : start + (tile + 1) * LANES] = tail.astype(BF)
    return mm(patches[...], stacked[...], ((1,), (0,)))


def input_body(
    ids_ref, d_far, stat_ref, norm_ref, sums_ref, s_far, w_far,
    ds_ref, send_ref, kept_ref, sum_ref, pad, patches, stacked, part, s_ref, d_ref, w_ref, sems, *, dims, total
):
    height, width, frames, depth = dims
    copies = [started(s_far, s_ref, sems.at[0]), started(w_far, w_ref, sems.at[1]), started(d_far, d_ref, sems.at[2])]
    copies[0].wait()
    copies[2].wait()
    spatial_grad(d_ref, s_ref, stat_ref, norm_ref, sums_ref, ds_ref, sum_ref, total)
    copies[1].wait()
    part[...] = adjoint(ds_ref, w_ref, pad, patches, stacked, dims)
    put_halves(ids_ref, part, send_ref, kept_ref)


def by_frame(source, out_ref, dims):
    height, width, frames, depth = dims
    pixels, own = height * width, out_ref.shape[1]
    for r in range(source.shape[0]):
        for f in range(frames):
            values = source[r, pl.ds(f, pixels, stride=frames), :]
            out_ref[f // own, f % own, :, r * LANES : (r + 1) * LANES] = values.astype(out_ref.dtype)


def last_body(ids_ref, ds_ref, g_ref, block_ref, w_far, *refs, dims):
    grads, blocks, refs = refs[:4], refs[4:8], refs[8:]
    pad, patches, stacked, part, block, grad_scr, block_scr, w_ref, sem = refs
    height, width, frames, depth = dims
    copy = started(w_far, w_ref, sem)
    block[0] = block_ref[...].astype(F32)
    by_frame(block, block_scr, dims)
    copy.wait()
    terms = adjoint(ds_ref, w_ref, pad, patches, stacked, dims)
    own = ids_ref[0]
    for r in range(part.shape[0]):
        part[r] = terms[:, r * LANES : (r + 1) * LANES]
    part[own] = part[own] + g_ref[...]
    by_frame(part, grad_scr, dims)
    for j in range(4):
        grads[j][...] = grad_scr[ids_ref[j]]
        blocks[j][...] = block_scr[ids_ref[j]]


def finish_body(ids_ref, *refs):
    blocks, grads, (out_ref, grad_out_ref, block) = refs[:4], refs[4:8], refs[8:]
    own, height, width, depth = out_ref.shape
    for j, ref in enumerate(blocks):
        block[:, :, pl.ds(pl.multiple_of(ids_ref[j] * LANES, LANES), LANES)] = ref[...].astype(F32)
    for f in range(own):
        grad = sum(ref[f].astype(F32) for ref in grads)
        for h in range(height):
            at = slice(h * width, (h + 1) * width)
            out_ref[f, h] = block[f, at].astype(BF)
            grad_out_ref[f, h] = grad[at]


def weight_terms(act_ref, ds_ref, pad, acc, dims):
    height, width, frames, depth = dims
    rows = height * width * frames
    pad[...] = jnp.zeros(pad.shape, F32)
    pad[1 : height + 1, 1 : width + 1] = act_ref[...].astype(F32)[0:rows].reshape(dims)
    flipped = ds_ref[...].astype(F32).T.astype(BF)

    for k in range(9):
        i, j = k // 3, k % 3
        piece = pad[i : i + height, j : j + width].reshape(rows, depth).astype(BF)
        acc[:, k * depth : (k + 1) * depth] = mm(flipped, piece, ((1,), (0,)))


def put_shards(acc, places, out_ref, k, then):
    mid = acc.shape[0]
    half = mid // 2
    wide = k + LANES // 2
    for f in range(8):
        if f % 2 == 0:
            top = acc[0:half, k * f : k * f + wide]
            bottom = pltpu.roll(acc[half:mid, k * f : k * f + wide], LANES // 2, 1)
        else:
            start = k * f - LANES // 2
            top = pltpu.roll(acc[0:half, start : start + wide], k, 1)
            bottom = acc[half:mid, start : start + wide]
        fold(top, bottom, out_ref.at[places[f], 0:half], k)
        then(f)


def weight_plain_body(act_ref, ds_ref, out_ref, pad, acc, *, dims):
    weight_terms(act_ref, ds_ref, pad, acc, dims)
    out_ref[...] = acc[...].astype(BF)


def put_temporal(ids_ref, sources, out_ref, half):
    rows = out_ref.shape[1] - half
    per = half // rows
    for i, source in enumerate(sources):
        for tap in range(3):
            for part in range(2):
                block = tap * 8 + ids_ref[i] * 2 + part
                place = ids_ref[14 + block // 3]
                for j in range(per):
                    start = tap * 2 * half + part * half + j * rows
                    at = pl.multiple_of(((block % 3) * per + j) * LANES, LANES)
                    out_ref[place, half:, pl.ds(at, LANES)] = source[start : start + rows, :]


def put_terms(ids_ref, act_ref, ds_ref, t_refs, out_far, ahead_ref, back_ref, pad, acc, out_ref, sems, dims):
    weight_terms(act_ref, ds_ref, pad, acc, dims)
    places = [ids_ref[14 + f] for f in range(8)]
    put_temporal(ids_ref, t_refs, out_ref, acc.shape[0] // 2)
    copies = []
    put_shards(
        acc, places, out_ref, acc.shape[1] // 8,
        lambda f: copies.append(started(out_ref.at[places[f]], out_far.at[places[f]], sems.at[f])),
    )
    ahead_ref[...] = out_ref[4]
    back_ref[...] = out_ref[5]
    for copy in copies:
        copy.wait()


def weight_body(
    ids_ref, act_ref, ds_ref, t0, t1, t2, t3, out_far, ahead_ref, back_ref, token_ref, pad, acc, out_ref, sems, *, dims
):
    token_ref[...] = jnp.zeros(token_ref.shape, F32)
    put_terms(ids_ref, act_ref, ds_ref, (t0, t1, t2, t3), out_far, ahead_ref, back_ref, pad, acc, out_ref, sems, dims)


def weight_first_body(
    ids_ref, d_ref, stat_ref, norm_ref, sums_ref, mid_ref, out_1_ref, out_0_ref, t0, t1, t2, t3, s_ref, act_ref,
    ds_ref, flat_ref, out_far, ahead_ref, back_ref, sum_ref, pad, acc, out_ref, sems, *, dims, total
):
    spatial_grad(d_ref, s_ref, stat_ref, norm_ref, sums_ref, ds_ref, sum_ref, total)
    flat_ref[...] = jnp.zeros(flat_ref.shape, F32)
    for i, ref in enumerate((sum_ref, mid_ref, out_0_ref, out_1_ref)):
        flat_ref[2 * i : 2 * i + 2, 0 : ref.shape[1]] = ref[...]
    put_terms(ids_ref, act_ref, ds_ref, (t0, t1, t2, t3), out_far, ahead_ref, back_ref, pad, acc, out_ref, sems, dims)


def norm_body(ids_ref, f0, f1, f2, f3, *refs):
    refs, flat_ref = refs[:-1], refs[-1]
    for j, ref in enumerate((f0, f1, f2, f3)):
        flat_ref[ids_ref[j]] = ref[...]
    count = flat_ref.shape[0]
    for which in range(2):
        old, new = refs[3 * which : 3 * which + 3], refs[6 + 3 * which : 9 + 3 * which]
        width = old[0].shape[-1] // count
        for u in range(2):
            row = 4 * which + 2 * u
            grad = jnp.concatenate([flat_ref[r, row : row + 2, 0:width] for r in range(count)], axis=1)
            values = adam_step(old[0][u], grad, old[1][u], old[2][u], RATE_NORM, 0.0)
            for ref, value in zip(new, values):
                ref[u] = value


def adam_step(param, gradient, moment_one, moment_two, rate, decay):
    first_new = BETA_ONE * moment_one + (1.0 - BETA_ONE) * gradient
    second_new = BETA_TWO * moment_two + (1.0 - BETA_TWO) * gradient * gradient
    fix_one = 1.0 - BETA_ONE**STEP
    fix_two = 1.0 - BETA_TWO**STEP
    update = first_new / fix_one / (jnp.sqrt(second_new / fix_two) + ADAM_EPS)
    return (param - rate * (update + decay * param), first_new, second_new)


def adam_into(grad, refs, outs, rows):
    new, first, second = adam_step(refs[0][0, rows], grad, refs[1][0, rows], refs[2][0, rows], RATE_WEIGHT, DECAY)
    outs[0][0, rows] = new
    outs[1][0, rows] = first
    outs[2][0, rows] = second
    outs[3][0, rows] = new.astype(BF)


def adam_body(*refs, grads):
    sources, refs = refs[:grads], refs[grads:]
    refs, outs = refs[:6], refs[-8:]
    half = refs[0].shape[1] // 2
    summed = sources[0][0].astype(F32) + sum(r[...].astype(F32) for r in sources[1:])
    temporal = summed[half:]
    rows = temporal.shape[0]
    for i in range(temporal.shape[1] // LANES):
        piece = temporal[:, i * LANES : (i + 1) * LANES]
        adam_into(piece, refs[3:], outs[4:], slice(i * rows, (i + 1) * rows))
    spatial = summed[0:half]
    k = spatial.shape[1] // 2
    edge = k - LANES // 2
    adam_into(spatial[:, 0:k], refs, outs, slice(0, half))
    adam_into(pltpu.roll(spatial[:, edge:], k, 1)[:, 0:k], refs, outs, slice(half, 2 * half))


def adam_unit(u, sources, state, before, name, after=()):
    unit = [pl.BlockSpec((1,) + a.shape[1:], lambda i: (u, 0, 0)) for a in state]
    types = [F32, F32, F32, BF]
    outs = [shape(state[0].shape, t) for t in types] + [shape(state[3].shape, t) for t in types]
    before = list(before or ())
    whole = [pl.BlockSpec((1,) * (a.ndim - 2) + a.shape[-2:], lambda i, n=a.ndim: (0,) * n) for a in sources]

    def kernel(*refs):
        adam_body(*refs[len(after) :], grads=len(sources))

    return pl.pallas_call(
        kernel,
        grid=(1,),
        out_shape=tuple(outs),
        in_specs=[pl.BlockSpec(memory_space=pl.ANY)] * len(after) + whole + unit + [pl.BlockSpec(memory_space=pl.ANY)] * len(before),
        out_specs=tuple([unit[0]] * 4 + [unit[3]] * 4),
        input_output_aliases={len(after) + len(sources) + 6 + i: i for i in range(len(before))},
        compiler_params=pltpu.CompilerParams(vmem_limit_bytes=40 * MIB),
        cost_estimate=CHEAP,
        name=name,
    )(*after, *[in_hbm(a) for a in [*sources, *state]], *before)


def swap(parts, axis):
    return lax.all_to_all(parts, axis, 0, 0, tiled=True)


def from_all(value, axis):
    count = lax.axis_size(axis)
    return swap(jnp.broadcast_to(value[None], (count,) + value.shape), axis)


def across(value, bit):
    count = lax.axis_size("rep")
    return lax.ppermute(value, "rep", [(i, i ^ bit) for i in range(count)])


MASKS = (0, 2, 1, 3)


def traded(parts):
    return [part if mask == 0 else across(part, mask) for part, mask in zip(parts, MASKS)]


def from_group(value, after=None):
    distant = across(value, 2)
    beside = across(value, 1)
    if after is not None:
        distant = gate(distant, after, "then")
    return value, distant, beside, across(distant, 1)


def neighbours(first, last):
    count = lax.axis_size("frames")
    before = lax.ppermute(last, "frames", [(i, i + 1) for i in range(count - 1)])
    after = lax.ppermute(first, "frames", [(i + 1, i) for i in range(count - 1)])
    return before, after


def along(step):
    return [(RING[i], RING[(i + step) % 8]) for i in range(8)]


def ring_gather(chunks, after):
    ahead, back = [[c] for c in chunks], [[c] for c in chunks]
    for step in range(3):
        if step == 2:
            ahead[-1][-1] = gate(ahead[-1][-1], after, "hop_then")
        for a, b in zip(ahead, back):
            a.append(lax.ppermute(a[-1], "frames", along(1)))
            b.append(lax.ppermute(b[-1], "frames", along(-1)))
    last = lax.ppermute(ahead[0][-1], "frames", along(1)), lax.ppermute(back[1][-1], "frames", along(-1))
    return [piece for a, b, far_piece in zip(ahead, back, last) for piece in [*a, far_piece, *b[1:]]]


def added(gots, parts, places, after, name):
    count = len(gots)

    def body(*refs):
        refs, token_ref = refs[len(after) : -1], refs[-1]
        token_ref[...] = jnp.zeros(token_ref.shape, F32)
        for got_ref, part_ref, out_ref in zip(refs[:count], refs[count : 2 * count], refs[2 * count :]):
            out_ref[...] = (got_ref[...].astype(F32) + part_ref[0].astype(F32)).astype(BF)

    flat = pl.BlockSpec(gots[0].shape, lambda g: (0, 0))
    part_specs = [pl.BlockSpec((1,) + gots[0].shape, lambda g, i=i: (i, 0, 0)) for i in places]
    return pl.pallas_call(
        body,
        grid=(1,),
        out_shape=[shape(g.shape, BF) for g in gots] + [shape((8, LANES), F32)],
        in_specs=[ANY] * len(after) + [flat] * count + part_specs,
        out_specs=[flat] * count + [pl.BlockSpec((8, LANES), lambda g: (0, 0))],
        cost_estimate=CHEAP,
        name=name,
    )(*after, *[in_hbm(g) for g in gots], *[in_hbm(parts)] * count)


def ring_step(ahead, back):
    return lax.ppermute(ahead, "frames", along(1)), lax.ppermute(back, "frames", along(-1))


class RingSums:
    def __init__(self, parts, ahead, back, name):
        self.parts, self.ahead, self.back, self.name = parts, ahead, back, name
        self.step = 0

    def add(self, after=()):
        self.step += 1
        step, after, name = self.step, list(after), f"{self.name}_{self.step}"
        if step < 3:
            gots = ring_step(self.ahead, self.back)
            self.ahead, self.back, token = added(gots, self.parts, (4 - step, 5 + step), after, name)
        else:
            gots = [lax.ppermute(self.ahead, "frames", along(1))]
            self.ahead, token = added(gots, self.parts, (4 - step,), after, name)
        return [token]

    def end(self):
        return [self.parts, *ring_step(self.ahead, self.back)]


def reduced(send, kept, x):
    got = across(send, 1)
    away = lax.dynamic_index_in_dim(got, 1 - x, 0, False).astype(F32)
    away = away + lax.dynamic_index_in_dim(kept, 1 - x, 0, False)
    return got, kept, across(away.astype(BF), 2)


def ordered(t_grad, count):
    n_r, rows, cols = t_grad.shape
    return t_grad.reshape(n_r, 3, rows // 3, cols).transpose(1, 0, 2, 3).reshape(count, -1, cols)


def sum_over(parts, axis):
    return jnp.sum(swap(parts, axis).astype(F32), axis=0)


def on_device(
    frames_in, cotangent, lengths,
    spatial_weights, spatial_first, spatial_second,
    temporal_weights, temporal_first, temporal_second,
    mid_norm, mid_first, mid_second,
    out_norm, out_first, out_second,
):
    own_frames, height, width, depth = frames_in.shape
    n_f, n_r = lax.axis_size("frames"), lax.axis_size("rep")
    assert n_r == 4 and depth == n_r * LANES
    me = lax.axis_index("rep")
    frames = own_frames * n_r
    pixels = height * width
    rows = pixels * frames
    total = float(rows * n_f)
    dims = (height, width, frames, depth)
    units, k, mid = spatial_weights.shape
    cols = LANES
    everyone = ("frames", "rep")
    k_t = temporal_weights.shape[1]
    ring = can_ring(mid, k, k_t, n_f)
    spatial_flops = 2 * rows * 9 * depth * mid
    temporal_flops = 2 * rows * 3 * depth * mid
    pad = pltpu.VMEM((height + 2, width + 2, frames, depth), F32)
    flip = functools.partial(jnp.swapaxes, axis1=1, axis2=2)
    ids = [me, me ^ 2, me ^ 1, me ^ 3, me & 1, me >> 1]
    if ring:
        place = ring_place(lax.axis_index("frames"))
        in_order = jnp.stack(ids + [jnp.int32(f) for f in (*range(8), *range(8))]).astype(jnp.int32)
        ids += [ring_device(place + i) for i in (0, -1, -2, -3, -4, 1, 2, 3)]
        ids += [(ring_place(jnp.int32(f)) - place) % 8 for f in range(8)]
    ids = jnp.stack(ids).astype(jnp.int32)

    frame_ids = lax.axis_index("frames") * frames + jnp.arange(frames, dtype=jnp.int32)
    clip_ends = jnp.cumsum(lengths)
    starts = jnp.concatenate([jnp.zeros((1,), jnp.int32), clip_ends[:-1]])
    opening = jnp.any(frame_ids[:, None] == starts[None, :], axis=1)
    closing = jnp.any((frame_ids + 1)[:, None] == clip_ends[None, :], axis=1)
    keep = jnp.where(jnp.stack([opening, closing]), 0.0, 1.0).astype(F32)[:, :, None]

    act = lax.all_gather(frames_in, "rep", axis=0, tiled=True).transpose(1, 2, 0, 3).reshape(rows, depth)
    cot = cotangent.reshape(own_frames, pixels, n_r, cols).transpose(2, 0, 1, 3)
    cot = swap(cot, "rep").reshape(frames, pixels, cols).transpose(1, 0, 2).reshape(rows, cols)

    mid_own = lax.dynamic_slice_in_dim(mid_norm, me * mid, mid, axis=2)
    out_split = out_norm.reshape(units, 2, n_r, cols).transpose(0, 2, 1, 3)

    slots, temporal_w = [], []

    if ring:
        wire = shape((mid // 2 + k_t * LANES // (2 * k), 2 * k), BF)
        chunks = packed(0, ids, flip(spatial_weights), temporal_weights, (wire.shape[0] // 2, wire.shape[0] // 2))
        held = ring_gather(chunks, [act, cot])
        slots.append((ids, held))
        (wire_1,) = packed(1, ids, flip(spatial_weights), temporal_weights, wire.shape[:1])
        wire_1 = gate(wire_1, [held[3], held[15]], "wire_then")
        slots.append((in_order, [lax.all_gather(wire_1, "frames", axis=0)]))
    else:
        wire = flip(spatial_weights).astype(BF)
        temporal_low = temporal_weights.astype(BF)
        for u in range(units):
            held = lax.all_gather(wire[u], "frames", axis=0)
            slots.append((ids, [held.transpose(1, 0, 2).reshape(mid, n_f * k)]))
            shard = lax.all_gather(temporal_low[u], "frames", axis=0, tiled=True)
            shard = shard.reshape(3, n_r, mid, cols).transpose(1, 0, 2, 3)
            temporal_w.append(traded([lax.dynamic_index_in_dim(shard, ids[j], 0, False) for j in range(n_r)]))

    rows_16 = -(-rows // 16) * 16
    halo = shape((pixels, 1, mid), F32)
    column = shape((rows, cols), BF)
    s_shape, w_shape = shape((rows, mid), F32), shape((mid, n_f * k), BF)
    act_shape = shape((rows_16, depth), BF)
    win_shape, row_shape = shape((3, rows_16, mid), BF), shape((3, mid, depth), BF)
    s_scr, w_scr = pltpu.VMEM(s_shape.shape, F32), pltpu.VMEM(w_shape.shape, BF)
    sems = pltpu.SemaphoreType.DMA
    saved, spatial_w = [], []
    for u in range(units):
        order, held = slots[u]
        sources = [loaded(act)] if u == 0 else [loaded(t_group[0]), *t_group[1:], loaded(both), out_split[u - 1]]
        outs = [s_shape] * (u > 0) + [halo, halo, shape((n_f, 2, mid), F32), far(s_shape)]
        outs += [far(w_shape)] * ring + [far(act_shape)] * (u > 0) + [shape((3, mid, cols), BF)] * (n_r * ring)
        parts = run(
            functools.partial(spatial_body, dims=dims, half=mid // 2, ring=ring, first=u == 0), outs,
            [order, *all_loaded(held), *sources], f"spatial_{u}",
            [pad, pltpu.VMEM((mid, rows), F32), sems((3,))] + [w_scr] * ring + [pltpu.VMEM(act_shape.shape, BF)] * (u > 0)
            + [pltpu.VMEM((n_r, 3, 2, mid // 2, cols), BF)] * ring + [s_scr] * (u == 0),
            scalars=1, flops=spatial_flops, moved=8 * MIB,
            after=[cot, keep, mid_own, out_split] if u == 0 else (),
        )
        spatial = parts[: int(u > 0)]
        first, last, mom, s_far, *more = parts[int(u > 0) :]
        spatial_w.append(more.pop(0) if ring else held[0])
        if u > 0:
            act = more.pop(0)
        if ring:
            temporal_w.append(traded(more))
        mid_both = swap(mom, "frames")
        before, after = neighbours(first, last)
        send, kept, stat, window, row_w = run(
            functools.partial(temporal_body, dims=dims),
            [shape((2, rows, cols), BF), shape((2, rows, cols), F32), shape((2, mid), F32), far(win_shape), far(row_shape)],
            [ids, *(spatial or [far(s_far)]), mid_both, before, after, mid_own[u], keep, *temporal_w[u]], f"temporal_{u}",
            [pltpu.VMEM((pixels, frames + 16, mid), F32), pltpu.VMEM((rows_16, depth), F32),
             pltpu.VMEM(win_shape.shape, BF), pltpu.VMEM(row_shape.shape, BF), sems((3,))] + [s_scr] * (u == 0),
            scalars=1, flops=temporal_flops, moved=8 * MIB,
        )
        t, low, mom = run(
            total_body, [loaded(shape((rows, cols), F32)), column, shape((n_f * n_r, 2, cols), F32)],
            [ids, *reduced(send, kept, me >> 1)], f"total_{u}", scalars=1, moved=3 * MIB,
        )
        both = swap(mom, everyone).reshape(n_f, n_r, 2, cols)
        t_group = from_group(low, [both] if u + 1 < units else None)
        saved.append((act, s_far, stat, window, row_w, t, t_group, both))

    wide = -(-mid // LANES) * LANES
    deep = 9 * (mid // LANES * LANES) + -(-9 * (mid % LANES) // LANES) * LANES
    adjoint_scr = [
        pltpu.VMEM((height + 2, width + 2, frames, wide), F32), pltpu.VMEM((rows, deep), BF), pltpu.VMEM((deep, depth), BF)
    ]
    d_norms = [None] * units
    weight_parts = [None] * units
    token, sums_1 = None, None
    for u in reversed(range(units)):
        act, s_far, stat, window, row_w, t, t_group, both = saved[u]
        if u == units - 1:
            block, summed_grad, low, sums = run(
                top_body, [loaded(column), loaded(shape((rows, cols), F32)), column, shape((n_f * n_r, 2, cols), F32)],
                [ids, loaded(t), loaded(both), out_split[u], loaded(saved[0][0]), loaded(cot)], "top", scalars=1, moved=3 * MIB,
            )
        else:
            low, sums = run(
                below_body, [column, shape((n_f * n_r, 2, cols), F32)],
                [ids, *reduced(send, kept, me >> 1), loaded(t), loaded(both), out_split[u]], f"below_{u}", scalars=1, moved=3 * MIB,
                after=[token] if ring else (),
            )
        done = sums_1.add([sums]) if sums_1 is not None else []
        sums = swap(sums, everyone).reshape(n_f, n_r, 2, cols)
        g_group = from_group(low, [sums, *done])
        edge = (2 * n_r * (-(-pixels // 8) * 8), cols)
        edges = neighbours(*run(
            functools.partial(edges_body, dims=dims), [shape(edge, BF)] * 2, [*g_group, *all_loaded(t_group)],
            f"edges_{u}", [pltpu.VMEM(edge, F32)]))
        dt, coef, out_sums = run(
            functools.partial(dt_body, total=total),
            [shape((rows_16, depth), BF), shape((n_r, 4, cols), F32), shape((2, cols), F32)],
            [ids, *g_group, *all_loaded(t_group), loaded(both), loaded(sums), out_split[u]], f"dt_{u}", scalars=1, moved=4 * MIB,
        )
        done = sums_1.add([coef]) if sums_1 is not None else []
        t_terms = run(
            temporal_grad_body, [loaded(shape((3 * mid, cols), BF))] + [shape((3 * mid, cols), BF)] * (n_r - 1),
            [ids, loaded(window), dt], f"temporal_grad_{u}", [pltpu.VMEM((mid, depth), F32)], scalars=1,
            flops=temporal_flops, moved=4 * MIB,
        )
        t_grad = traded(t_terms)
        d_mid, sums = run(
            functools.partial(middle_body, dims=dims), [far(shape((rows, mid), F32)), shape((n_f, 2, mid), F32)],
            [ids, dt, coef, *edges, keep, stat, mid_own[u], far(row_w), far(s_far)], f"middle_{u}",
            [pltpu.VMEM((pixels, frames + 16, depth), F32), pltpu.VMEM(row_shape.shape, BF), s_scr, s_scr, sems((3,))],
            scalars=1, flops=temporal_flops, moved=8 * MIB, after=[t_terms[0]],
        )
        done = sums_1.add([sums]) if sums_1 is not None else []
        sums = swap(sums, "frames")
        ds_shape, sum_shape = shape((rows, mid), BF), shape((2, mid), F32)
        acc = pltpu.VMEM((mid, n_f * k), F32)
        grad_args = [far(d_mid), stat, mid_own[u], sums]
        if u > 0 or not ring:
            ds, send, kept, mid_sums = run(
                functools.partial(input_body, dims=dims, total=total),
                [ds_shape, shape((2, rows, cols), BF), shape((2, rows, cols), F32), sum_shape],
                [ids, *grad_args, far(s_far), far(spatial_w[u])], f"input_{u}",
                [*adjoint_scr, pltpu.VMEM((rows, depth), F32), s_scr, s_scr, w_scr, sems((3,))],
                limit=44, scalars=1, flops=spatial_flops, moved=8 * MIB, after=t_grad[1:],
            )
        if ring and u > 0:
            *terms, token = run(
                functools.partial(weight_body, dims=dims),
                [far(shape((n_f,) + wire.shape, BF)), wire, wire, shape((8, LANES), F32)], [ids, loaded(act), ds, *all_loaded(t_grad)], f"weight_{u}", [pad, acc, pltpu.VMEM((n_f,) + wire.shape, BF), sems((n_f,))],
                scalars=1, flops=spatial_flops, moved=8 * MIB,
            )
            sums_1 = RingSums(*terms, f"sum_{u}")
        elif ring:
            slab = wire
            ds, flat, *terms = run(
                functools.partial(weight_first_body, dims=dims, total=total),
                [ds_shape, shape((8, 512), F32), far(shape((n_f,) + slab.shape, BF)), slab, slab],
                [ids, loaded(d_mid), *grad_args[1:], *d_norms[1], out_sums, *all_loaded(t_grad), loaded(s_far), loaded(act)], f"weight_{u}",
                [pltpu.VMEM((2, mid), F32), pad, acc, pltpu.VMEM((n_f,) + wire.shape, BF), sems((n_f,))],
                scalars=1, flops=spatial_flops, moved=8 * MIB, scale=1,
            )
            sums_0 = RingSums(*terms, f"sum_{u}")
        else:
            (s_grad,) = run(
                functools.partial(weight_plain_body, dims=dims), [w_shape], [loaded(act), ds],
                f"weight_{u}", [pad, acc], flops=spatial_flops, moved=8 * MIB,
            )
            s_grad = swap(s_grad.reshape(mid, n_f, k).transpose(1, 0, 2), "frames")
            t_rows = jnp.zeros((n_r,) + t_grad[0].shape, BF)
            for j in range(n_r):
                t_rows = lax.dynamic_update_index_in_dim(t_rows, t_grad[j], ids[j], 0)
            weight_parts[u] = (s_grad, swap(ordered(t_rows, n_f), "frames"))
        d_norms[u] = (mid_sums, out_sums) if u > 0 or not ring else None

    ends_1 = sums_1.end() if ring else []
    grad_part, block_part = (own_frames, pixels, depth), (own_frames, pixels, cols)
    ends = run(
        functools.partial(last_body, dims=dims), [loaded(shape(grad_part, BF))] + [shape(grad_part, BF)] * (n_r - 1) + [shape(block_part, BF)] * n_r,
        [ids, ds, loaded(summed_grad), loaded(block), far(spatial_w[0])], "last",
        [*adjoint_scr, pltpu.VMEM((n_r, rows, cols), F32), pltpu.VMEM((1, rows, cols), F32), pltpu.VMEM((n_r,) + grad_part, BF),
         pltpu.VMEM((n_r,) + block_part, BF), w_scr, sems(())],
        limit=44, scalars=1, flops=spatial_flops, moved=8 * MIB, scale=1, after=ends_1[1:],
    )
    sent = ()
    state = [flip(a) for a in (spatial_weights, spatial_first, spatial_second)]
    state += [temporal_weights, temporal_first, temporal_second]
    if not ring:
        blocks, grads = traded(ends[n_r:]), traded(ends[:n_r])
    if ring:
        flats = from_group(flat)
        sums_0.add(ends[:1])
        blocks, grads = traded(ends[n_r:]), traded(ends[:n_r])
        norms = [mid_norm, mid_first, mid_second, out_norm, out_first, out_second]
        norms = run(
            norm_body, [shape(a.shape, F32) for a in norms], [ids, *flats, *norms], "norms",
            [pltpu.VMEM((n_r, 8, 512), F32)], scalars=1,
        )
        sent = sums_0.add([grads[1], norms[0]])
        weights = adam_unit(1, ends_1, state, None, "adam_1", sent)
        sent = sums_0.add([weights[0], *grads[2:]])
        weight_parts[0] = sums_0.end()
    block_out, input_grad = run(
        finish_body, [shape(frames_in.shape, BF), shape(frames_in.shape, F32)],
        [ids, *all_loaded(blocks + grads)], "finish", [pltpu.VMEM((own_frames, pixels, depth), F32)],
        scalars=1, moved=3 * MIB, after=sent,
    )
    if not ring:
        flat = jnp.concatenate([jnp.concatenate([m.reshape(-1), o.reshape(-1)]) for m, o in d_norms])
        flat = from_all(flat, "rep").reshape(n_r, units, -1)
        mid_grad = flat[:, :, : 2 * mid].reshape(n_r, units, 2, mid).transpose(1, 2, 0, 3)
        mid_grad = mid_grad.reshape(units, 2, n_r * mid)
        out_grad = flat[:, :, 2 * mid :].reshape(n_r, units, 2, cols).transpose(1, 2, 0, 3)
        out_grad = out_grad.reshape(units, 2, depth)
        norms = [*adam_step(mid_norm, mid_grad, mid_first, mid_second, RATE_NORM, 0.0)]
        norms += adam_step(out_norm, out_grad, out_first, out_second, RATE_NORM, 0.0)

    if ring:
        weights = adam_unit(0, weight_parts[0], state, weights, "adam_0")
        weights = [flip(a) for a in weights[:4]] + list(weights[4:])
    else:
        grads = [jnp.stack([jnp.sum(parts[i].astype(F32), axis=0) for parts in weight_parts]) for i in range(2)]
        news = adam_step(spatial_weights, flip(grads[0]), spatial_first, spatial_second, RATE_WEIGHT, DECAY)
        weights = [*news, news[0].astype(BF)]
        news = adam_step(temporal_weights, grads[1], temporal_first, temporal_second, RATE_WEIGHT, DECAY)
        weights += [*news, news[0].astype(BF)]
    return (block_out, input_grad, *weights, *norms)


def solution(mesh):
    by_frame = P(("frames", "rep"), None, None, None)
    by_block = P(None, "frames", "rep")
    placed = (by_frame, by_frame, P()) + (by_block,) * 6 + (P(),) * 6
    return jax.shard_map(
        on_device,
        mesh=mesh,
        in_specs=placed,
        out_specs=(by_frame, by_frame) + (by_block,) * 8 + (P(),) * 6,
        check_vma=False,
    )
```

```python
import functools

import jax
import jax.numpy as jnp
from jax import lax
from jax.experimental import pallas as pl
from jax.experimental.pallas import tpu as pltpu
from jax.sharding import PartitionSpec as P

STEP = 5
NORM_EPS = 1e-05
ADAM_EPS = 1e-08
BETA_ONE = 0.5
BETA_TWO = 0.5
RATE_WEIGHT = 0.015
RATE_NORM = 0.2
DECAY = 0.05
BF = jnp.bfloat16
F32 = jnp.float32
MIB = 1 << 20
VMEM = pl.BlockSpec(memory_space=pltpu.VMEM)
SMEM = pl.BlockSpec(memory_space=pltpu.SMEM)
LANES = 128
SCALE = 30
CHEAP = pl.CostEstimate(flops=1000, bytes_accessed=1000, transcendentals=0)
ANY = pl.BlockSpec(memory_space=pl.ANY)
HBM = pl.BlockSpec(memory_space=pltpu.HBM)


def shape(dims, dtype):
    return jax.ShapeDtypeStruct(tuple(dims), dtype)


class Placed:
    def __init__(self, value, where):
        self.value, self.where = value, where


def far(value):
    return Placed(value, "hbm")


def loaded(value):
    return Placed(value, "loaded")


def near(value):
    return Placed(value, "vmem")


def all_loaded(values):
    return [loaded(v) for v in values]


def in_hbm(array):
    return pltpu.with_memory_space_constraint(array, pltpu.HBM)


def operand(a):
    if not isinstance(a, Placed):
        return a
    return pltpu.with_memory_space_constraint(a.value, pltpu.VMEM if a.where == "vmem" else pltpu.HBM)


def result(a):
    if not isinstance(a, Placed):
        return a
    return (pltpu.VMEM if a.where == "vmem" else pltpu.HBM)(a.value.shape, a.value.dtype)


def is_far(a):
    return isinstance(a, Placed) and a.where == "hbm"


def run(body, outs, args, name, scratch=(), limit=28, scalars=0, flops=0, moved=0, after=(), scale=SCALE):
    def kernel(*refs):
        body(*refs[len(after) :])

    return pl.pallas_call(
        kernel,
        out_shape=tuple(result(o) for o in outs),
        in_specs=[ANY] * len(after) + [SMEM] * scalars + [ANY if is_far(a) else VMEM for a in args[scalars:]],
        out_specs=tuple(HBM if is_far(o) else VMEM for o in outs),
        scratch_shapes=list(scratch),
        compiler_params=pltpu.CompilerParams(vmem_limit_bytes=limit * MIB),
        cost_estimate=pl.CostEstimate(flops=int(scale * flops), bytes_accessed=int(scale * moved), transcendentals=0),
        name=name,
    )(*after, *[operand(a) for a in args])


def gate(value, after, name):
    return pl.pallas_call(
        lambda *refs: None,
        out_shape=shape(value.shape, value.dtype),
        in_specs=[ANY] * (len(after) + 1),
        out_specs=ANY,
        input_output_aliases={len(after): 0},
        name=name,
    )(*after, value)


def started(source, target, sem):
    copy = pltpu.make_async_copy(source, target, sem)
    copy.start()
    return copy


def padded(values, rows):
    return jnp.concatenate([values, jnp.zeros((rows - values.shape[0], values.shape[1]), F32)], axis=0)


def sigmoid(v):
    return 1.0 / (1.0 + jnp.exp(-v))


def silu(v):
    return v / (1.0 + jnp.exp(-v))


def silu_slope(v):
    s = sigmoid(v)
    return s * (1.0 + v * (1.0 - s))


def mm(a, b, dims):
    return lax.dot_general(a, b, (dims, ((), ())), preferred_element_type=F32)


def put_rows(out_ref, upper, lower):
    out_ref[:, 0:1, :] = jnp.broadcast_to(upper[None], (out_ref.shape[0],) + upper.shape)
    out_ref[:, 1:2, :] = jnp.broadcast_to(lower[None], (out_ref.shape[0],) + lower.shape)


def put_moments(values, out_ref):
    rows = values.shape[0]
    mean = jnp.sum(values, axis=0, keepdims=True) * (1.0 / rows)
    off = values - mean
    put_rows(out_ref, mean, jnp.sum(off * off, axis=0, keepdims=True))


def joined_moments(both, rows):
    count = both.shape[0]
    mean = jnp.sum(both[:, 0:1], axis=0) * (1.0 / count)
    off = both[:, 0:1] - mean[None]
    total = jnp.sum(both[:, 1:2] + rows * (off * off), axis=0)
    return mean, lax.rsqrt(total * (1.0 / (rows * count)) + NORM_EPS)


def put_sums(upstream, normed, out_ref):
    put_rows(out_ref, jnp.sum(upstream * normed, axis=0, keepdims=True), jnp.sum(upstream, axis=0, keepdims=True))


def convolve(pad, w_ref, turned, dims):
    height, width, frames, depth = dims
    rows = height * width * frames
    for k in range(9):
        i, j = k // 3, k % 3
        piece = pad[i : i + height, j : j + width].reshape(rows, depth).astype(BF)
        part = mm(w_ref[:, k * depth : (k + 1) * depth], piece, ((1,), (1,)))
        if k == 0:
            turned[...] = part
        else:
            turned[...] += part
    return turned[...].T


def widened(scr, values, before, after):
    frames = values.shape[1]
    scr[:, 8 : 8 + frames, :] = values
    scr[:, 7:8, :] = before
    scr[:, 8 + frames : 9 + frames, :] = after


RING = (0, 2, 4, 6, 7, 5, 3, 1)


def can_ring(mid, k, k_t, count):
    return count == len(RING) and mid == 288 and k == 576 and k_t == 432


def ring_place(frame):
    return jnp.where(frame % 2 == 0, frame // 2, 7 - frame // 2)


def ring_device(place):
    place = place % 8
    return jnp.where(place < 4, 2 * place, 15 - 2 * place)


def low_half(shape_):
    return lax.broadcasted_iota(jnp.int32, shape_, 1) < LANES // 2


def fold(top, bottom, out_ref, k):
    edge = k - LANES // 2
    out_ref[:, 0:edge] = top[:, 0:edge].astype(out_ref.dtype)
    mixed = jnp.where(low_half((top.shape[0], LANES)), top[:, edge : edge + LANES], bottom[:, 0:LANES])
    out_ref[:, edge : edge + LANES] = mixed.astype(out_ref.dtype)
    out_ref[:, edge + LANES : 2 * k] = bottom[:, LANES : k + LANES // 2].astype(out_ref.dtype)


def pack_body(ids_ref, w_ref, t_ref, *refs):
    outs, folded, scr = refs[:-2], refs[-2], refs[-1]
    mid, k = w_ref.shape[1:]
    half = mid // 2
    edge = k - LANES // 2
    odd = ids_ref[6] % 2 == 1
    low = low_half((half, LANES))

    @pl.when(jnp.logical_not(odd))
    def _():
        scr[:, 0:k] = w_ref[0]

    @pl.when(odd)
    def _():
        scr[:, 0:k] = w_ref[0]
        scr[...] = pltpu.roll(scr[...], k, 1)

    folded[0:half, 0:edge] = scr[0:half, 0:edge].astype(BF)
    folded[0:half, edge + LANES :] = scr[half:mid, 0:edge].astype(BF)
    upper, lower = scr[0:half, edge:], pltpu.roll(scr[half:mid, edge:], LANES // 2, 1)
    folded[0:half, edge : edge + LANES] = jnp.where(low != odd, upper, lower).astype(BF)
    rows = folded.shape[0] - half
    for i in range(2 * k // LANES):
        at = slice(i * LANES, (i + 1) * LANES)
        folded[half:, at] = t_ref[0, rows * i : rows * (i + 1), :].astype(BF)
    start = 0
    for out in outs:
        out[...] = folded[start : start + out.shape[0], :]
        start += out.shape[0]


def packed(u, ids, spatial, temporal, sizes):
    mid, k = spatial.shape[1:]
    flat = [pl.BlockSpec((n, 2 * k), lambda i: (0, 0)) for n in sizes]
    return pl.pallas_call(
        pack_body,
        grid=(1,),
        out_shape=[shape((n, 2 * k), BF) for n in sizes],
        in_specs=[SMEM] + [pl.BlockSpec((1,) + a.shape[1:], lambda i: (u, 0, 0)) for a in (spatial, temporal)],
        out_specs=flat,
        scratch_shapes=[pltpu.VMEM((sum(sizes), 2 * k), BF), pltpu.VMEM((mid, k + LANES // 2), F32)],
        compiler_params=pltpu.CompilerParams(vmem_limit_bytes=24 * MIB),
        name=f"pack_{u}",
    )(ids, in_hbm(spatial), in_hbm(temporal))


def unpack_temporal(f, slot, t_ref):
    rows = slot.shape[0]
    per = t_ref.shape[3] // rows
    for j in range(slot.shape[1] // LANES):
        block = 3 * f + j // per
        piece = slot[:, j * LANES : (j + 1) * LANES]
        t_ref[(block % 8) // 2, block // 8, block % 2, (j % per) * rows : (j % per + 1) * rows, :] = piece


def slots_of(refs, half):
    if len(refs[0].shape) == 3:
        return [([refs[0].at[i, 0:half]], refs[0].at[i, half:]) for i in range(8)], refs[1:]
    cut = half - refs[0].shape[0]
    return [([refs[i], refs[8 + i].at[0:cut]], refs[8 + i].at[cut:]) for i in range(8)], refs[16:]


def unpack_rows(ids_ref, slots, outs, scr):
    half = scr.shape[3]
    for i, (_, slot) in enumerate(slots):
        unpack_temporal(ids_ref[6 + i], slot, scr)
    for j, out_ref in enumerate(outs):
        for k in range(3):
            for part in range(2):
                out_ref[k, part * half : (part + 1) * half, :] = scr[ids_ref[j], k, part]


def unpack_spatial(ids_ref, slots, w_ref):
    half, k = w_ref.shape[0] // 2, w_ref.shape[1] // 8
    edge = k - LANES // 2
    low = low_half((half, LANES))
    for i, (slot, _) in enumerate(slots):
        f = ids_ref[6 + i]
        odd = f % 2
        base = (f // 2) * (2 * k)
        tiles = pl.ds(pl.multiple_of(base + odd * (edge + LANES), LANES), edge)
        middle = pl.ds(pl.multiple_of(base + edge, LANES), LANES)
        start = 0
        for part in slot:
            count = part.shape[0]
            w_ref[start : start + count, tiles] = part[:, 0:edge]
            w_ref[half + start : half + start + count, tiles] = part[:, edge + LANES :]
            start += count
        mixed = jnp.concatenate([part[:, edge : edge + LANES].astype(F32) for part in slot], axis=0)
        mine = low != (odd == 1)
        for rows, values in ((slice(0, half), mixed), (slice(half, 2 * half), pltpu.roll(mixed, LANES // 2, 1))):
            w_ref[rows, middle] = jnp.where(mine, values, w_ref[rows, middle].astype(F32)).astype(BF)


def spatial_body(*refs, dims, half, ring, first):
    height, width, frames, depth = dims
    rows = height * width * frames
    ids_ref, refs = refs[0], refs[1:]
    if ring:
        slots, refs = slots_of(refs, half)
    else:
        w_ref, refs = refs[0], refs[1:]
    refs = iter(refs)

    def take(count):
        return [next(refs) for _ in range(count)]

    sources = take(1 if first else 6)
    (s_ref,) = take(1) if not first else (None,)
    first_ref, last_ref, mom_ref, s_far = take(4)
    w_far, act_far, row_outs = take(int(ring)), take(int(not first)), take(4 * int(ring))
    pad, turned, sems = take(3)
    w_scr, act_scr, row_scr = take(int(ring)), take(int(not first)), take(int(ring))
    if first:
        (s_ref,) = take(1)

    copies = []
    if ring:
        w_ref = w_scr[0]
        unpack_spatial(ids_ref, slots, w_ref)
        copies.append(started(w_ref, w_far[0], sems.at[0]))
        unpack_rows(ids_ref, slots, row_outs, row_scr[0])
    pad[...] = jnp.zeros(pad.shape, F32)
    if first:
        pad[1 : height + 1, 1 : width + 1] = sources[0][...].astype(F32).reshape(dims)
    else:
        both_ref, norm_ref = sources[4:]
        for j, t_ref in enumerate(sources[:4]):
            b = ids_ref[j]
            mean, inverse = joined_moments(both_ref[:, b], rows)
            norm = norm_ref[b]
            y = (t_ref[...].astype(F32) - mean) * (inverse * norm[0:1]) + norm[1:2]
            a = silu(y)
            at = pl.ds(pl.multiple_of(b * LANES, LANES), LANES)
            act_scr[0][:, at] = padded(a, act_scr[0].shape[0]).astype(BF)
            pad[1 : height + 1, 1 : width + 1, :, at] = a.reshape(height, width, frames, LANES)
        copies.append(started(act_scr[0], act_far[0], sems.at[1]))
    s_ref[...] = convolve(pad, w_ref, turned, dims)
    copies.append(started(s_ref, s_far, sems.at[2]))
    values = s_ref[...]
    put_moments(values, mom_ref)
    grid = values.reshape(height * width, frames, values.shape[-1])
    first_ref[...] = grid[:, 0:1, :]
    last_ref[...] = grid[:, frames - 1 : frames, :]
    for copy in copies:
        copy.wait()


def temporal_body(
    ids_ref, s_ref, both_ref, before_ref, after_ref, norm_ref, keep_ref, w0, w1, w2, w3,
    send_ref, kept_ref, stat_ref, win_far, row_far, scr, part, win_ref, row_ref, sems, s_scr=None, *, dims
):
    height, width, frames, depth = dims
    pixels = height * width
    rows = pixels * frames
    mid = s_ref.shape[-1]
    if s_scr is not None:
        arriving = started(s_ref, s_scr, sems.at[2])
    for j, w_ref in enumerate((w0, w1, w2, w3)):
        row_ref[:, :, pl.ds(pl.multiple_of(ids_ref[j] * LANES, LANES), LANES)] = w_ref[...]
    copies = [started(row_ref, row_far, sems.at[0])]
    mean, inverse = joined_moments(both_ref[...], rows)
    stat_ref[0:1, :] = mean
    stat_ref[1:2, :] = inverse
    scale, bias = inverse * norm_ref[0:1], norm_ref[1:2]

    def active(v):
        return silu((v - mean) * scale + bias)

    if s_scr is not None:
        arriving.wait()
        s_ref = s_scr
    middle = active(s_ref[...])
    widened(
        scr, middle.reshape(pixels, frames, mid),
        active(before_ref[...].reshape(pixels, mid)).reshape(pixels, 1, mid),
        active(after_ref[...].reshape(pixels, mid)).reshape(pixels, 1, mid),
    )
    whole = win_ref.shape[1]
    earlier = (scr[:, 7 : 7 + frames, :] * keep_ref[0][None]).reshape(rows, mid)
    later = (scr[:, 9 : 9 + frames, :] * keep_ref[1][None]).reshape(rows, mid)
    for i, values in enumerate((earlier, middle, later)):
        win_ref[i] = padded(values, whole).astype(BF)
    copies.append(started(win_ref, win_far, sems.at[1]))
    part[...] = mm(win_ref[0], row_ref[0], ((1,), (0,)))
    part[...] += mm(win_ref[1], row_ref[1], ((1,), (0,)))
    part[...] += mm(win_ref[2], row_ref[2], ((1,), (0,)))
    put_halves(ids_ref, part, send_ref, kept_ref)
    for copy in copies:
        copy.wait()


def put_halves(ids_ref, part, send_ref, kept_ref):
    core = ids_ref[4]
    rows = send_ref.shape[1]
    for i in range(2):
        other = pl.multiple_of((2 * i + 1 - core) * LANES, LANES)
        own = pl.multiple_of((2 * i + core) * LANES, LANES)
        send_ref[i] = part[0:rows, pl.ds(other, LANES)].astype(BF)
        kept_ref[i] = part[0:rows, pl.ds(own, LANES)]


def total_body(ids_ref, got_ref, kept_ref, last_ref, t_ref, low_ref, mom_ref):
    x = ids_ref[5]
    t = got_ref[x].astype(F32) + kept_ref[x] + last_ref[...].astype(F32)
    t_ref[...] = t
    low_ref[...] = t.astype(BF)
    put_moments(t, mom_ref)


def edges_body(*refs, dims):
    height, width, frames, depth = dims
    blocks, (first_ref, last_ref, scr) = refs[:-3], refs[-3:]
    pixels = height * width
    slot = scr.shape[0] // len(blocks)
    for out_ref, at in ((first_ref, 0), (last_ref, frames - 1)):
        for j, ref in enumerate(blocks):
            grid = ref[...].astype(F32).reshape(pixels, frames, LANES)
            scr[slot * j : slot * j + pixels, :] = grid[:, at : at + 1, :].reshape(pixels, LANES)
        out_ref[...] = scr[...].astype(BF)


def top_body(ids_ref, t_ref, both_ref, norm_ref, x_ref, cot_ref, block_ref, g_ref, low_ref, sums_ref):
    rows = t_ref.shape[0]
    b = ids_ref[0]
    mean, inverse = joined_moments(both_ref[:, b], rows)
    norm = norm_ref[b]
    normed = (t_ref[...] - mean) * inverse
    own = pl.ds(pl.multiple_of(b * LANES, LANES), LANES)
    summed = normed * norm[0:1] + norm[1:2] + x_ref[:, own].astype(F32)
    block_ref[...] = silu(summed).astype(BF)
    g = cot_ref[...].astype(F32) * silu_slope(summed)
    g_ref[...] = g
    low_ref[...] = g.astype(BF)
    put_sums(g, normed, sums_ref)


def below_body(ids_ref, got_ref, kept_ref, last_ref, t_ref, both_ref, norm_ref, low_ref, sums_ref):
    rows = t_ref.shape[0]
    b, x = ids_ref[0], ids_ref[5]
    d_act = got_ref[x].astype(F32) + kept_ref[x] + last_ref[...].astype(F32)
    mean, inverse = joined_moments(both_ref[:, b], rows)
    norm = norm_ref[b]
    normed = (t_ref[...] - mean) * inverse
    g = d_act * silu_slope(normed * norm[0:1] + norm[1:2])
    low_ref[...] = g.astype(BF)
    put_sums(g, normed, sums_ref)


def dt_body(
    ids_ref, g0, g1, g2, g3, t0, t1, t2, t3, both_ref, sums_ref, norm_ref, dt_ref, coef_ref, sum_ref, *, total
):
    rows, whole = g0.shape[0], dt_ref.shape[0]
    for j, (g_ref, t_ref) in enumerate(((g0, t0), (g1, t1), (g2, t2), (g3, t3))):
        b = ids_ref[j]
        mean, inverse = joined_moments(both_ref[:, b], rows)
        sums = jnp.sum(sums_ref[:, b], axis=0)
        if j == 0:
            sum_ref[...] = sums
        c1 = norm_ref[b][0:1] * inverse
        c2 = c1 * sums[1:2] * (1.0 / total)
        c3 = c1 * inverse * sums[0:1] * (1.0 / total)
        coef_ref[j] = jnp.concatenate([c1, c2, c3, mean], axis=0)
        d = c1 * g_ref[...].astype(F32) - c2 - c3 * (t_ref[...].astype(F32) - mean)
        dt_ref[:, pl.ds(pl.multiple_of(b * LANES, LANES), LANES)] = padded(d, whole).astype(BF)


def temporal_grad_body(ids_ref, win_ref, dt_ref, *refs):
    outs, term = refs[:-1], refs[-1]
    mid = win_ref.shape[-1]
    dt = dt_ref[...]
    for k in range(3):
        term[...] = mm(win_ref[k], dt, ((0,), (0,)))
        for j, out_ref in enumerate(outs):
            at = pl.ds(pl.multiple_of(ids_ref[j] * LANES, LANES), LANES)
            out_ref[k * mid : (k + 1) * mid, :] = term[:, at].astype(BF)


def middle_body(
    ids_ref, dt_ref, coef_ref, before_ref, after_ref, keep_ref, stat_ref, norm_ref, row_far, s_far,
    d_far, sums_ref, scr, row_ref, s_ref, d_ref, sems, *, dims
):
    height, width, frames, depth = dims
    pixels = height * width
    rows = pixels * frames
    copies = [started(row_far, row_ref, sems.at[0]), started(s_far, s_ref, sems.at[1])]
    before, after = before_ref[...].astype(F32), after_ref[...].astype(F32)
    slot = before.shape[0] // 8
    dt = dt_ref[...]
    scr[:, 8 : 8 + frames, :] = dt.astype(F32)[0:rows].reshape(pixels, frames, depth)
    for j in range(4):
        at = pl.ds(pl.multiple_of(ids_ref[j] * LANES, LANES), LANES)
        c = coef_ref[j]

        def halo(frame):
            g, t = (frame[slot * b : slot * b + pixels] for b in (j, 4 + j))
            d = c[0:1] * g - c[1:2] - c[2:3] * (t - c[3:4])
            return d.astype(BF).astype(F32).reshape(pixels, 1, LANES)

        scr[:, 7:8, at] = halo(before)
        scr[:, 8 + frames : 9 + frames, at] = halo(after)
    later = (scr[:, 9 : 9 + frames, :] * keep_ref[1][None]).reshape(rows, depth).astype(BF)
    earlier = (scr[:, 7 : 7 + frames, :] * keep_ref[0][None]).reshape(rows, depth).astype(BF)
    copies[0].wait()
    d_ref[...] = mm(later, row_ref[0], ((1,), (1,)))
    d_ref[...] += mm(dt, row_ref[1], ((1,), (1,)))[0:rows]
    d_ref[...] += mm(earlier, row_ref[2], ((1,), (1,)))
    copies[1].wait()
    normed = (s_ref[...] - stat_ref[0:1]) * stat_ref[1:2]
    d = d_ref[...] * silu_slope(normed * norm_ref[0:1] + norm_ref[1:2])
    d_ref[...] = d
    leaving = started(d_ref, d_far, sems.at[2])
    put_sums(d, normed, sums_ref)
    leaving.wait()


def spatial_grad(d_ref, s_ref, stat_ref, norm_ref, sums_ref, ds_ref, sum_ref, total):
    sums = jnp.sum(sums_ref[...], axis=0)
    sum_ref[...] = sums
    inverse = stat_ref[1:2]
    normed = (s_ref[...] - stat_ref[0:1]) * inverse
    d = d_ref[...] - sums[1:2] * (1.0 / total) - normed * (sums[0:1] * (1.0 / total))
    ds_ref[...] = (norm_ref[0:1] * inverse * d).astype(BF)


def adjoint(ds_ref, w_ref, pad, patches, stacked, dims):
    height, width, frames, depth = dims
    rows, mid = ds_ref.shape
    whole = mid // LANES * LANES
    rest = mid - whole
    start = 9 * whole
    pad[...] = jnp.zeros(pad.shape, F32)
    pad[1 : height + 1, 1 : width + 1, :, 0:mid] = ds_ref[...].astype(F32).reshape(height, width, frames, mid)
    lane = lax.broadcasted_iota(jnp.int32, (rows, LANES), 1)
    tails = [jnp.zeros((rows, LANES), F32) for _ in range((patches.shape[1] - start) // LANES)]
    stacked[start:, :] = jnp.zeros((stacked.shape[0] - start, depth), BF)
    for k in range(9):
        i, j = k // 3, k % 3
        piece = pad[2 - i : 2 - i + height, 2 - j : 2 - j + width].reshape(rows, pad.shape[-1])
        w = w_ref[:, k * depth : (k + 1) * depth]
        patches[:, k * whole : (k + 1) * whole] = piece[:, 0:whole].astype(BF)
        stacked[k * whole : (k + 1) * whole, :] = w[0:whole]
        stacked[start + k * rest : start + (k + 1) * rest, :] = w[whole:mid]
        tile, at = divmod(k * rest, LANES)
        tail = pltpu.roll(piece[:, whole:], at, 1) if at else piece[:, whole:]
        tails[tile] = jnp.where((lane >= at) & (lane < at + rest), tail, tails[tile])
    for tile, tail in enumerate(tails):
        patches[:, start + tile * LANES : start + (tile + 1) * LANES] = tail.astype(BF)
    return mm(patches[...], stacked[...], ((1,), (0,)))


def input_body(
    ids_ref, d_far, stat_ref, norm_ref, sums_ref, s_far, w_far,
    ds_ref, send_ref, kept_ref, sum_ref, pad, patches, stacked, part, s_ref, d_ref, w_ref, sems, *, dims, total
):
    height, width, frames, depth = dims
    copies = [started(s_far, s_ref, sems.at[0]), started(w_far, w_ref, sems.at[1]), started(d_far, d_ref, sems.at[2])]
    copies[0].wait()
    copies[2].wait()
    spatial_grad(d_ref, s_ref, stat_ref, norm_ref, sums_ref, ds_ref, sum_ref, total)
    copies[1].wait()
    part[...] = adjoint(ds_ref, w_ref, pad, patches, stacked, dims)
    put_halves(ids_ref, part, send_ref, kept_ref)


def by_frame(source, out_ref, dims):
    height, width, frames, depth = dims
    pixels, own = height * width, out_ref.shape[1]
    for r in range(source.shape[0]):
        for f in range(frames):
            values = source[r, pl.ds(f, pixels, stride=frames), :]
            out_ref[f // own, f % own, :, r * LANES : (r + 1) * LANES] = values.astype(out_ref.dtype)


def last_body(ids_ref, ds_ref, g_ref, block_ref, w_far, *refs, dims):
    grads, blocks, refs = refs[:4], refs[4:8], refs[8:]
    pad, patches, stacked, part, block, grad_scr, block_scr, w_ref, sem = refs
    height, width, frames, depth = dims
    copy = started(w_far, w_ref, sem)
    rows = block_ref.shape[0]
    block[0, 0:rows] = block_ref[...].astype(F32)
    by_frame(block, block_scr, dims)
    copy.wait()
    terms = adjoint(ds_ref, w_ref, pad, patches, stacked, dims)
    own = ids_ref[0]
    for r in range(part.shape[0]):
        part[r, 0:rows] = terms[:, r * LANES : (r + 1) * LANES]
    part[own, 0:rows] = part[own, 0:rows] + g_ref[...]
    by_frame(part, grad_scr, dims)
    for j in range(4):
        grads[j][...] = grad_scr[ids_ref[j]]
        blocks[j][...] = block_scr[ids_ref[j]]


def finish_body(ids_ref, *refs):
    blocks, grads, (out_ref, grad_out_ref, block) = refs[:4], refs[4:8], refs[8:]
    own, height, width, depth = out_ref.shape
    for j, ref in enumerate(blocks):
        block[:, :, pl.ds(pl.multiple_of(ids_ref[j] * LANES, LANES), LANES)] = ref[...].astype(F32)
    for f in range(own):
        grad = sum(ref[f].astype(F32) for ref in grads)
        for h in range(height):
            at = slice(h * width, (h + 1) * width)
            out_ref[f, h] = block[f, at].astype(BF)
            grad_out_ref[f, h] = grad[at]


def weight_terms(act_ref, ds_ref, pad, acc, dims):
    height, width, frames, depth = dims
    rows = height * width * frames
    pad[...] = jnp.zeros(pad.shape, F32)
    pad[1 : height + 1, 1 : width + 1] = act_ref[...].astype(F32)[0:rows].reshape(dims)
    flipped = ds_ref[...].astype(F32).T.astype(BF)

    for k in range(9):
        i, j = k // 3, k % 3
        piece = pad[i : i + height, j : j + width].reshape(rows, depth).astype(BF)
        acc[:, k * depth : (k + 1) * depth] = mm(flipped, piece, ((1,), (0,)))


def put_shards(acc, places, out_ref, k, then):
    mid = acc.shape[0]
    half = mid // 2
    wide = k + LANES // 2
    for f in range(8):
        if f % 2 == 0:
            top = acc[0:half, k * f : k * f + wide]
            bottom = pltpu.roll(acc[half:mid, k * f : k * f + wide], LANES // 2, 1)
        else:
            start = k * f - LANES // 2
            top = pltpu.roll(acc[0:half, start : start + wide], k, 1)
            bottom = acc[half:mid, start : start + wide]
        fold(top, bottom, out_ref.at[places[f], 0:half], k)
        then(f)


def weight_plain_body(act_ref, ds_ref, out_ref, pad, acc, *, dims):
    weight_terms(act_ref, ds_ref, pad, acc, dims)
    out_ref[...] = acc[...].astype(BF)


def put_temporal(ids_ref, sources, out_ref, half):
    rows = out_ref.shape[1] - half
    per = half // rows
    for i, source in enumerate(sources):
        for tap in range(3):
            for part in range(2):
                block = tap * 8 + ids_ref[i] * 2 + part
                place = ids_ref[14 + block // 3]
                for j in range(per):
                    start = tap * 2 * half + part * half + j * rows
                    at = pl.multiple_of(((block % 3) * per + j) * LANES, LANES)
                    out_ref[place, half:, pl.ds(at, LANES)] = source[start : start + rows, :]


def put_terms(ids_ref, act_ref, ds_ref, t_refs, out_far, ahead_ref, back_ref, pad, acc, out_ref, sems, dims):
    weight_terms(act_ref, ds_ref, pad, acc, dims)
    places = [ids_ref[14 + f] for f in range(8)]
    put_temporal(ids_ref, t_refs, out_ref, acc.shape[0] // 2)
    copies = []
    put_shards(
        acc, places, out_ref, acc.shape[1] // 8,
        lambda f: copies.append(started(out_ref.at[places[f]], out_far.at[places[f]], sems.at[f])),
    )
    ahead_ref[...] = out_ref[4]
    back_ref[...] = out_ref[5]
    for copy in copies:
        copy.wait()


def weight_body(
    ids_ref, act_ref, ds_ref, t0, t1, t2, t3, out_far, ahead_ref, back_ref, token_ref, pad, acc, out_ref, sems, *, dims
):
    token_ref[...] = jnp.zeros(token_ref.shape, F32)
    put_terms(ids_ref, act_ref, ds_ref, (t0, t1, t2, t3), out_far, ahead_ref, back_ref, pad, acc, out_ref, sems, dims)


def weight_first_body(
    ids_ref, d_ref, stat_ref, norm_ref, sums_ref, mid_ref, out_1_ref, out_0_ref, t0, t1, t2, t3, s_ref, act_ref,
    ds_ref, flat_ref, out_far, ahead_ref, back_ref, sum_ref, pad, acc, out_ref, sems, *, dims, total
):
    spatial_grad(d_ref, s_ref, stat_ref, norm_ref, sums_ref, ds_ref, sum_ref, total)
    flat_ref[...] = jnp.zeros(flat_ref.shape, F32)
    for i, ref in enumerate((sum_ref, mid_ref, out_0_ref, out_1_ref)):
        flat_ref[2 * i : 2 * i + 2, 0 : ref.shape[1]] = ref[...]
    put_terms(ids_ref, act_ref, ds_ref, (t0, t1, t2, t3), out_far, ahead_ref, back_ref, pad, acc, out_ref, sems, dims)


def norm_body(ids_ref, f0, f1, f2, f3, *refs):
    refs, flat_ref = refs[:-1], refs[-1]
    for j, ref in enumerate((f0, f1, f2, f3)):
        flat_ref[ids_ref[j]] = ref[...]
    count = flat_ref.shape[0]
    for which in range(2):
        old, new = refs[3 * which : 3 * which + 3], refs[6 + 3 * which : 9 + 3 * which]
        width = old[0].shape[-1] // count
        for u in range(2):
            row = 4 * which + 2 * u
            grad = jnp.concatenate([flat_ref[r, row : row + 2, 0:width] for r in range(count)], axis=1)
            values = adam_step(old[0][u], grad, old[1][u], old[2][u], RATE_NORM, 0.0)
            for ref, value in zip(new, values):
                ref[u] = value


def adam_step(param, gradient, moment_one, moment_two, rate, decay):
    first_new = BETA_ONE * moment_one + (1.0 - BETA_ONE) * gradient
    second_new = BETA_TWO * moment_two + (1.0 - BETA_TWO) * gradient * gradient
    fix_one = 1.0 - BETA_ONE**STEP
    fix_two = 1.0 - BETA_TWO**STEP
    update = first_new / fix_one / (jnp.sqrt(second_new / fix_two) + ADAM_EPS)
    return (param - rate * (update + decay * param), first_new, second_new)


def adam_into(grad, refs, outs, rows):
    new, first, second = adam_step(refs[0][0, rows], grad, refs[1][0, rows], refs[2][0, rows], RATE_WEIGHT, DECAY)
    outs[0][0, rows] = new
    outs[1][0, rows] = first
    outs[2][0, rows] = second
    outs[3][0, rows] = new.astype(BF)


def adam_body(*refs, grads):
    sources, refs = refs[:grads], refs[grads:]
    refs, outs = refs[:6], refs[-8:]
    half = refs[0].shape[1] // 2
    summed = sources[0][0].astype(F32) + sum(r[...].astype(F32) for r in sources[1:])
    temporal = summed[half:]
    rows = temporal.shape[0]
    for i in range(temporal.shape[1] // LANES):
        piece = temporal[:, i * LANES : (i + 1) * LANES]
        adam_into(piece, refs[3:], outs[4:], slice(i * rows, (i + 1) * rows))
    spatial = summed[0:half]
    k = spatial.shape[1] // 2
    edge = k - LANES // 2
    adam_into(spatial[:, 0:k], refs, outs, slice(0, half))
    adam_into(pltpu.roll(spatial[:, edge:], k, 1)[:, 0:k], refs, outs, slice(half, 2 * half))


def adam_unit(u, sources, state, before, name, after=()):
    unit = [pl.BlockSpec((1,) + a.shape[1:], lambda i: (u, 0, 0)) for a in state]
    types = [F32, F32, F32, BF]
    outs = [shape(state[0].shape, t) for t in types] + [shape(state[3].shape, t) for t in types]
    before = list(before or ())
    whole = [pl.BlockSpec((1,) * (a.ndim - 2) + a.shape[-2:], lambda i, n=a.ndim: (0,) * n) for a in sources]

    def kernel(*refs):
        adam_body(*refs[len(after) :], grads=len(sources))

    return pl.pallas_call(
        kernel,
        grid=(1,),
        out_shape=tuple(outs),
        in_specs=[pl.BlockSpec(memory_space=pl.ANY)] * len(after) + whole + unit + [pl.BlockSpec(memory_space=pl.ANY)] * len(before),
        out_specs=tuple([unit[0]] * 4 + [unit[3]] * 4),
        input_output_aliases={len(after) + len(sources) + 6 + i: i for i in range(len(before))},
        compiler_params=pltpu.CompilerParams(vmem_limit_bytes=40 * MIB),
        cost_estimate=CHEAP,
        name=name,
    )(*after, *[in_hbm(a) for a in [*sources, *state]], *before)


def swap(parts, axis):
    return lax.all_to_all(parts, axis, 0, 0, tiled=True)


def from_all(value, axis):
    count = lax.axis_size(axis)
    return swap(jnp.broadcast_to(value[None], (count,) + value.shape), axis)


def across(value, bit):
    count = lax.axis_size("rep")
    return lax.ppermute(value, "rep", [(i, i ^ bit) for i in range(count)])


MASKS = (0, 2, 1, 3)


def traded(parts):
    return [part if mask == 0 else across(part, mask) for part, mask in zip(parts, MASKS)]


def from_group(value, after=None):
    distant = across(value, 2)
    beside = across(value, 1)
    if after is not None:
        distant = gate(distant, after, "then")
    return value, distant, beside, across(distant, 1)


def neighbours(first, last):
    count = lax.axis_size("frames")
    before = lax.ppermute(last, "frames", [(i, i + 1) for i in range(count - 1)])
    after = lax.ppermute(first, "frames", [(i + 1, i) for i in range(count - 1)])
    return before, after


def along(step):
    return [(RING[i], RING[(i + step) % 8]) for i in range(8)]


def ring_gather(chunks, after):
    ahead, back = [[c] for c in chunks], [[c] for c in chunks]
    for step in range(3):
        if step == 2:
            ahead[-1][-1] = gate(ahead[-1][-1], after, "hop_then")
        for a, b in zip(ahead, back):
            a.append(lax.ppermute(a[-1], "frames", along(1)))
            b.append(lax.ppermute(b[-1], "frames", along(-1)))
    last = lax.ppermute(ahead[0][-1], "frames", along(1)), lax.ppermute(back[1][-1], "frames", along(-1))
    return [piece for a, b, far_piece in zip(ahead, back, last) for piece in [*a, far_piece, *b[1:]]]


def added(gots, parts, places, after, name):
    count = len(gots)

    def body(*refs):
        refs, token_ref = refs[len(after) : -1], refs[-1]
        token_ref[...] = jnp.zeros(token_ref.shape, F32)
        for got_ref, part_ref, out_ref in zip(refs[:count], refs[count : 2 * count], refs[2 * count :]):
            out_ref[...] = (got_ref[...].astype(F32) + part_ref[0].astype(F32)).astype(BF)

    flat = pl.BlockSpec(gots[0].shape, lambda g: (0, 0))
    part_specs = [pl.BlockSpec((1,) + gots[0].shape, lambda g, i=i: (i, 0, 0)) for i in places]
    return pl.pallas_call(
        body,
        grid=(1,),
        out_shape=[shape(g.shape, BF) for g in gots] + [shape((8, LANES), F32)],
        in_specs=[ANY] * len(after) + [flat] * count + part_specs,
        out_specs=[flat] * count + [pl.BlockSpec((8, LANES), lambda g: (0, 0))],
        cost_estimate=CHEAP,
        name=name,
    )(*after, *[in_hbm(g) for g in gots], *[in_hbm(parts)] * count)


def ring_step(ahead, back):
    return lax.ppermute(ahead, "frames", along(1)), lax.ppermute(back, "frames", along(-1))


class RingSums:
    def __init__(self, parts, ahead, back, name):
        self.parts, self.ahead, self.back, self.name = parts, ahead, back, name
        self.step = 0

    def add(self, after=()):
        self.step += 1
        step, after, name = self.step, list(after), f"{self.name}_{self.step}"
        if step < 3:
            gots = ring_step(self.ahead, self.back)
            self.ahead, self.back, token = added(gots, self.parts, (4 - step, 5 + step), after, name)
        else:
            gots = [lax.ppermute(self.ahead, "frames", along(1))]
            self.ahead, token = added(gots, self.parts, (4 - step,), after, name)
        return [token]

    def end(self):
        return [self.parts, *ring_step(self.ahead, self.back)]


def reduced(send, kept, x):
    got = across(send, 1)
    away = lax.dynamic_index_in_dim(got, 1 - x, 0, False).astype(F32)
    away = away + lax.dynamic_index_in_dim(kept, 1 - x, 0, False)
    return got, kept, across(away.astype(BF), 2)


def ordered(t_grad, count):
    n_r, rows, cols = t_grad.shape
    return t_grad.reshape(n_r, 3, rows // 3, cols).transpose(1, 0, 2, 3).reshape(count, -1, cols)


def sum_over(parts, axis):
    return jnp.sum(swap(parts, axis).astype(F32), axis=0)


def on_device(
    frames_in, cotangent, lengths,
    spatial_weights, spatial_first, spatial_second,
    temporal_weights, temporal_first, temporal_second,
    mid_norm, mid_first, mid_second,
    out_norm, out_first, out_second,
):
    own_frames, height, width, depth = frames_in.shape
    n_f, n_r = lax.axis_size("frames"), lax.axis_size("rep")
    assert n_r == 4 and depth == n_r * LANES
    me = lax.axis_index("rep")
    frames = own_frames * n_r
    pixels = height * width
    rows = pixels * frames
    total = float(rows * n_f)
    dims = (height, width, frames, depth)
    units, k, mid = spatial_weights.shape
    cols = LANES
    everyone = ("frames", "rep")
    k_t = temporal_weights.shape[1]
    ring = can_ring(mid, k, k_t, n_f)
    spatial_flops = 2 * rows * 9 * depth * mid
    temporal_flops = 2 * rows * 3 * depth * mid
    pad = pltpu.VMEM((height + 2, width + 2, frames, depth), F32)
    flip = functools.partial(jnp.swapaxes, axis1=1, axis2=2)
    ids = [me, me ^ 2, me ^ 1, me ^ 3, me & 1, me >> 1]
    if ring:
        place = ring_place(lax.axis_index("frames"))
        in_order = jnp.stack(ids + [jnp.int32(f) for f in (*range(8), *range(8))]).astype(jnp.int32)
        ids += [ring_device(place + i) for i in (0, -1, -2, -3, -4, 1, 2, 3)]
        ids += [(ring_place(jnp.int32(f)) - place) % 8 for f in range(8)]
    ids = jnp.stack(ids).astype(jnp.int32)

    frame_ids = lax.axis_index("frames") * frames + jnp.arange(frames, dtype=jnp.int32)
    clip_ends = jnp.cumsum(lengths)
    starts = jnp.concatenate([jnp.zeros((1,), jnp.int32), clip_ends[:-1]])
    opening = jnp.any(frame_ids[:, None] == starts[None, :], axis=1)
    closing = jnp.any((frame_ids + 1)[:, None] == clip_ends[None, :], axis=1)
    keep = jnp.where(jnp.stack([opening, closing]), 0.0, 1.0).astype(F32)[:, :, None]

    act = lax.all_gather(frames_in, "rep", axis=0, tiled=True).transpose(1, 2, 0, 3).reshape(rows, depth)
    cot = cotangent.reshape(own_frames, pixels, n_r, cols).transpose(2, 0, 1, 3)
    cot = swap(cot, "rep").reshape(frames, pixels, cols).transpose(1, 0, 2).reshape(rows, cols)

    mid_own = lax.dynamic_slice_in_dim(mid_norm, me * mid, mid, axis=2)
    out_split = out_norm.reshape(units, 2, n_r, cols).transpose(0, 2, 1, 3)

    slots, temporal_w = [], []

    if ring:
        wire = shape((mid // 2 + k_t * LANES // (2 * k), 2 * k), BF)
        chunks = packed(0, ids, flip(spatial_weights), temporal_weights, (wire.shape[0] // 2, wire.shape[0] // 2))
        held = ring_gather(chunks, [act, cot])
        slots.append((ids, held))
        (wire_1,) = packed(1, ids, flip(spatial_weights), temporal_weights, wire.shape[:1])
        wire_1 = gate(wire_1, [held[3], held[15]], "wire_then")
        slots.append((in_order, [lax.all_gather(wire_1, "frames", axis=0)]))
    else:
        wire = flip(spatial_weights).astype(BF)
        temporal_low = temporal_weights.astype(BF)
        for u in range(units):
            held = lax.all_gather(wire[u], "frames", axis=0)
            slots.append((ids, [held.transpose(1, 0, 2).reshape(mid, n_f * k)]))
            shard = lax.all_gather(temporal_low[u], "frames", axis=0, tiled=True)
            shard = shard.reshape(3, n_r, mid, cols).transpose(1, 0, 2, 3)
            temporal_w.append(traded([lax.dynamic_index_in_dim(shard, ids[j], 0, False) for j in range(n_r)]))

    rows_16 = -(-rows // 16) * 16
    halo = shape((pixels, 1, mid), F32)
    column = shape((rows, cols), BF)
    s_shape, w_shape = shape((rows, mid), F32), shape((mid, n_f * k), BF)
    act_shape = shape((rows_16, depth), BF)
    win_shape, row_shape = shape((3, rows_16, mid), BF), shape((3, mid, depth), BF)
    s_scr, w_scr = pltpu.VMEM(s_shape.shape, F32), pltpu.VMEM(w_shape.shape, BF)
    sems = pltpu.SemaphoreType.DMA
    saved, spatial_w = [], []
    for u in range(units):
        order, held = slots[u]
        sources = [loaded(act)] if u == 0 else [loaded(t_group[0]), *t_group[1:], loaded(both), out_split[u - 1]]
        outs = [s_shape] * (u > 0) + [halo, halo, shape((n_f, 2, mid), F32), far(s_shape)]
        outs += [far(w_shape)] * ring + [far(act_shape)] * (u > 0) + [shape((3, mid, cols), BF)] * (n_r * ring)
        parts = run(
            functools.partial(spatial_body, dims=dims, half=mid // 2, ring=ring, first=u == 0), outs,
            [order, *all_loaded(held), *sources], f"spatial_{u}",
            [pad, pltpu.VMEM((mid, rows), F32), sems((3,))] + [w_scr] * ring + [pltpu.VMEM(act_shape.shape, BF)] * (u > 0)
            + [pltpu.VMEM((n_r, 3, 2, mid // 2, cols), BF)] * ring + [s_scr] * (u == 0),
            scalars=1, flops=spatial_flops, moved=8 * MIB,
            after=[cot, keep, mid_own, out_split] if u == 0 else (),
        )
        spatial = parts[: int(u > 0)]
        first, last, mom, s_far, *more = parts[int(u > 0) :]
        spatial_w.append(more.pop(0) if ring else held[0])
        if u > 0:
            act = more.pop(0)
        if ring:
            temporal_w.append(traded(more))
        mid_both = swap(mom, "frames")
        before, after = neighbours(first, last)
        send, kept, stat, window, row_w = run(
            functools.partial(temporal_body, dims=dims),
            [shape((2, rows, cols), BF), shape((2, rows, cols), F32), shape((2, mid), F32), far(win_shape), far(row_shape)],
            [ids, *(spatial or [far(s_far)]), mid_both, before, after, mid_own[u], keep, *temporal_w[u]], f"temporal_{u}",
            [pltpu.VMEM((pixels, frames + 16, mid), F32), pltpu.VMEM((rows_16, depth), F32),
             pltpu.VMEM(win_shape.shape, BF), pltpu.VMEM(row_shape.shape, BF), sems((3,))] + [s_scr] * (u == 0),
            scalars=1, flops=temporal_flops, moved=8 * MIB,
        )
        t, low, mom = run(
            total_body, [loaded(shape((rows, cols), F32)), column, shape((n_f * n_r, 2, cols), F32)],
            [ids, *reduced(send, kept, me >> 1)], f"total_{u}", scalars=1, moved=3 * MIB,
        )
        both = swap(mom, everyone).reshape(n_f, n_r, 2, cols)
        t_group = from_group(low, [both] if u + 1 < units else None)
        saved.append((act, s_far, stat, window, row_w, t, t_group, both))

    wide = -(-mid // LANES) * LANES
    deep = 9 * (mid // LANES * LANES) + -(-9 * (mid % LANES) // LANES) * LANES
    adjoint_scr = [
        pltpu.VMEM((height + 2, width + 2, frames, wide), F32), pltpu.VMEM((rows, deep), BF), pltpu.VMEM((deep, depth), BF)
    ]
    d_norms = [None] * units
    weight_parts = [None] * units
    token, sums_1 = None, None
    for u in reversed(range(units)):
        act, s_far, stat, window, row_w, t, t_group, both = saved[u]
        if u == units - 1:
            block, summed_grad, low, sums = run(
                top_body, [loaded(column), loaded(shape((rows, cols), F32)), column, shape((n_f * n_r, 2, cols), F32)],
                [ids, loaded(t), loaded(both), out_split[u], loaded(saved[0][0]), loaded(cot)], "top", scalars=1, moved=3 * MIB,
            )
        else:
            low, sums = run(
                below_body, [column, shape((n_f * n_r, 2, cols), F32)],
                [ids, *reduced(send, kept, me >> 1), loaded(t), loaded(both), out_split[u]], f"below_{u}", scalars=1, moved=3 * MIB,
                after=[token] if ring else (),
            )
        done = sums_1.add([sums]) if sums_1 is not None else []
        sums = swap(sums, everyone).reshape(n_f, n_r, 2, cols)
        g_group = from_group(low, [sums, *done])
        edge = (2 * n_r * (-(-pixels // 8) * 8), cols)
        edges = neighbours(*run(
            functools.partial(edges_body, dims=dims), [shape(edge, BF)] * 2, [*g_group, *all_loaded(t_group)],
            f"edges_{u}", [pltpu.VMEM(edge, F32)]))
        dt, coef, out_sums = run(
            functools.partial(dt_body, total=total),
            [shape((rows_16, depth), BF), shape((n_r, 4, cols), F32), shape((2, cols), F32)],
            [ids, *g_group, *all_loaded(t_group), loaded(both), loaded(sums), out_split[u]], f"dt_{u}", scalars=1, moved=4 * MIB,
        )
        done = sums_1.add([coef]) if sums_1 is not None else []
        t_terms = run(
            temporal_grad_body, [loaded(shape((3 * mid, cols), BF))] + [shape((3 * mid, cols), BF)] * (n_r - 1),
            [ids, loaded(window), dt], f"temporal_grad_{u}", [pltpu.VMEM((mid, depth), F32)], scalars=1,
            flops=temporal_flops, moved=4 * MIB,
        )
        t_grad = traded(t_terms)
        d_mid, sums = run(
            functools.partial(middle_body, dims=dims), [far(shape((rows, mid), F32)), shape((n_f, 2, mid), F32)],
            [ids, dt, coef, *edges, keep, stat, mid_own[u], far(row_w), far(s_far)], f"middle_{u}",
            [pltpu.VMEM((pixels, frames + 16, depth), F32), pltpu.VMEM(row_shape.shape, BF), s_scr, s_scr, sems((3,))],
            scalars=1, flops=temporal_flops, moved=8 * MIB, after=[t_terms[0]],
        )
        done = sums_1.add([sums]) if sums_1 is not None else []
        sums = swap(sums, "frames")
        ds_shape, sum_shape = shape((rows, mid), BF), shape((2, mid), F32)
        acc = pltpu.VMEM((mid, n_f * k), F32)
        grad_args = [far(d_mid), stat, mid_own[u], sums]
        if u > 0 or not ring:
            ds, send, kept, mid_sums = run(
                functools.partial(input_body, dims=dims, total=total),
                [ds_shape, shape((2, rows, cols), BF), shape((2, rows, cols), F32), sum_shape],
                [ids, *grad_args, far(s_far), far(spatial_w[u])], f"input_{u}",
                [*adjoint_scr, pltpu.VMEM((rows, depth), F32), s_scr, s_scr, w_scr, sems((3,))],
                limit=44, scalars=1, flops=spatial_flops, moved=8 * MIB, after=t_grad[1:],
            )
        if ring and u > 0:
            *terms, token = run(
                functools.partial(weight_body, dims=dims),
                [far(shape((n_f,) + wire.shape, BF)), wire, wire, shape((8, LANES), F32)], [ids, loaded(act), ds, *all_loaded(t_grad)], f"weight_{u}", [pad, acc, pltpu.VMEM((n_f,) + wire.shape, BF), sems((n_f,))],
                scalars=1, flops=spatial_flops, moved=8 * MIB,
            )
            sums_1 = RingSums(*terms, f"sum_{u}")
        elif ring:
            slab = wire
            ds, flat, *terms = run(
                functools.partial(weight_first_body, dims=dims, total=total),
                [ds_shape, shape((8, 512), F32), far(shape((n_f,) + slab.shape, BF)), slab, slab],
                [ids, loaded(d_mid), *grad_args[1:], *d_norms[1], out_sums, *all_loaded(t_grad), loaded(s_far), loaded(act)], f"weight_{u}",
                [pltpu.VMEM((2, mid), F32), pad, acc, pltpu.VMEM((n_f,) + wire.shape, BF), sems((n_f,))],
                scalars=1, flops=spatial_flops, moved=8 * MIB, scale=1,
            )
            sums_0 = RingSums(*terms, f"sum_{u}")
        else:
            (s_grad,) = run(
                functools.partial(weight_plain_body, dims=dims), [w_shape], [loaded(act), ds],
                f"weight_{u}", [pad, acc], flops=spatial_flops, moved=8 * MIB,
            )
            s_grad = swap(s_grad.reshape(mid, n_f, k).transpose(1, 0, 2), "frames")
            t_rows = jnp.zeros((n_r,) + t_grad[0].shape, BF)
            for j in range(n_r):
                t_rows = lax.dynamic_update_index_in_dim(t_rows, t_grad[j], ids[j], 0)
            weight_parts[u] = (s_grad, swap(ordered(t_rows, n_f), "frames"))
        d_norms[u] = (mid_sums, out_sums) if u > 0 or not ring else None

    ends_1 = sums_1.end() if ring else []
    strided = frames * (-(-pixels // 8) * 8)
    grad_part, block_part = (own_frames, pixels, depth), (own_frames, pixels, cols)
    ends = run(
        functools.partial(last_body, dims=dims), [loaded(shape(grad_part, BF))] + [shape(grad_part, BF)] * (n_r - 1) + [shape(block_part, BF)] * n_r,
        [ids, ds, loaded(summed_grad), loaded(block), far(spatial_w[0])], "last",
        [*adjoint_scr, pltpu.VMEM((n_r, strided, cols), F32), pltpu.VMEM((1, strided, cols), F32), pltpu.VMEM((n_r,) + grad_part, BF),
         pltpu.VMEM((n_r,) + block_part, BF), w_scr, sems(())],
        limit=44, scalars=1, flops=spatial_flops, moved=8 * MIB, scale=1, after=ends_1[1:],
    )
    sent = ()
    state = [flip(a) for a in (spatial_weights, spatial_first, spatial_second)]
    state += [temporal_weights, temporal_first, temporal_second]
    if not ring:
        blocks, grads = traded(ends[n_r:]), traded(ends[:n_r])
    if ring:
        flats = from_group(flat)
        sums_0.add(ends[:1])
        blocks, grads = traded(ends[n_r:]), traded(ends[:n_r])
        norms = [mid_norm, mid_first, mid_second, out_norm, out_first, out_second]
        norms = run(
            norm_body, [shape(a.shape, F32) for a in norms], [ids, *flats, *norms], "norms",
            [pltpu.VMEM((n_r, 8, 512), F32)], scalars=1,
        )
        sent = sums_0.add([grads[1], norms[0]])
        weights = adam_unit(1, ends_1, state, None, "adam_1", sent)
        sent = sums_0.add([weights[0], *grads[2:]])
        weight_parts[0] = sums_0.end()
    block_out, input_grad = run(
        finish_body, [shape(frames_in.shape, BF), shape(frames_in.shape, F32)],
        [ids, *all_loaded(blocks + grads)], "finish", [pltpu.VMEM((own_frames, pixels, depth), F32)],
        scalars=1, moved=3 * MIB, after=sent,
    )
    if not ring:
        flat = jnp.concatenate([jnp.concatenate([m.reshape(-1), o.reshape(-1)]) for m, o in d_norms])
        flat = from_all(flat, "rep").reshape(n_r, units, -1)
        mid_grad = flat[:, :, : 2 * mid].reshape(n_r, units, 2, mid).transpose(1, 2, 0, 3)
        mid_grad = mid_grad.reshape(units, 2, n_r * mid)
        out_grad = flat[:, :, 2 * mid :].reshape(n_r, units, 2, cols).transpose(1, 2, 0, 3)
        out_grad = out_grad.reshape(units, 2, depth)
        norms = [*adam_step(mid_norm, mid_grad, mid_first, mid_second, RATE_NORM, 0.0)]
        norms += adam_step(out_norm, out_grad, out_first, out_second, RATE_NORM, 0.0)

    if ring:
        weights = adam_unit(0, weight_parts[0], state, weights, "adam_0")
        weights = [flip(a) for a in weights[:4]] + list(weights[4:])
    else:
        grads = [jnp.stack([jnp.sum(parts[i].astype(F32), axis=0) for parts in weight_parts]) for i in range(2)]
        news = adam_step(spatial_weights, flip(grads[0]), spatial_first, spatial_second, RATE_WEIGHT, DECAY)
        weights = [*news, news[0].astype(BF)]
        news = adam_step(temporal_weights, grads[1], temporal_first, temporal_second, RATE_WEIGHT, DECAY)
        weights += [*news, news[0].astype(BF)]
    return (block_out, input_grad, *weights, *norms)


def solution(mesh):
    by_frame = P(("frames", "rep"), None, None, None)
    by_block = P(None, "frames", "rep")
    placed = (by_frame, by_frame, P()) + (by_block,) * 6 + (P(),) * 6
    return jax.shard_map(
        on_device,
        mesh=mesh,
        in_specs=placed,
        out_specs=(by_frame, by_frame) + (by_block,) * 8 + (P(),) * 6,
        check_vma=False,
    )
```
